32 devices in a mesh: dp: 8 (over z, x), tensor: 4 (over y, core).
Axes of the slice: x: 2, y: 2, z: 4, core: 2. Of those that a mesh axis runs over, the one named last changes fastest.
Arguments:
- tokens: bfloat16 [4096, 8192], P('dp', 'tensor'), may hold values from -6 to 6
- query_weight: bfloat16 [8192, 4096], P(None, 'tensor'), may hold values from -0.0625 to 0.0625
- keyvalue_weight: bfloat16 [8192, 2048], P(None, 'tensor'), may hold values from -0.0625 to 0.0625
- adapter_down_weight: bfloat16 [256, 8192, 64], P('dp', 'tensor'), may hold values from -0.0625 to 0.0625
- adapter_up_weight: bfloat16 [256, 64, 4096], P('dp', None, 'tensor'), may hold values from -0.75 to 0.75
- keyvalue_page_store: bfloat16 [384, 64, 2048], P('dp', None, 'tensor')
- span_token_length: int32 [8, 16], P('dp'), may hold values from 1 to 128, 512 in all within a row
- adapter_owner: int32 [128, 1], P('dp'), may hold values from 0 to 7; in each aligned block of 16 rows (0 to 15, 16 to 31, ...) at most 2 rows name the same one
- adapter_local_index: int32 [128], P('dp'), may hold values from 0 to 31
- page_owner: int32 [512, 1], P('dp'), may hold values from 0 to 7; in each aligned block of 64 rows (0 to 63, 64 to 127, ...) at most 16 rows name the same one
- page_local_index: int32 [512], P('dp'), may hold values from 0 to 47
Outputs:
- attn_out: bfloat16 [4096, 4096], P('dp', 'tensor')
- new_cache: bfloat16 [4096, 2048], P('dp', 'tensor')
The draws below stay inside these ranges and needn't reach their ends.
Inputs may be any that keep to these rules, and one draw needn't show every extreme that they name: `adapter_owner`: in each aligned block of 16 rows (the requests of one index of dp) at most 2 rows name the same holder. `page_owner`: in each aligned block of 64 rows (the pages of one index of dp) at most 16 rows name the same holder. `span_token_length`: each row sums to 512.
All inputs are finite; a program needn't handle non-finite values.
Results may differ from the reference program's by a relative error of at most 0.012.
The reference program's roundings to bfloat16 on the way count: a program that leaves them out, or rounds other values in their place, can miss the bound.
Values may be sent and summed in bfloat16 or wider, within the bound.
No kernel may reach another device: no remote copies, remote signals or barrier semaphores. Data moves between devices by JAX's collectives and lax.ppermute only.
A program may use at most 192 MiB of HBM per device.

```python
import math
import jax
import jax.numpy as jnp
import numpy as np
from jax import lax

MODEL_WIDTH = 8192
QUERY_HEADS = 32
KV_HEADS = 8
HEAD_WIDTH = 128
ADAPTER_RANK = 64
ADP_DEV = 32
ADP_CAP = 2
PAGE = 64
HITS = 4
POOL = 48
REQUESTS_LOCAL = 16
TOK_DEV = 512
MOST = 128
HITS_DEV = 64
CAP = 16
TOKENS = 4096
ADAPTER_TOTAL = 256
N_DP = 8


def draw_keyvalue_page_store(key, part):
    key = jax.random.fold_in(key, 11)
    base = jax.random.normal(key, (N_DP * POOL, PAGE, KV_HEADS, 2, HEAD_WIDTH), jnp.float32)
    base = jnp.clip(base, -6.0, 6.0)
    return base.reshape(N_DP * POOL, PAGE, KV_HEADS * 2 * HEAD_WIDTH).astype(jnp.bfloat16)


def touch_ends(drawn, rng, smallest, largest):
    extent = drawn.shape
    index_at = [jax.random.randint(jax.random.fold_in(rng, axis), (), 0, extent[axis]) for axis in range(len(extent))]
    drawn = drawn.at[tuple(index_at)].set(smallest)
    longest = extent.index(max(extent))
    index_at[longest] = (index_at[longest] + 1) % extent[longest]
    return drawn.at[tuple(index_at)].set(largest)


def levels(own_key, shape, cuts, least, top_value):
    def one(axis_at, blocks):
        draws = jax.random.uniform(jax.random.fold_in(jax.random.fold_in(own_key, 6), axis_at), (blocks,), jnp.float32, least / len(cuts), top_value / len(cuts))
        return jnp.repeat(jnp.exp(draws), shape[axis_at] // blocks).reshape((-1,) + (1,) * (len(shape) - axis_at - 1))

    level = one(*cuts[0])
    for cut in cuts[1:]:
        level = level * one(*cut)
    return level


def length_profile(number_of, total, bound, slope):
    weights = [(1 << 20) // math.isqrt(standing ** slope) + 1 for standing in range(2, number_of + 1)]
    spare, holding = total - bound - (number_of - 1), [1] * (number_of - 1)
    while spare > 0:
        free = [i for i in range(number_of - 1) if holding[i] < bound]
        whole, left = sum([weights[i] for i in free]), spare
        for i in free:
            addition = min(bound - holding[i], max(1, left * weights[i] // whole), spare)
            holding[i] = holding[i] + addition
            spare = spare - addition
    return np.array([bound] + holding)


def uneven_parts(key, count, total, reach, skew):
    if count == 2:
        one = jax.random.randint(key, (), max(1, total - reach), min(reach, total - 1) + 1)
        return jnp.stack([one, total - one])
    sizes = jnp.asarray(length_profile(count, total, reach, skew), jnp.int32)
    couples = (count - 1) // 2
    donor, receiver = sizes[1:1 + 2 * couples:2], sizes[2:2 + 2 * couples:2]
    room = jnp.minimum(donor - 1, reach - receiver)
    shifted = jax.random.randint(jax.random.fold_in(key, 1), (couples,), 0, 1 << 20) % (room + 1)
    sizes = sizes.at[1:1 + 2 * couples:2].set(donor - shifted).at[2:2 + 2 * couples:2].set(receiver + shifted)
    return sizes[jax.random.permutation(jax.random.fold_in(key, 2), count)]


def deal_out(stream_key, own, number, rows, amount, top, limit, lean):
    sequence = jax.random.permutation(stream_key, amount)
    crowded, ordinary = shares(amount, rows * top, limit, lean, True), shares(amount, rows * top, limit, lean, False)
    places = jnp.arange(amount)

    def named(sizes, turn):
        used = int((sizes > 0).sum())
        fixed = max(1, used // 4)
        passed = fixed + (places - fixed + turn * (used - fixed)) % max(1, amount - fixed)
        return jnp.zeros((amount,), jnp.int32).at[sequence[jnp.where(places < fixed, places, passed)]].set(jnp.asarray(sizes, jnp.int32))

    sizes = jnp.where(number % 4 == 0, named(crowded, number // 4), named(ordinary, number - number // 4 - 1))
    mixed = jax.random.permutation(jax.random.fold_in(own, 3), amount)
    donor, taker = mixed[0:amount // 2 * 2:2], mixed[1:amount // 2 * 2:2]
    room = jnp.minimum(sizes[donor] - 1, limit - sizes[taker]) // 2
    room = jnp.where((donor == sequence[0]) | (taker == sequence[0]) | (sizes[taker] == 0), 0, jnp.maximum(room, 0))
    passed = jax.random.randint(jax.random.fold_in(own, 4), (amount // 2,), 0, 1 << 20) % (room + 1)
    sizes = sizes.at[donor].add(-passed).at[taker].add(passed)
    items = jnp.searchsorted(jnp.cumsum(sizes), jnp.arange(rows * top), side="right").astype(jnp.int32)
    grid = items.reshape(top, rows).T
    grid = grid[jax.random.permutation(jax.random.fold_in(own, 1), rows)]
    turn = jax.random.randint(jax.random.fold_in(own, 2), (rows, 1), 0, top)
    return jnp.take_along_axis(grid, (jnp.arange(top)[None, :] + turn) % top, axis=1)


def shares(amount, total, bound, slope, full):
    portions = [(1 << 20) // math.isqrt(grade ** slope) + 1 for grade in range(1, amount + 1)]
    largest = bound if full else min(bound, max(-(-total // amount), total * portions[0] // sum(portions)))
    least = 1 if total - largest >= amount - 1 else 0
    holding, rest = [largest] + [least] * (amount - 1), total - largest - least * (amount - 1)
    while rest > 0:
        candidates = [i for i in range(1, amount) if holding[i] < largest] or [i for i in range(1, amount) if holding[i] < bound]
        whole, remaining = sum([portions[i] for i in candidates]), rest
        for i in candidates:
            addition = min(bound - holding[i], max(1, remaining * portions[i] // whole), rest)
            holding[i] = holding[i] + addition
            rest = rest - addition
    return np.array(holding)


def scatter_about(rng, dims, deviation, limit, split=(), kind=jnp.bfloat16):
    array = deviation * jax.random.normal(rng, dims, jnp.float32)
    if split:
        array = array * levels(rng, dims, split, -0.22, 0.18)
    return jnp.clip(array, -limit, limit).astype(kind)


def setup_inputs(seed: int = 0) -> dict:
    streams_of = jax.random.split(jax.random.key(seed), 12)
    tokens = scatter_about(streams_of[0], (TOKENS, MODEL_WIDTH), 1.0, 6.0, ((0, 8), (1, 4)))
    query_weight = scatter_about(streams_of[1], (MODEL_WIDTH, QUERY_HEADS * HEAD_WIDTH), MODEL_WIDTH ** -0.5, 0.0625, ((1, 4),))
    keyvalue_weight = scatter_about(streams_of[2], (MODEL_WIDTH, KV_HEADS * 2 * HEAD_WIDTH), MODEL_WIDTH ** -0.5, 0.0625, ((1, 4),))
    adapter_down_weight = scatter_about(streams_of[3], (ADAPTER_TOTAL, MODEL_WIDTH, ADAPTER_RANK), MODEL_WIDTH ** -0.5, 0.0625, ((0, 8), (1, 4)))
    adapter_up_weight = scatter_about(streams_of[4], (ADAPTER_TOTAL, ADAPTER_RANK, QUERY_HEADS * HEAD_WIDTH), ADAPTER_RANK ** -0.5, 0.75, ((0, 8), (2, 4)))
    keyvalue_page_store = draw_keyvalue_page_store(jax.random.fold_in(streams_of[11], 71), 0)
    span_token_length = jax.vmap(lambda own: uneven_parts(own, REQUESTS_LOCAL, TOK_DEV, MOST, 2))(jax.random.split(streams_of[6], N_DP)).reshape((N_DP, REQUESTS_LOCAL)).astype(jnp.int32)
    adapter_owner_keys = jax.random.split(jax.random.fold_in(streams_of[7], 1), (N_DP * REQUESTS_LOCAL) // REQUESTS_LOCAL)
    adapter_owner_turns = jax.random.permutation(jax.random.fold_in(streams_of[7], 3), (N_DP * REQUESTS_LOCAL) // REQUESTS_LOCAL)
    adapter_owner = jax.vmap(lambda own, number: deal_out(jax.random.fold_in(streams_of[7], 2), own, number, REQUESTS_LOCAL, N_DP, 1, ADP_CAP, 2))(adapter_owner_keys, adapter_owner_turns).reshape((N_DP * REQUESTS_LOCAL, 1))
    adapter_local_index = touch_ends(jax.random.randint(streams_of[8], (N_DP * REQUESTS_LOCAL,), 0, ADP_DEV), jax.random.fold_in(streams_of[8], 1), 0, ADP_DEV - 1).astype(jnp.int32)
    page_owner_keys = jax.random.split(jax.random.fold_in(streams_of[9], 1), (N_DP * HITS_DEV) // HITS_DEV)
    page_owner_turns = jax.random.permutation(jax.random.fold_in(streams_of[9], 3), (N_DP * HITS_DEV) // HITS_DEV)
    page_owner = jax.vmap(lambda own, number: deal_out(jax.random.fold_in(streams_of[9], 2), own, number, HITS_DEV, N_DP, 1, CAP, 2))(page_owner_keys, page_owner_turns).reshape((N_DP * HITS_DEV, 1))
    page_local_index = touch_ends(jax.random.randint(streams_of[10], (N_DP * HITS_DEV,), 0, POOL), jax.random.fold_in(streams_of[10], 1), 0, POOL - 1).astype(jnp.int32)
    return dict(tokens=tokens, query_weight=query_weight, keyvalue_weight=keyvalue_weight, adapter_down_weight=adapter_down_weight, adapter_up_weight=adapter_up_weight, keyvalue_page_store=keyvalue_page_store, span_token_length=span_token_length, adapter_owner=adapter_owner, adapter_local_index=adapter_local_index, page_owner=page_owner, page_local_index=page_local_index)


ADAPTER_SCALE = 0.5
NEGATIVE = -1e30


def attend_reference(rows_q, prefix, fresh):
    rows = rows_q.shape[0]
    keys = jnp.concatenate([prefix[:, :, 0], fresh[:, :, 0]], axis=0).astype(jnp.float32)
    values = jnp.concatenate([prefix[:, :, 1], fresh[:, :, 1]], axis=0).astype(jnp.float32)
    steps = jnp.arange(rows, dtype=jnp.int32)
    causal = steps[None, :] <= steps[:, None]
    visible = jnp.concatenate([jnp.ones((rows, prefix.shape[0]), bool), causal], axis=1)
    scores = jnp.einsum("qkgd,pkd->kgqp", rows_q.astype(jnp.float32), keys) * (HEAD_WIDTH ** -0.5)
    scores = jnp.where(visible, scores, NEGATIVE)
    top = jnp.max(scores, axis=-1, keepdims=True)
    expo = jnp.where(visible, jnp.exp(scores - top), 0.0)
    total = jnp.sum(expo, axis=-1)
    weights = expo.astype(jnp.bfloat16).astype(jnp.float32)
    summed = jnp.einsum("kgqp,pkd->qkgd", weights, values)
    return summed / jnp.transpose(total, (2, 0, 1))[..., None]


def reference(tokens, query_weight, keyvalue_weight, adapter_down_weight, adapter_up_weight, keyvalue_page_store, span_token_length, adapter_owner, adapter_local_index, page_owner, page_local_index):
    group = QUERY_HEADS // KV_HEADS
    adapter_ids = (adapter_owner[:, 0] * ADP_DEV + adapter_local_index).astype(jnp.int32).reshape(N_DP, REQUESTS_LOCAL)
    page_ids = (page_owner[:, 0] * POOL + page_local_index).astype(jnp.int32).reshape(N_DP, HITS_DEV)
    token_blocks = tokens.reshape(N_DP, TOK_DEV, MODEL_WIDTH)

    def one_device(items):
        block, lengths, adapter_set, pages = items
        ends = jnp.cumsum(lengths).astype(jnp.int32)
        starts = (ends - lengths).astype(jnp.int32)
        steps = jnp.arange(TOK_DEV, dtype=jnp.int32)[:, None]
        member = ((steps >= starts[None, :]) & (steps < ends[None, :])).astype(jnp.float32)
        query_plain = jnp.dot(block, query_weight, preferred_element_type=jnp.float32)
        keyval = jnp.dot(block, keyvalue_weight, preferred_element_type=jnp.float32).astype(jnp.bfloat16)
        down_product = adapter_down_weight[adapter_set].astype(jnp.float32)
        terms = jnp.einsum("td,rdk->trk", block.astype(jnp.float32), down_product)
        shrink = jnp.sum(member[:, :, None] * terms, axis=1)
        up_product = (member[:, :, None] * shrink[:, None, :]).astype(jnp.bfloat16).reshape(TOK_DEV, REQUESTS_LOCAL * ADAPTER_RANK)
        query_correction = jnp.dot(up_product, adapter_up_weight[adapter_set].reshape(REQUESTS_LOCAL * ADAPTER_RANK, QUERY_HEADS * HEAD_WIDTH), preferred_element_type=jnp.float32)
        query_final = (query_plain + ADAPTER_SCALE * query_correction).astype(jnp.bfloat16)
        prefix = keyvalue_page_store[pages].reshape(REQUESTS_LOCAL, HITS * PAGE, KV_HEADS, 2, HEAD_WIDTH)
        query_pad = jnp.concatenate([query_final, jnp.zeros((MOST, QUERY_HEADS * HEAD_WIDTH), jnp.bfloat16)], axis=0)
        cache_pad = jnp.concatenate([keyval, jnp.zeros((MOST, KV_HEADS * 2 * HEAD_WIDTH), jnp.bfloat16)], axis=0)
        output = jnp.zeros((TOK_DEV + MOST, QUERY_HEADS * HEAD_WIDTH), jnp.bfloat16)
        for index in range(REQUESTS_LOCAL):
            start = starts[index]
            rows_q = lax.dynamic_slice_in_dim(query_pad, start, MOST, 0).reshape(MOST, KV_HEADS, group, HEAD_WIDTH)
            fresh = lax.dynamic_slice_in_dim(cache_pad, start, MOST, 0).reshape(MOST, KV_HEADS, 2, HEAD_WIDTH)
            result = attend_reference(rows_q, prefix[index], fresh).reshape(MOST, QUERY_HEADS * HEAD_WIDTH).astype(jnp.bfloat16)
            output = lax.dynamic_update_slice_in_dim(output, result, start, 0)
        return output[:TOK_DEV], keyval

    outputs, caches = lax.map(one_device, (token_blocks, span_token_length, adapter_ids, page_ids))
    return outputs.reshape(TOKENS, QUERY_HEADS * HEAD_WIDTH), caches.reshape(TOKENS, KV_HEADS * 2 * HEAD_WIDTH)
```

```python
import functools

import jax
import jax.numpy as jnp
from jax import lax
from jax.experimental import pallas as pl
from jax.experimental.pallas import tpu as pltpu
from jax.sharding import PartitionSpec as P

HEAD_WIDTH = 128
ADP_CAP = 2
PAGE = 64
HITS = 4
MOST = 128
BLOCK = 32

ADAPTER_SCALE = 0.5
NEGATIVE = -1e30


def bucket_positions(holder, peers, capacity):
    onehot = (holder[:, None] == jnp.arange(peers, dtype=jnp.int32)[None, :]).astype(jnp.int32)
    earlier = jnp.cumsum(onehot, axis=0) - onehot
    return holder * capacity + jnp.sum(earlier * onehot, axis=1)


def fill_requests(position, wanted, slots_total):
    match = position[None, :] == jnp.arange(slots_total, dtype=jnp.int32)[:, None]
    return jnp.sum(jnp.where(match, wanted[None, :], 0), axis=1)


def attention_steps(starts, ends, total):
    first = starts // BLOCK
    count = (ends - 1) // BLOCK - first + 1
    upto = jnp.cumsum(count)
    step = jnp.minimum(jnp.arange(total, dtype=jnp.int32), upto[-1] - 1)
    request = jnp.sum((upto[None, :] <= step[:, None]).astype(jnp.int32), axis=1)
    pick = request[:, None] == jnp.arange(starts.shape[0], dtype=jnp.int32)[None, :]

    def at(values):
        return jnp.sum(jnp.where(pick, values[None, :], 0), axis=1)

    block = at(first) + step - at(upto - count)
    return jnp.stack([request, block, at(starts), at(ends)])


def attention_kernel(steps_ref, query_ref, cache_ref, pages_ref, out_ref):
    rows_total, q_cols = query_ref.shape
    kv_heads = cache_ref.shape[1] // (2 * HEAD_WIDTH)
    group = q_cols // HEAD_WIDTH // kv_heads
    window = min(rows_total, MOST + BLOCK)
    scale = HEAD_WIDTH ** -0.5
    out_ref[...] = jnp.zeros_like(out_ref)

    def step(index, carry):
        request = steps_ref[0, index]
        row = pl.multiple_of(steps_ref[1, index] * BLOCK, BLOCK)
        start = steps_ref[2, index]
        end = steps_ref[3, index]
        base = pl.multiple_of(jnp.minimum(start // BLOCK * BLOCK, rows_total - window), BLOCK)
        q_at = row + lax.broadcasted_iota(jnp.int32, (group * BLOCK, window), 0) % BLOCK
        k_at = base + lax.broadcasted_iota(jnp.int32, (group * BLOCK, window), 1)
        visible = (k_at >= start) & (k_at <= q_at)
        own_at = row + lax.broadcasted_iota(jnp.int32, (BLOCK, HEAD_WIDTH), 0)
        own = (own_at >= start) & (own_at < end)
        for head in range(kv_heads):
            at = head * 2 * HEAD_WIDTH
            wide = head * group * HEAD_WIDTH
            rows_q = jnp.concatenate(
                [
                    query_ref[pl.ds(row, BLOCK), wide + g * HEAD_WIDTH : wide + (g + 1) * HEAD_WIDTH]
                    for g in range(group)
                ],
                axis=0,
            )
            old_k = pages_ref[pl.ds(request * HITS, HITS), :, at : at + HEAD_WIDTH].reshape(HITS * PAGE, HEAD_WIDTH)
            old_v = pages_ref[
                pl.ds(request * HITS, HITS), :, at + HEAD_WIDTH : at + 2 * HEAD_WIDTH
            ].reshape(HITS * PAGE, HEAD_WIDTH)
            new_k = cache_ref[pl.ds(base, window), at : at + HEAD_WIDTH]
            new_v = cache_ref[pl.ds(base, window), at + HEAD_WIDTH : at + 2 * HEAD_WIDTH]
            dims = (((1,), (1,)), ((), ()))
            old_s = lax.dot_general(rows_q, old_k, dims, preferred_element_type=jnp.float32) * scale
            new_s = lax.dot_general(rows_q, new_k, dims, preferred_element_type=jnp.float32) * scale
            new_s = jnp.where(visible, new_s, NEGATIVE)
            top = jnp.maximum(
                jnp.max(old_s, axis=1, keepdims=True), jnp.max(new_s, axis=1, keepdims=True)
            )
            old_e = jnp.exp(old_s - top)
            new_e = jnp.where(visible, jnp.exp(new_s - top), 0.0)
            total = jnp.sum(old_e, axis=1, keepdims=True) + jnp.sum(new_e, axis=1, keepdims=True)
            summed = jnp.dot(old_e.astype(jnp.bfloat16), old_v, preferred_element_type=jnp.float32)
            summed += jnp.dot(new_e.astype(jnp.bfloat16), new_v, preferred_element_type=jnp.float32)
            result = summed / total
            for g in range(group):
                cols = slice(wide + g * HEAD_WIDTH, wide + (g + 1) * HEAD_WIDTH)
                before = out_ref[pl.ds(row, BLOCK), cols]
                mine = result[g * BLOCK : (g + 1) * BLOCK].astype(jnp.bfloat16)
                out_ref[pl.ds(row, BLOCK), cols] = jnp.where(own, mine, before)
        return carry

    lax.fori_loop(0, steps_ref.shape[1], step, 0)


def attend(query, cache, pages, starts, ends):
    rows, q_cols = query.shape
    steps_total = rows // BLOCK + starts.shape[0] - 1
    steps = attention_steps(starts, ends, steps_total)
    vmem = pl.BlockSpec(memory_space=pltpu.VMEM)
    return pl.pallas_call(
        attention_kernel,
        out_shape=jax.ShapeDtypeStruct((rows, q_cols), jnp.bfloat16),
        in_specs=[pl.BlockSpec(memory_space=pltpu.SMEM), vmem, vmem, vmem],
        out_specs=vmem,
        compiler_params=pltpu.CompilerParams(vmem_limit_bytes=40 * 1024 * 1024),
        cost_estimate=pl.CostEstimate(
            flops=4 * steps_total * BLOCK * q_cols * (HITS * PAGE + MOST + BLOCK),
            bytes_accessed=2 * (query.size * 2 + cache.size + pages.size),
            transcendentals=0,
        ),
        name="attend",
    )(steps, query, cache, pages)


def on_device(
    tokens,
    query_weight,
    keyvalue_weight,
    adapter_down_weight,
    adapter_up_weight,
    keyvalue_page_store,
    span_token_length,
    adapter_owner,
    adapter_local_index,
    page_owner,
    page_local_index,
):
    peers = lax.axis_size("dp")
    tok_rows = tokens.shape[0]
    q_cols = query_weight.shape[1]
    rank = adapter_down_weight.shape[2]
    adapter_slots = peers * ADP_CAP
    page_cap = max(2, 2 * page_local_index.shape[0] // peers)
    adapter_pos = bucket_positions(adapter_owner[:, 0], peers, ADP_CAP)
    adapter_wanted = fill_requests(adapter_pos, adapter_local_index, adapter_slots)
    page_pos = bucket_positions(page_owner[:, 0], peers, page_cap)
    page_wanted = fill_requests(page_pos, page_local_index, peers * page_cap)
    wanted = jnp.concatenate(
        [adapter_wanted.reshape(peers, ADP_CAP), page_wanted.reshape(peers, page_cap)], axis=1
    )
    asked = lax.all_to_all(wanted, "dp", split_axis=0, concat_axis=0, tiled=True)
    adapter_asked = asked[:, :ADP_CAP].reshape(-1)
    page_asked = asked[:, ADP_CAP:].reshape(-1)
    down_sent = lax.all_to_all(
        adapter_down_weight[adapter_asked], "dp", split_axis=0, concat_axis=0, tiled=True
    )
    up_sent = lax.all_to_all(
        adapter_up_weight[adapter_asked], "dp", split_axis=0, concat_axis=0, tiled=True
    )
    page_sent = lax.all_to_all(
        keyvalue_page_store[page_asked], "dp", split_axis=0, concat_axis=0, tiled=True
    )
    prefix_pages = page_sent[page_pos]

    lengths = span_token_length[0]
    ends = jnp.cumsum(lengths)
    starts = ends - lengths
    steps = jnp.arange(tok_rows, dtype=jnp.int32)[:, None]
    member = (steps >= starts[None, :]) & (steps < ends[None, :])
    slot = jnp.sum(jnp.where(member, adapter_pos[None, :], 0), axis=1)
    in_slot = slot[:, None] == jnp.arange(adapter_slots, dtype=jnp.int32)[None, :]

    down_part = jnp.einsum("tn,snk->tsk", tokens, down_sent, preferred_element_type=jnp.float32)
    shrink_part = jnp.sum(jnp.where(in_slot[:, :, None], down_part, 0.0), axis=1)
    shrink = lax.psum(shrink_part, "tensor").astype(jnp.bfloat16)

    piece = lax.all_gather(tokens, "tensor", axis=1, tiled=True)
    query_base = jnp.dot(piece, query_weight, preferred_element_type=jnp.float32)
    new_cache = jnp.dot(piece, keyvalue_weight, preferred_element_type=jnp.float32).astype(jnp.bfloat16)

    spread = jnp.where(in_slot[:, :, None], shrink[:, None, :], 0).reshape(tok_rows, adapter_slots * rank)
    correction = jnp.dot(
        spread, up_sent.reshape(adapter_slots * rank, q_cols), preferred_element_type=jnp.float32
    )
    query = (query_base + ADAPTER_SCALE * correction).astype(jnp.bfloat16)
    out = attend(query, new_cache, prefix_pages, starts, ends)
    return (out, new_cache)


def solution(mesh):
    return jax.shard_map(
        on_device,
        mesh=mesh,
        in_specs=(
            P("dp", "tensor"),
            P(None, "tensor"),
            P(None, "tensor"),
            P("dp", "tensor", None),
            P("dp", None, "tensor"),
            P("dp", None, "tensor"),
            P("dp", None),
            P("dp", None),
            P("dp"),
            P("dp", None),
            P("dp"),
        ),
        out_specs=(P("dp", "tensor"), P("dp", "tensor")),
        check_vma=False,
    )
```

```python
import math

import jax
import jax.numpy as jnp
from jax import lax
from jax.experimental import pallas as pl
from jax.experimental.pallas import tpu as pltpu
from jax.sharding import PartitionSpec as P

HEAD_WIDTH = 128
ADP_CAP = 2
PAGE = 64
HITS = 4
MOST = 128
BLOCK = 32

ADAPTER_SCALE = 0.5
NEGATIVE = -1e30


def bucket_positions(holder, peers, capacity):
    onehot = (holder[:, None] == jnp.arange(peers, dtype=jnp.int32)[None, :]).astype(jnp.int32)
    earlier = jnp.cumsum(onehot, axis=0) - onehot
    return holder * capacity + jnp.sum(earlier * onehot, axis=1)


def fill_requests(position, wanted, slots_total):
    match = position[None, :] == jnp.arange(slots_total, dtype=jnp.int32)[:, None]
    return jnp.sum(jnp.where(match, wanted[None, :], 0), axis=1)


def attention_steps(starts, ends, total):
    first = starts // BLOCK
    count = (ends - 1) // BLOCK - first + 1
    upto = jnp.cumsum(count)
    step = jnp.minimum(jnp.arange(total, dtype=jnp.int32), upto[-1] - 1)
    request = jnp.sum((upto[None, :] <= step[:, None]).astype(jnp.int32), axis=1)
    pick = request[:, None] == jnp.arange(starts.shape[0], dtype=jnp.int32)[None, :]

    def at(values):
        return jnp.sum(jnp.where(pick, values[None, :], 0), axis=1)

    block = at(first) + step - at(upto - count)
    return jnp.stack([request, block, at(starts), at(ends)])


def attention_kernel(steps_ref, base_ref, spread_ref, up_ref, cache_ref, pages_ref, out_ref, query_ref):
    rows_total, q_cols = base_ref.shape
    kv_heads = cache_ref.shape[1] // (2 * HEAD_WIDTH)
    group = q_cols // HEAD_WIDTH // kv_heads
    window = min(rows_total, MOST + BLOCK)
    sharp = HEAD_WIDTH ** -0.5 * math.log2(math.e)

    def project(index, carry):
        cols = pl.ds(pl.multiple_of(index * 256, 256), 256)
        correction = jnp.dot(spread_ref[...], up_ref[:, cols], preferred_element_type=jnp.float32)
        query_ref[:, cols] = (base_ref[:, cols] + ADAPTER_SCALE * correction).astype(jnp.bfloat16)
        return carry

    lax.fori_loop(0, q_cols // 256, project, 0)

    def step(index, carry):
        request = steps_ref[0, index]
        row = pl.multiple_of(steps_ref[1, index] * BLOCK, BLOCK)
        start = steps_ref[2, index]
        end = steps_ref[3, index]
        base = pl.multiple_of(jnp.minimum(start // BLOCK * BLOCK, rows_total - window), BLOCK)
        q_at = row + lax.broadcasted_iota(jnp.int32, (group * BLOCK, window), 0) % BLOCK
        k_at = base + lax.broadcasted_iota(jnp.int32, (group * BLOCK, window), 1)
        visible = (k_at >= start) & (k_at <= q_at)
        own_at = row + lax.broadcasted_iota(jnp.int32, (BLOCK, HEAD_WIDTH), 0)
        own = (own_at >= start) & (own_at < end)
        dims = (((1,), (1,)), ((), ()))
        scores = []
        for head in range(kv_heads):
            at = head * 2 * HEAD_WIDTH
            wide = head * group * HEAD_WIDTH
            rows_q = jnp.concatenate(
                [
                    query_ref[pl.ds(row, BLOCK), wide + g * HEAD_WIDTH : wide + (g + 1) * HEAD_WIDTH]
                    for g in range(group)
                ],
                axis=0,
            )
            old_k = pages_ref[pl.ds(request * HITS, HITS), :, at : at + HEAD_WIDTH].reshape(HITS * PAGE, HEAD_WIDTH)
            new_k = cache_ref[pl.ds(base, window), at : at + HEAD_WIDTH]
            old_s = lax.dot_general(rows_q, old_k, dims, preferred_element_type=jnp.float32)
            new_s = lax.dot_general(rows_q, new_k, dims, preferred_element_type=jnp.float32)
            scores.append((old_s, jnp.where(visible, new_s, NEGATIVE)))
        weights = []
        for old_s, new_s in scores:
            top = jnp.maximum(
                jnp.max(old_s, axis=1, keepdims=True), jnp.max(new_s, axis=1, keepdims=True)
            )
            old_e = jnp.exp2((old_s - top) * sharp)
            new_e = jnp.exp2((new_s - top) * sharp)
            total = jnp.sum(old_e, axis=1, keepdims=True) + jnp.sum(new_e, axis=1, keepdims=True)
            weights.append((old_e.astype(jnp.bfloat16), new_e.astype(jnp.bfloat16), total))
        for head in range(kv_heads):
            at = head * 2 * HEAD_WIDTH + HEAD_WIDTH
            wide = head * group * HEAD_WIDTH
            old_e, new_e, total = weights[head]
            old_v = pages_ref[pl.ds(request * HITS, HITS), :, at : at + HEAD_WIDTH].reshape(HITS * PAGE, HEAD_WIDTH)
            new_v = cache_ref[pl.ds(base, window), at : at + HEAD_WIDTH]
            summed = jnp.dot(old_e, old_v, preferred_element_type=jnp.float32)
            summed += jnp.dot(new_e, new_v, preferred_element_type=jnp.float32)
            result = (summed / total).astype(jnp.bfloat16)
            for g in range(group):
                cols = slice(wide + g * HEAD_WIDTH, wide + (g + 1) * HEAD_WIDTH)
                before = out_ref[pl.ds(row, BLOCK), cols]
                out_ref[pl.ds(row, BLOCK), cols] = jnp.where(own, result[g * BLOCK : (g + 1) * BLOCK], before)
        return carry

    lax.fori_loop(0, steps_ref.shape[1], step, 0)


def attend(query_base, spread, up, cache, pages, starts, ends):
    rows, q_cols = query_base.shape
    steps_total = rows // BLOCK + starts.shape[0] - 1
    steps = attention_steps(starts, ends, steps_total)
    vmem = pl.BlockSpec(memory_space=pltpu.VMEM)
    return pl.pallas_call(
        attention_kernel,
        out_shape=jax.ShapeDtypeStruct((rows, q_cols), jnp.bfloat16),
        in_specs=[pl.BlockSpec(memory_space=pltpu.SMEM)] + [vmem] * 5,
        out_specs=vmem,
        scratch_shapes=[pltpu.VMEM((rows, q_cols), jnp.bfloat16)],
        compiler_params=pltpu.CompilerParams(vmem_limit_bytes=40 * 1024 * 1024),
        cost_estimate=pl.CostEstimate(
            flops=4 * steps_total * BLOCK * q_cols * (HITS * PAGE + MOST + BLOCK) + 2 * spread.size * q_cols,
            bytes_accessed=4 * query_base.size + 2 * (2 * spread.size + up.size + cache.size + pages.size),
            transcendentals=0,
        ),
        name="attend",
    )(steps, query_base, spread, up, cache, pages)


def on_device(
    tokens,
    query_weight,
    keyvalue_weight,
    adapter_down_weight,
    adapter_up_weight,
    keyvalue_page_store,
    span_token_length,
    adapter_owner,
    adapter_local_index,
    page_owner,
    page_local_index,
):
    peers = lax.axis_size("dp")
    half = peers // 2
    me = lax.axis_index("dp")
    tok_rows = tokens.shape[0]
    q_cols = query_weight.shape[1]
    rank = adapter_down_weight.shape[2]
    adapter_slots = peers * ADP_CAP

    def swap(array, distance):
        return lax.ppermute(array, "dp", [(peer, peer ^ distance) for peer in range(peers)])

    mirrored_store = swap(keyvalue_page_store, half)

    page_cap = max(2, 2 * page_local_index.shape[0] // peers)
    adapter_pos = bucket_positions(adapter_owner[:, 0], peers, ADP_CAP)
    adapter_wanted = fill_requests(adapter_pos, adapter_local_index, adapter_slots).reshape(peers, ADP_CAP)
    page_pos = bucket_positions(page_owner[:, 0] ^ me, peers, page_cap)
    page_wanted = fill_requests(page_pos, page_local_index, peers * page_cap).reshape(peers, page_cap)
    by_peer = page_wanted[jnp.arange(peers, dtype=jnp.int32) ^ me]
    by_mirror = page_wanted[jnp.arange(peers, dtype=jnp.int32) ^ me ^ half]
    wanted = jnp.concatenate([adapter_wanted, by_peer, by_mirror], axis=1)
    asked = lax.all_to_all(wanted, "dp", split_axis=0, concat_axis=0, tiled=True)
    adapter_asked = asked[:, :ADP_CAP].reshape(-1)
    page_asked = asked[jnp.arange(half, dtype=jnp.int32) ^ me][:, ADP_CAP:]

    near = [keyvalue_page_store[page_asked[i, :page_cap]] for i in range(half)]
    near = [near[0]] + [swap(near[i], i) for i in range(1, half)]
    far = [mirrored_store[page_asked[i, page_cap:]] for i in range(half)]
    down_rows, *far = lax.optimization_barrier((adapter_down_weight[adapter_asked], *far))
    far = [far[0]] + [swap(far[i], i) for i in range(1, half)]
    prefix_pages = jnp.concatenate(near + far, axis=0)[page_pos]

    down_sent = lax.all_to_all(down_rows, "dp", split_axis=0, concat_axis=0, tiled=True)
    up_rows, down_sent = lax.optimization_barrier((adapter_up_weight[adapter_asked], down_sent))
    up_sent = lax.all_to_all(up_rows, "dp", split_axis=0, concat_axis=0, tiled=True)

    lengths = span_token_length[0]
    ends = jnp.cumsum(lengths)
    starts = ends - lengths
    steps = jnp.arange(tok_rows, dtype=jnp.int32)[:, None]
    member = (steps >= starts[None, :]) & (steps < ends[None, :])
    slot = jnp.sum(jnp.where(member, adapter_pos[None, :], 0), axis=1)
    in_slot = slot[:, None] == jnp.arange(adapter_slots, dtype=jnp.int32)[None, :]

    down_part = jnp.einsum("tn,snk->tsk", tokens, down_sent, preferred_element_type=jnp.float32)
    shrink_part = jnp.sum(jnp.where(in_slot[:, :, None], down_part, 0.0), axis=1)
    shrink = lax.psum(shrink_part, "tensor").astype(jnp.bfloat16)
    spread = jnp.where(in_slot[:, :, None], shrink[:, None, :], 0).reshape(tok_rows, adapter_slots * rank)

    piece = lax.all_gather(tokens, "tensor", axis=1, tiled=True)
    query_base = jnp.dot(piece, query_weight, preferred_element_type=jnp.float32)
    new_cache = jnp.dot(piece, keyvalue_weight, preferred_element_type=jnp.float32).astype(jnp.bfloat16)

    up = up_sent.reshape(adapter_slots * rank, q_cols)
    out = attend(query_base, spread, up, new_cache, prefix_pages, starts, ends)
    return (out, new_cache)


def solution(mesh):
    return jax.shard_map(
        on_device,
        mesh=mesh,
        in_specs=(
            P("dp", "tensor"),
            P(None, "tensor"),
            P(None, "tensor"),
            P("dp", "tensor", None),
            P("dp", None, "tensor"),
            P("dp", None, "tensor"),
            P("dp", None),
            P("dp", None),
            P("dp"),
            P("dp", None),
            P("dp"),
        ),
        out_specs=(P("dp", "tensor"), P("dp", "tensor")),
        check_vma=False,
    )
```

```python
import math

import jax
import jax.numpy as jnp
from jax import lax
from jax.experimental import pallas as pl
from jax.experimental.pallas import tpu as pltpu
from jax.sharding import PartitionSpec as P

HEAD_WIDTH = 128
ADP_CAP = 2
PAGE = 64
HITS = 4
MOST = 128
BLOCK = 32
TOGETHER = 4

ADAPTER_SCALE = 0.5
NEGATIVE = -1e30


def earlier_alike(owner):
    count = owner.shape[-1]
    ahead = jnp.arange(count, dtype=jnp.int32)[None, :] < jnp.arange(count, dtype=jnp.int32)[:, None]
    alike = owner[..., None, :] == owner[..., :, None]
    return jnp.sum((alike & ahead).astype(jnp.int32), axis=-1)


def asked_of(holder, owner, order, local, capacity):
    place = jnp.arange(capacity, dtype=jnp.int32)[None, :, None]
    match = (owner[:, None, :] == holder) & (order[:, None, :] == place)
    return jnp.sum(jnp.where(match, local[:, None, :], 0), axis=2)


def attention_steps(starts, ends, total):
    first = starts // BLOCK
    count = (ends - 1) // BLOCK - first + 1
    upto = jnp.cumsum(count)
    step = jnp.minimum(jnp.arange(total, dtype=jnp.int32), upto[-1] - 1)
    request = jnp.sum((upto[None, :] <= step[:, None]).astype(jnp.int32), axis=1)
    pick = request[:, None] == jnp.arange(starts.shape[0], dtype=jnp.int32)[None, :]

    def at(values):
        return jnp.sum(jnp.where(pick, values[None, :], 0), axis=1)

    block = at(first) + step - at(upto - count)
    return jnp.stack([request, block, at(starts), at(ends)])


def attention_kernel(
    steps_ref, spread_ref, up_ref, base_hbm, cache_hbm, pages_hbm, out_ref, query_ref, base_ref, cache_ref, pages_ref, sems
):
    copies = [
        pltpu.make_async_copy(base_hbm, base_ref, sems.at[0]),
        pltpu.make_async_copy(cache_hbm, cache_ref, sems.at[1]),
        pltpu.make_async_copy(pages_hbm, pages_ref, sems.at[2]),
    ]
    for copy in copies:
        copy.start()
    rows_total, q_cols = base_ref.shape
    kv_heads = cache_ref.shape[1] // (2 * HEAD_WIDTH)
    group = q_cols // HEAD_WIDTH // kv_heads
    window = min(rows_total, MOST + BLOCK)
    sharp = HEAD_WIDTH ** -0.5 * math.log2(math.e)
    copies[0].wait()

    def project(index, carry):
        cols = pl.ds(pl.multiple_of(index * 256, 256), 256)
        correction = jnp.dot(spread_ref[...], up_ref[:, cols], preferred_element_type=jnp.float32)
        query_ref[:, cols] = (base_ref[:, cols] + ADAPTER_SCALE * correction).astype(jnp.bfloat16)
        return carry

    lax.fori_loop(0, q_cols // 256, project, 0)

    copies[1].wait()
    copies[2].wait()
    dims = (((1,), (1,)), ((), ()))

    def several(turn, carry):
        places = []
        for lane in range(TOGETHER):
            index = turn * TOGETHER + lane
            row = pl.multiple_of(steps_ref[1, index] * BLOCK, BLOCK)
            start = steps_ref[2, index]
            base = pl.multiple_of(jnp.minimum(start // BLOCK * BLOCK, rows_total - window), BLOCK)
            old = pl.ds(steps_ref[0, index] * HITS, HITS)
            places.append((row, pl.ds(base, window), old, base, start, steps_ref[3, index]))
        chains = [(place, head) for place in places for head in range(kv_heads)]
        scores = []
        for (row, new, old, base, start, _), head in chains:
            at = head * 2 * HEAD_WIDTH
            wide = head * group * HEAD_WIDTH
            q_at = row + lax.broadcasted_iota(jnp.int32, (group * BLOCK, window), 0) % BLOCK
            k_at = base + lax.broadcasted_iota(jnp.int32, (group * BLOCK, window), 1)
            visible = (k_at >= start) & (k_at <= q_at)
            rows_q = jnp.concatenate(
                [
                    query_ref[pl.ds(row, BLOCK), wide + g * HEAD_WIDTH : wide + (g + 1) * HEAD_WIDTH]
                    for g in range(group)
                ],
                axis=0,
            )
            old_k = pages_ref[old, :, at : at + HEAD_WIDTH].reshape(HITS * PAGE, HEAD_WIDTH)
            new_k = cache_ref[new, at : at + HEAD_WIDTH]
            old_s = lax.dot_general(rows_q, old_k, dims, preferred_element_type=jnp.float32)
            new_s = lax.dot_general(rows_q, new_k, dims, preferred_element_type=jnp.float32)
            scores.append((old_s, jnp.where(visible, new_s, NEGATIVE)))
        weights = []
        for old_s, new_s in scores:
            top = jnp.maximum(
                jnp.max(old_s, axis=1, keepdims=True), jnp.max(new_s, axis=1, keepdims=True)
            )
            old_e = jnp.exp2((old_s - top) * sharp)
            new_e = jnp.exp2((new_s - top) * sharp)
            total = jnp.sum(old_e, axis=1, keepdims=True) + jnp.sum(new_e, axis=1, keepdims=True)
            weights.append((old_e.astype(jnp.bfloat16), new_e.astype(jnp.bfloat16), total))
        results = []
        for ((_, new, old, _, _, _), head), (old_e, new_e, total) in zip(chains, weights):
            at = head * 2 * HEAD_WIDTH + HEAD_WIDTH
            old_v = pages_ref[old, :, at : at + HEAD_WIDTH].reshape(HITS * PAGE, HEAD_WIDTH)
            new_v = cache_ref[new, at : at + HEAD_WIDTH]
            summed = jnp.dot(old_e, old_v, preferred_element_type=jnp.float32)
            summed += jnp.dot(new_e, new_v, preferred_element_type=jnp.float32)
            results.append((summed / total).astype(jnp.bfloat16))
        for ((row, _, _, _, start, end), head), result in zip(chains, results):
            own_at = row + lax.broadcasted_iota(jnp.int32, (BLOCK, HEAD_WIDTH), 0)
            own = (own_at >= start) & (own_at < end)
            for g in range(group):
                col = (head * group + g) * HEAD_WIDTH
                cols = slice(col, col + HEAD_WIDTH)
                before = out_ref[pl.ds(row, BLOCK), cols]
                out_ref[pl.ds(row, BLOCK), cols] = jnp.where(own, result[g * BLOCK : (g + 1) * BLOCK], before)
        return carry

    lax.fori_loop(0, steps_ref.shape[1] // TOGETHER, several, 0)


def attend(query_base, spread, up, cache, pages, starts, ends):
    rows, q_cols = query_base.shape
    steps_total = -(-(rows // BLOCK + starts.shape[0] - 1) // TOGETHER) * TOGETHER
    steps = attention_steps(starts, ends, steps_total)
    vmem = pl.BlockSpec(memory_space=pltpu.VMEM)
    return pl.pallas_call(
        attention_kernel,
        out_shape=jax.ShapeDtypeStruct((rows, q_cols), jnp.bfloat16),
        in_specs=[pl.BlockSpec(memory_space=pltpu.SMEM)] + [vmem] * 2 + [pl.BlockSpec(memory_space=pl.ANY)] * 3,
        out_specs=vmem,
        scratch_shapes=[
            pltpu.VMEM((rows, q_cols), jnp.bfloat16),
            pltpu.VMEM(query_base.shape, query_base.dtype),
            pltpu.VMEM(cache.shape, cache.dtype),
            pltpu.VMEM(pages.shape, pages.dtype),
            pltpu.SemaphoreType.DMA((3,)),
        ],
        compiler_params=pltpu.CompilerParams(vmem_limit_bytes=48 * 1024 * 1024),
        cost_estimate=pl.CostEstimate(
            flops=4 * steps_total * BLOCK * q_cols * (HITS * PAGE + MOST + BLOCK) + 2 * spread.size * q_cols,
            bytes_accessed=4 * query_base.size + 2 * (2 * spread.size + up.size + cache.size + pages.size),
            transcendentals=0,
        ),
        name="attend",
    )(steps, spread, up, query_base, cache, pages)


def on_device(
    tokens,
    query_weight,
    keyvalue_weight,
    adapter_down_weight,
    adapter_up_weight,
    keyvalue_page_store,
    span_token_length,
    adapter_owner,
    adapter_local_index,
    page_owner,
    page_local_index,
):
    peers = lax.axis_size("dp")
    half = peers // 2
    me = lax.axis_index("dp")
    tok_rows = tokens.shape[0]
    q_cols = query_weight.shape[1]
    rank = adapter_down_weight.shape[2]
    adapter_slots = peers * ADP_CAP

    def swap(array, distance):
        return lax.ppermute(array, "dp", [(peer, peer ^ distance) for peer in range(peers)])

    page_count = page_local_index.shape[0]
    request_count = adapter_local_index.shape[0]
    raw = jnp.concatenate([page_owner[:, 0], page_local_index, adapter_owner[:, 0], adapter_local_index])
    everyone = lax.all_to_all(
        jnp.broadcast_to(raw[None], (peers, raw.shape[0])), "dp", split_axis=0, concat_axis=0, tiled=True
    )
    store, down_store, everyone = lax.optimization_barrier((keyvalue_page_store, adapter_down_weight, everyone))
    mirrored_store = swap(store, half)

    page_cap = max(2, 2 * page_count // peers)
    group = everyone[jnp.arange(half, dtype=jnp.int32) ^ me]
    group_owner = group[:, :page_count]
    group_local = group[:, page_count : 2 * page_count]
    group_order = earlier_alike(group_owner)
    near_asked = asked_of(me, group_owner, group_order, group_local, page_cap)
    far_asked = asked_of(me ^ half, group_owner, group_order, group_local, page_cap)
    all_owner = everyone[:, 2 * page_count : 2 * page_count + request_count]
    all_local = everyone[:, 2 * page_count + request_count :]
    adapter_asked = asked_of(me, all_owner, earlier_alike(all_owner), all_local, ADP_CAP).reshape(-1)
    adapter_pos = adapter_owner[:, 0] * ADP_CAP + earlier_alike(adapter_owner[:, 0])
    page_pos = (page_owner[:, 0] ^ me) * page_cap + earlier_alike(page_owner[:, 0])

    near = [store[near_asked[i]] for i in range(half)]
    near = [near[0]] + [swap(near[i], i) for i in range(1, half)]
    down_rows = down_store[adapter_asked]
    up_rows = adapter_up_weight[adapter_asked]

    piece = lax.all_gather(tokens, "tensor", axis=1, tiled=True)
    query_base = jnp.dot(piece, query_weight, preferred_element_type=jnp.float32)
    new_cache = jnp.dot(piece, keyvalue_weight, preferred_element_type=jnp.float32).astype(jnp.bfloat16)

    down_rows, mirrored_store, query_base, new_cache, *near = lax.optimization_barrier(
        (down_rows, mirrored_store, query_base, new_cache, *near)
    )
    down_sent = lax.all_to_all(down_rows, "dp", split_axis=0, concat_axis=0, tiled=True)
    far = [mirrored_store[far_asked[i]] for i in range(half)]
    far = [far[0]] + [swap(far[i], i) for i in range(1, half)]
    up_rows, down_sent = lax.optimization_barrier((up_rows, down_sent))
    up_sent = lax.all_to_all(up_rows, "dp", split_axis=0, concat_axis=0, tiled=True)

    lengths = span_token_length[0]
    ends = jnp.cumsum(lengths)
    starts = ends - lengths
    steps = jnp.arange(tok_rows, dtype=jnp.int32)[:, None]
    member = (steps >= starts[None, :]) & (steps < ends[None, :])
    slot = jnp.sum(jnp.where(member, adapter_pos[None, :], 0), axis=1)
    in_slot = slot[:, None] == jnp.arange(adapter_slots, dtype=jnp.int32)[None, :]

    down_part = jnp.einsum("tn,snk->tsk", tokens, down_sent, preferred_element_type=jnp.float32)
    shrink_part = jnp.sum(jnp.where(in_slot[:, :, None], down_part, 0.0), axis=1)
    shrink = lax.psum(shrink_part, "tensor").astype(jnp.bfloat16)
    shrink, *far = lax.optimization_barrier((shrink, *far))
    spread = jnp.where(in_slot[:, :, None], shrink[:, None, :], 0).reshape(tok_rows, adapter_slots * rank)
    prefix_pages = jnp.concatenate(near + far, axis=0)[page_pos]
    up = up_sent.reshape(adapter_slots * rank, q_cols)
    out = attend(query_base, spread, up, new_cache, prefix_pages, starts, ends)
    return (out, new_cache)


def solution(mesh):
    return jax.shard_map(
        on_device,
        mesh=mesh,
        in_specs=(
            P("dp", "tensor"),
            P(None, "tensor"),
            P(None, "tensor"),
            P("dp", "tensor", None),
            P("dp", None, "tensor"),
            P("dp", None, "tensor"),
            P("dp", None),
            P("dp", None),
            P("dp"),
            P("dp", None),
            P("dp"),
        ),
        out_specs=(P("dp", "tensor"), P("dp", "tensor")),
        check_vma=False,
    )
```

```python
import math

import jax
import jax.numpy as jnp
from jax import lax
from jax.experimental import pallas as pl
from jax.experimental.pallas import tpu as pltpu
from jax.sharding import PartitionSpec as P

HEAD_WIDTH = 128
ADP_CAP = 2
PAGE = 64
HITS = 4
MOST = 128
BLOCK = 32
TOGETHER = 4

ADAPTER_SCALE = 0.5
NEGATIVE = -1e30


def earlier_alike(owner):
    count = owner.shape[-1]
    ahead = jnp.arange(count, dtype=jnp.int32)[None, :] < jnp.arange(count, dtype=jnp.int32)[:, None]
    alike = owner[..., None, :] == owner[..., :, None]
    return jnp.sum((alike & ahead).astype(jnp.int32), axis=-1)


def asked_of(holder, owner, order, local, capacity):
    place = jnp.arange(capacity, dtype=jnp.int32)[None, :, None]
    match = (owner[:, None, :] == holder) & (order[:, None, :] == place)
    return jnp.sum(jnp.where(match, local[:, None, :], 0), axis=2)


def attention_steps(starts, ends, total):
    first = starts // BLOCK
    count = (ends - 1) // BLOCK - first + 1
    upto = jnp.cumsum(count)
    step = jnp.minimum(jnp.arange(total, dtype=jnp.int32), upto[-1] - 1)
    request = jnp.sum((upto[None, :] <= step[:, None]).astype(jnp.int32), axis=1)
    pick = request[:, None] == jnp.arange(starts.shape[0], dtype=jnp.int32)[None, :]

    def at(values):
        return jnp.sum(jnp.where(pick, values[None, :], 0), axis=1)

    block = at(first) + step - at(upto - count)
    return jnp.stack([request, block, at(starts), at(ends)])


def attention_kernel(
    steps_ref, spread_ref, up_ref, base_hbm, cache_hbm, pages_hbm, out_ref, query_ref, base_ref, cache_ref, pages_ref, sems
):
    copies = [
        pltpu.make_async_copy(base_hbm, base_ref, sems.at[0]),
        pltpu.make_async_copy(cache_hbm, cache_ref, sems.at[1]),
        pltpu.make_async_copy(pages_hbm, pages_ref, sems.at[2]),
    ]
    for copy in copies:
        copy.start()
    rows_total, q_cols = base_ref.shape
    kv_heads = cache_ref.shape[1] // (2 * HEAD_WIDTH)
    group = q_cols // HEAD_WIDTH // kv_heads
    window = min(rows_total, MOST + BLOCK)
    sharp = HEAD_WIDTH ** -0.5 * math.log2(math.e)
    copies[0].wait()

    def project(index, carry):
        cols = pl.ds(pl.multiple_of(index * 256, 256), 256)
        correction = jnp.dot(spread_ref[...], up_ref[:, cols], preferred_element_type=jnp.float32)
        query_ref[:, cols] = (base_ref[:, cols] + ADAPTER_SCALE * correction).astype(jnp.bfloat16)
        return carry

    lax.fori_loop(0, q_cols // 256, project, 0)

    copies[1].wait()
    copies[2].wait()
    dims = (((1,), (1,)), ((), ()))

    def several(turn, carry):
        places = []
        for lane in range(TOGETHER):
            index = turn * TOGETHER + lane
            row = pl.multiple_of(steps_ref[1, index] * BLOCK, BLOCK)
            start = steps_ref[2, index]
            base = pl.multiple_of(jnp.minimum(start // BLOCK * BLOCK, rows_total - window), BLOCK)
            old = pl.ds(steps_ref[0, index] * HITS, HITS)
            places.append((row, pl.ds(base, window), old, base, start, steps_ref[3, index]))
        chains = [(place, head) for place in places for head in range(kv_heads)]
        scores = []
        for (row, new, old, base, start, _), head in chains:
            at = head * 2 * HEAD_WIDTH
            wide = head * group * HEAD_WIDTH
            q_at = row + lax.broadcasted_iota(jnp.int32, (group * BLOCK, window), 0) % BLOCK
            k_at = base + lax.broadcasted_iota(jnp.int32, (group * BLOCK, window), 1)
            visible = (k_at >= start) & (k_at <= q_at)
            rows_q = jnp.concatenate(
                [
                    query_ref[pl.ds(row, BLOCK), wide + g * HEAD_WIDTH : wide + (g + 1) * HEAD_WIDTH]
                    for g in range(group)
                ],
                axis=0,
            )
            old_k = pages_ref[old, :, at : at + HEAD_WIDTH].reshape(HITS * PAGE, HEAD_WIDTH)
            new_k = cache_ref[new, at : at + HEAD_WIDTH]
            old_s = lax.dot_general(rows_q, old_k, dims, preferred_element_type=jnp.float32)
            new_s = lax.dot_general(rows_q, new_k, dims, preferred_element_type=jnp.float32)
            scores.append((old_s, jnp.where(visible, new_s, NEGATIVE)))
        weights = []
        for old_s, new_s in scores:
            top = jnp.maximum(
                jnp.max(old_s, axis=1, keepdims=True), jnp.max(new_s, axis=1, keepdims=True)
            )
            old_e = jnp.exp2((old_s - top) * sharp)
            new_e = jnp.exp2((new_s - top) * sharp)
            total = jnp.sum(old_e, axis=1, keepdims=True) + jnp.sum(new_e, axis=1, keepdims=True)
            weights.append((old_e.astype(jnp.bfloat16), new_e.astype(jnp.bfloat16), total))
        results = []
        for ((_, new, old, _, _, _), head), (old_e, new_e, total) in zip(chains, weights):
            at = head * 2 * HEAD_WIDTH + HEAD_WIDTH
            old_v = pages_ref[old, :, at : at + HEAD_WIDTH].reshape(HITS * PAGE, HEAD_WIDTH)
            new_v = cache_ref[new, at : at + HEAD_WIDTH]
            summed = jnp.dot(old_e, old_v, preferred_element_type=jnp.float32)
            summed += jnp.dot(new_e, new_v, preferred_element_type=jnp.float32)
            results.append((summed / total).astype(jnp.bfloat16))
        for ((row, _, _, _, start, end), head), result in zip(chains, results):
            own_at = row + lax.broadcasted_iota(jnp.int32, (BLOCK, HEAD_WIDTH), 0)
            own = (own_at >= start) & (own_at < end)
            for g in range(group):
                col = (head * group + g) * HEAD_WIDTH
                cols = slice(col, col + HEAD_WIDTH)
                before = out_ref[pl.ds(row, BLOCK), cols]
                out_ref[pl.ds(row, BLOCK), cols] = jnp.where(own, result[g * BLOCK : (g + 1) * BLOCK], before)
        return carry

    lax.fori_loop(0, steps_ref.shape[1] // TOGETHER, several, 0)


def attend(query_base, spread, up, cache, pages, starts, ends):
    rows, q_cols = query_base.shape
    steps_total = -(-(rows // BLOCK + starts.shape[0] - 1) // TOGETHER) * TOGETHER
    steps = attention_steps(starts, ends, steps_total)
    vmem = pl.BlockSpec(memory_space=pltpu.VMEM)
    return pl.pallas_call(
        attention_kernel,
        out_shape=jax.ShapeDtypeStruct((rows, q_cols), jnp.bfloat16),
        in_specs=[pl.BlockSpec(memory_space=pltpu.SMEM)] + [vmem] * 2 + [pl.BlockSpec(memory_space=pl.ANY)] * 3,
        out_specs=vmem,
        scratch_shapes=[
            pltpu.VMEM((rows, q_cols), jnp.bfloat16),
            pltpu.VMEM(query_base.shape, query_base.dtype),
            pltpu.VMEM(cache.shape, cache.dtype),
            pltpu.VMEM(pages.shape, pages.dtype),
            pltpu.SemaphoreType.DMA((3,)),
        ],
        compiler_params=pltpu.CompilerParams(vmem_limit_bytes=48 * 1024 * 1024),
        cost_estimate=pl.CostEstimate(
            flops=4 * steps_total * BLOCK * q_cols * (HITS * PAGE + MOST + BLOCK) + 2 * spread.size * q_cols,
            bytes_accessed=4 * query_base.size + 2 * (2 * spread.size + up.size + cache.size + pages.size),
            transcendentals=0,
        ),
        name="attend",
    )(steps, spread, up, query_base, cache, pages)


def serve_kernel(asked_ref, store_ref, *refs):
    outs, sems = refs[:-1], refs[-1]
    for index, out in enumerate(outs):
        for place in range(out.shape[0]):
            page = asked_ref[index * out.shape[0] + place]
            pltpu.make_async_copy(store_ref.at[page], out.at[place], sems.at[index]).start()
    for index, out in enumerate(outs):
        pltpu.make_async_copy(out, out, sems.at[index]).wait()


def serve(asked, store):
    blocks, capacity = asked.shape
    anywhere = pl.BlockSpec(memory_space=pl.ANY)
    shape = (capacity,) + store.shape[1:]
    return pl.pallas_call(
        serve_kernel,
        out_shape=[jax.ShapeDtypeStruct(shape, store.dtype)] * blocks,
        in_specs=[pl.BlockSpec(memory_space=pltpu.SMEM), anywhere],
        out_specs=[anywhere] * blocks,
        scratch_shapes=[pltpu.SemaphoreType.DMA((blocks,))],
        cost_estimate=pl.CostEstimate(
            flops=0, bytes_accessed=4 * blocks * math.prod(shape), transcendentals=0
        ),
        name="serve",
    )(asked.reshape(-1), store)


def assemble_kernel(source_ref, place_ref, *refs):
    sources, out, sem = refs[:-2], refs[-2], refs[-1]

    def one(index, carry):
        source = source_ref[index]
        place = place_ref[index]
        for number, ref in enumerate(sources):

            @pl.when(source == number)
            def _():
                pltpu.make_async_copy(ref.at[place], out.at[index], sem).start()

        return carry

    lax.fori_loop(0, out.shape[0], one, 0)
    pltpu.make_async_copy(out, out, sem).wait()


def assemble(source, place, sources):
    anywhere = pl.BlockSpec(memory_space=pl.ANY)
    scalars = pl.BlockSpec(memory_space=pltpu.SMEM)
    shape = (source.shape[0],) + sources[0].shape[1:]
    return pl.pallas_call(
        assemble_kernel,
        out_shape=jax.ShapeDtypeStruct(shape, sources[0].dtype),
        in_specs=[scalars, scalars] + [anywhere] * len(sources),
        out_specs=anywhere,
        scratch_shapes=[pltpu.SemaphoreType.DMA],
        cost_estimate=pl.CostEstimate(flops=0, bytes_accessed=4 * math.prod(shape), transcendentals=0),
        name="assemble",
    )(source, place, *sources)


def on_device(
    tokens,
    query_weight,
    keyvalue_weight,
    adapter_down_weight,
    adapter_up_weight,
    keyvalue_page_store,
    span_token_length,
    adapter_owner,
    adapter_local_index,
    page_owner,
    page_local_index,
):
    peers = lax.axis_size("dp")
    half = peers // 2
    me = lax.axis_index("dp")
    tok_rows = tokens.shape[0]
    q_cols = query_weight.shape[1]
    rank = adapter_down_weight.shape[2]
    adapter_slots = peers * ADP_CAP

    def swap(array, distance):
        return lax.ppermute(array, "dp", [(peer, peer ^ distance) for peer in range(peers)])

    page_count = page_local_index.shape[0]
    request_count = adapter_local_index.shape[0]
    raw = jnp.concatenate([page_owner[:, 0], page_local_index, adapter_owner[:, 0], adapter_local_index])
    everyone = lax.all_to_all(
        jnp.broadcast_to(raw[None], (peers, raw.shape[0])), "dp", split_axis=0, concat_axis=0, tiled=True
    )
    store, down_store, everyone = lax.optimization_barrier((keyvalue_page_store, adapter_down_weight, everyone))
    mirrored_store = swap(store, half)

    page_cap = max(2, 2 * page_count // peers)
    group = everyone[jnp.arange(half, dtype=jnp.int32) ^ me]
    group_owner = group[:, :page_count]
    group_local = group[:, page_count : 2 * page_count]
    group_order = earlier_alike(group_owner)
    near_asked = asked_of(me, group_owner, group_order, group_local, page_cap)
    far_asked = asked_of(me ^ half, group_owner, group_order, group_local, page_cap)
    all_owner = everyone[:, 2 * page_count : 2 * page_count + request_count]
    all_local = everyone[:, 2 * page_count + request_count :]
    adapter_asked = asked_of(me, all_owner, earlier_alike(all_owner), all_local, ADP_CAP).reshape(-1)
    adapter_pos = adapter_owner[:, 0] * ADP_CAP + earlier_alike(adapter_owner[:, 0])
    page_source = page_owner[:, 0] ^ me
    page_place = jnp.where(page_source % half == 0, page_local_index, earlier_alike(page_owner[:, 0]))

    near = serve(near_asked[1:], store)
    near = [swap(pages, i + 1) for i, pages in enumerate(near)]
    down_rows = down_store[adapter_asked]
    up_rows = adapter_up_weight[adapter_asked]

    piece = lax.all_gather(tokens, "tensor", axis=1, tiled=True)
    query_base = jnp.dot(piece, query_weight, preferred_element_type=jnp.float32)
    new_cache = jnp.dot(piece, keyvalue_weight, preferred_element_type=jnp.float32).astype(jnp.bfloat16)

    down_rows, mirrored_store, query_base, new_cache, *near = lax.optimization_barrier(
        (down_rows, mirrored_store, query_base, new_cache, *near)
    )
    down_sent = lax.all_to_all(down_rows, "dp", split_axis=0, concat_axis=0, tiled=True)
    far = serve(far_asked[1:], mirrored_store)
    far = [swap(pages, i + 1) for i, pages in enumerate(far)]
    up_rows, down_sent, *far = lax.optimization_barrier((up_rows, down_sent, *far))
    up_sent = lax.all_to_all(up_rows, "dp", split_axis=0, concat_axis=0, tiled=True)

    lengths = span_token_length[0]
    ends = jnp.cumsum(lengths)
    starts = ends - lengths
    steps = jnp.arange(tok_rows, dtype=jnp.int32)[:, None]
    member = (steps >= starts[None, :]) & (steps < ends[None, :])
    slot = jnp.sum(jnp.where(member, adapter_pos[None, :], 0), axis=1)
    in_slot = slot[:, None] == jnp.arange(adapter_slots, dtype=jnp.int32)[None, :]

    down_part = jnp.einsum("tn,snk->tsk", tokens, down_sent, preferred_element_type=jnp.float32)
    shrink_part = jnp.sum(jnp.where(in_slot[:, :, None], down_part, 0.0), axis=1)
    shrink = lax.psum(shrink_part, "tensor").astype(jnp.bfloat16)
    spread = jnp.where(in_slot[:, :, None], shrink[:, None, :], 0).reshape(tok_rows, adapter_slots * rank)
    prefix_pages = assemble(page_source, page_place, [store, *near, mirrored_store, *far])
    up = up_sent.reshape(adapter_slots * rank, q_cols)
    out = attend(query_base, spread, up, new_cache, prefix_pages, starts, ends)
    return (out, new_cache)


def solution(mesh):
    return jax.shard_map(
        on_device,
        mesh=mesh,
        in_specs=(
            P("dp", "tensor"),
            P(None, "tensor"),
            P(None, "tensor"),
            P("dp", "tensor", None),
            P("dp", None, "tensor"),
            P("dp", None, "tensor"),
            P("dp", None),
            P("dp", None),
            P("dp"),
            P("dp", None),
            P("dp"),
        ),
        out_specs=(P("dp", "tensor"), P("dp", "tensor")),
        check_vma=False,
    )
```

```python
import math

import jax
import jax.numpy as jnp
from jax import lax
from jax.experimental import pallas as pl
from jax.experimental.pallas import tpu as pltpu
from jax.sharding import PartitionSpec as P

HEAD_WIDTH = 128
ADP_CAP = 2
PAGE = 64
HITS = 4
MOST = 128
BLOCK = 32
TOGETHER = 4

ADAPTER_SCALE = 0.5
NEGATIVE = -1e30


def earlier_alike(owner):
    count = owner.shape[-1]
    ahead = jnp.arange(count, dtype=jnp.int32)[None, :] < jnp.arange(count, dtype=jnp.int32)[:, None]
    alike = owner[..., None, :] == owner[..., :, None]
    return jnp.sum((alike & ahead).astype(jnp.int32), axis=-1)


def asked_of(holder, owner, order, local, capacity):
    place = jnp.arange(capacity, dtype=jnp.int32)[None, :, None]
    match = (owner[:, None, :] == holder) & (order[:, None, :] == place)
    return jnp.sum(jnp.where(match, local[:, None, :], 0), axis=2)


def attention_steps(starts, ends, total):
    first = starts // BLOCK
    count = (ends - 1) // BLOCK - first + 1
    upto = jnp.cumsum(count)
    step = jnp.minimum(jnp.arange(total, dtype=jnp.int32), upto[-1] - 1)
    request = jnp.sum((upto[None, :] <= step[:, None]).astype(jnp.int32), axis=1)
    pick = request[:, None] == jnp.arange(starts.shape[0], dtype=jnp.int32)[None, :]

    def at(values):
        return jnp.sum(jnp.where(pick, values[None, :], 0), axis=1)

    block = at(first) + step - at(upto - count)
    return jnp.stack([request, block, at(starts), at(ends)])


def attention_kernel(
    steps_ref, spread_ref, up_ref, base_hbm, cache_hbm, pages_hbm, out_ref, query_ref, base_ref, cache_ref, pages_ref, sems
):
    copies = [
        pltpu.make_async_copy(base_hbm, base_ref, sems.at[0]),
        pltpu.make_async_copy(cache_hbm, cache_ref, sems.at[1]),
        pltpu.make_async_copy(pages_hbm, pages_ref, sems.at[2]),
    ]
    for copy in copies:
        copy.start()
    rows_total, q_cols = base_ref.shape
    kv_heads = cache_ref.shape[1] // (2 * HEAD_WIDTH)
    group = q_cols // HEAD_WIDTH // kv_heads
    window = min(rows_total, MOST + BLOCK)
    sharp = HEAD_WIDTH ** -0.5 * math.log2(math.e)
    copies[0].wait()

    def project(index, carry):
        cols = pl.ds(pl.multiple_of(index * 256, 256), 256)
        correction = jnp.dot(spread_ref[...], up_ref[:, cols], preferred_element_type=jnp.float32)
        query_ref[:, cols] = (base_ref[:, cols] + ADAPTER_SCALE * correction).astype(jnp.bfloat16)
        return carry

    lax.fori_loop(0, q_cols // 256, project, 0)

    copies[1].wait()
    copies[2].wait()
    dims = (((1,), (1,)), ((), ()))

    def several(turn, carry):
        places = []
        for lane in range(TOGETHER):
            index = turn * TOGETHER + lane
            row = pl.multiple_of(steps_ref[1, index] * BLOCK, BLOCK)
            start = steps_ref[2, index]
            base = pl.multiple_of(jnp.minimum(start // BLOCK * BLOCK, rows_total - window), BLOCK)
            old = pl.ds(steps_ref[0, index] * HITS, HITS)
            places.append((row, pl.ds(base, window), old, base, start, steps_ref[3, index]))
        chains = [(place, head) for place in places for head in range(kv_heads)]
        scores = []
        for (row, new, old, base, start, _), head in chains:
            at = head * 2 * HEAD_WIDTH
            wide = head * group * HEAD_WIDTH
            q_at = row + lax.broadcasted_iota(jnp.int32, (group * BLOCK, window), 0) % BLOCK
            k_at = base + lax.broadcasted_iota(jnp.int32, (group * BLOCK, window), 1)
            visible = (k_at >= start) & (k_at <= q_at)
            rows_q = jnp.concatenate(
                [
                    query_ref[pl.ds(row, BLOCK), wide + g * HEAD_WIDTH : wide + (g + 1) * HEAD_WIDTH]
                    for g in range(group)
                ],
                axis=0,
            )
            old_k = pages_ref[old, :, at : at + HEAD_WIDTH].reshape(HITS * PAGE, HEAD_WIDTH)
            new_k = cache_ref[new, at : at + HEAD_WIDTH]
            old_s = lax.dot_general(rows_q, old_k, dims, preferred_element_type=jnp.float32)
            new_s = lax.dot_general(rows_q, new_k, dims, preferred_element_type=jnp.float32)
            scores.append((old_s, jnp.where(visible, new_s, NEGATIVE)))
        weights = []
        for old_s, new_s in scores:
            top = jnp.maximum(
                jnp.max(old_s, axis=1, keepdims=True), jnp.max(new_s, axis=1, keepdims=True)
            )
            old_e = jnp.exp2((old_s - top) * sharp)
            new_e = jnp.exp2((new_s - top) * sharp)
            total = jnp.sum(old_e, axis=1, keepdims=True) + jnp.sum(new_e, axis=1, keepdims=True)
            weights.append((old_e.astype(jnp.bfloat16), new_e.astype(jnp.bfloat16), total))
        results = []
        for ((_, new, old, _, _, _), head), (old_e, new_e, total) in zip(chains, weights):
            at = head * 2 * HEAD_WIDTH + HEAD_WIDTH
            old_v = pages_ref[old, :, at : at + HEAD_WIDTH].reshape(HITS * PAGE, HEAD_WIDTH)
            new_v = cache_ref[new, at : at + HEAD_WIDTH]
            summed = jnp.dot(old_e, old_v, preferred_element_type=jnp.float32)
            summed += jnp.dot(new_e, new_v, preferred_element_type=jnp.float32)
            results.append((summed / total).astype(jnp.bfloat16))
        for ((row, _, _, _, start, end), head), result in zip(chains, results):
            own_at = row + lax.broadcasted_iota(jnp.int32, (BLOCK, HEAD_WIDTH), 0)
            own = (own_at >= start) & (own_at < end)
            for g in range(group):
                col = (head * group + g) * HEAD_WIDTH
                cols = slice(col, col + HEAD_WIDTH)
                before = out_ref[pl.ds(row, BLOCK), cols]
                out_ref[pl.ds(row, BLOCK), cols] = jnp.where(own, result[g * BLOCK : (g + 1) * BLOCK], before)
        return carry

    lax.fori_loop(0, steps_ref.shape[1] // TOGETHER, several, 0)


def attend(query_base, spread, up, cache, pages, starts, ends):
    rows, q_cols = query_base.shape
    steps_total = -(-(rows // BLOCK + starts.shape[0] - 1) // TOGETHER) * TOGETHER
    steps = attention_steps(starts, ends, steps_total)
    vmem = pl.BlockSpec(memory_space=pltpu.VMEM)
    return pl.pallas_call(
        attention_kernel,
        out_shape=jax.ShapeDtypeStruct((rows, q_cols), jnp.bfloat16),
        in_specs=[pl.BlockSpec(memory_space=pltpu.SMEM)] + [vmem] * 2 + [pl.BlockSpec(memory_space=pl.ANY)] * 3,
        out_specs=vmem,
        scratch_shapes=[
            pltpu.VMEM((rows, q_cols), jnp.bfloat16),
            pltpu.VMEM(query_base.shape, query_base.dtype),
            pltpu.VMEM(cache.shape, cache.dtype),
            pltpu.VMEM(pages.shape, pages.dtype),
            pltpu.SemaphoreType.DMA((3,)),
        ],
        compiler_params=pltpu.CompilerParams(vmem_limit_bytes=48 * 1024 * 1024),
        cost_estimate=pl.CostEstimate(
            flops=4 * steps_total * BLOCK * q_cols * (HITS * PAGE + MOST + BLOCK) + 2 * spread.size * q_cols,
            bytes_accessed=4 * query_base.size + 2 * (2 * spread.size + up.size + cache.size + pages.size),
            transcendentals=0,
        ),
        name="attend",
    )(steps, spread, up, query_base, cache, pages)


def serve_kernel(asked_ref, store_ref, *refs):
    outs, sems = refs[:-1], refs[-1]
    for index, out in enumerate(outs):
        for place in range(out.shape[0]):
            page = asked_ref[index * out.shape[0] + place]
            pltpu.make_async_copy(store_ref.at[page], out.at[place], sems.at[index]).start()
    for index, out in enumerate(outs):
        pltpu.make_async_copy(out, out, sems.at[index]).wait()


def serve(asked, store):
    blocks, capacity = asked.shape
    anywhere = pl.BlockSpec(memory_space=pl.ANY)
    shape = (capacity,) + store.shape[1:]
    return pl.pallas_call(
        serve_kernel,
        out_shape=[jax.ShapeDtypeStruct(shape, store.dtype)] * blocks,
        in_specs=[pl.BlockSpec(memory_space=pltpu.SMEM), anywhere],
        out_specs=[pl.BlockSpec(memory_space=pltpu.VMEM)] * blocks,
        scratch_shapes=[pltpu.SemaphoreType.DMA((blocks,))],
        compiler_params=pltpu.CompilerParams(vmem_limit_bytes=16 * 1024 * 1024),
        cost_estimate=pl.CostEstimate(
            flops=0, bytes_accessed=4 * blocks * math.prod(shape), transcendentals=0
        ),
        name="serve",
    )(asked.reshape(-1), store)


def assemble_kernel(source_ref, place_ref, *refs):
    sources, out, sem = refs[:-2], refs[-2], refs[-1]

    def one(index, carry):
        source = source_ref[index]
        place = place_ref[index]
        for number, ref in enumerate(sources):

            @pl.when(source == number)
            def _():
                pltpu.make_async_copy(ref.at[place], out.at[index], sem).start()

        return carry

    lax.fori_loop(0, out.shape[0], one, 0)
    pltpu.make_async_copy(out, out, sem).wait()


def assemble(source, place, sources):
    anywhere = pl.BlockSpec(memory_space=pl.ANY)
    scalars = pl.BlockSpec(memory_space=pltpu.SMEM)
    shape = (source.shape[0],) + sources[0].shape[1:]
    return pl.pallas_call(
        assemble_kernel,
        out_shape=jax.ShapeDtypeStruct(shape, sources[0].dtype),
        in_specs=[scalars, scalars] + [anywhere] * len(sources),
        out_specs=pl.BlockSpec(memory_space=pltpu.VMEM),
        scratch_shapes=[pltpu.SemaphoreType.DMA],
        compiler_params=pltpu.CompilerParams(vmem_limit_bytes=16 * 1024 * 1024),
        cost_estimate=pl.CostEstimate(flops=0, bytes_accessed=4 * math.prod(shape), transcendentals=0),
        name="assemble",
    )(source, place, *sources)


def on_device(
    tokens,
    query_weight,
    keyvalue_weight,
    adapter_down_weight,
    adapter_up_weight,
    keyvalue_page_store,
    span_token_length,
    adapter_owner,
    adapter_local_index,
    page_owner,
    page_local_index,
):
    peers = lax.axis_size("dp")
    half = peers // 2
    me = lax.axis_index("dp")
    tok_rows = tokens.shape[0]
    q_cols = query_weight.shape[1]
    rank = adapter_down_weight.shape[2]
    adapter_slots = peers * ADP_CAP

    def swap(array, distance):
        return lax.ppermute(array, "dp", [(peer, peer ^ distance) for peer in range(peers)])

    page_count = page_local_index.shape[0]
    request_count = adapter_local_index.shape[0]
    raw = jnp.concatenate([page_owner[:, 0], page_local_index, adapter_owner[:, 0], adapter_local_index])
    everyone = lax.all_to_all(
        jnp.broadcast_to(raw[None], (peers, raw.shape[0])), "dp", split_axis=0, concat_axis=0, tiled=True
    )
    store, down_store, everyone = lax.optimization_barrier((keyvalue_page_store, adapter_down_weight, everyone))
    mirrored_store = swap(store, half)

    page_cap = max(2, 2 * page_count // peers)
    group = everyone[jnp.arange(half, dtype=jnp.int32) ^ me]
    group_owner = group[:, :page_count]
    group_local = group[:, page_count : 2 * page_count]
    group_order = earlier_alike(group_owner)
    near_asked = asked_of(me, group_owner, group_order, group_local, page_cap)
    far_asked = asked_of(me ^ half, group_owner, group_order, group_local, page_cap)
    all_owner = everyone[:, 2 * page_count : 2 * page_count + request_count]
    all_local = everyone[:, 2 * page_count + request_count :]
    adapter_asked = asked_of(me, all_owner, earlier_alike(all_owner), all_local, ADP_CAP).reshape(-1)
    adapter_pos = adapter_owner[:, 0] * ADP_CAP + earlier_alike(adapter_owner[:, 0])
    page_source = page_owner[:, 0] ^ me
    page_place = jnp.where(page_source % half == 0, page_local_index, earlier_alike(page_owner[:, 0]))

    near = serve(near_asked[1:], store)
    near = [swap(pages, i + 1) for i, pages in enumerate(near)]
    down_rows = down_store[adapter_asked]
    up_rows = adapter_up_weight[adapter_asked]

    piece = lax.all_gather(tokens, "tensor", axis=1, tiled=True)
    query_base = jnp.dot(piece, query_weight, preferred_element_type=jnp.float32)
    new_cache = jnp.dot(piece, keyvalue_weight, preferred_element_type=jnp.float32).astype(jnp.bfloat16)

    down_rows, mirrored_store, query_base, new_cache, *near = lax.optimization_barrier(
        (down_rows, mirrored_store, query_base, new_cache, *near)
    )
    down_sent = lax.all_to_all(down_rows, "dp", split_axis=0, concat_axis=0, tiled=True)
    far = serve(far_asked[1:], mirrored_store)
    far = [swap(pages, i + 1) for i, pages in enumerate(far)]
    up_rows, down_sent, *far = lax.optimization_barrier((up_rows, down_sent, *far))
    up_sent = lax.all_to_all(up_rows, "dp", split_axis=0, concat_axis=0, tiled=True)

    lengths = span_token_length[0]
    ends = jnp.cumsum(lengths)
    starts = ends - lengths
    steps = jnp.arange(tok_rows, dtype=jnp.int32)[:, None]
    member = (steps >= starts[None, :]) & (steps < ends[None, :])
    slot = jnp.sum(jnp.where(member, adapter_pos[None, :], 0), axis=1)
    in_slot = slot[:, None] == jnp.arange(adapter_slots, dtype=jnp.int32)[None, :]

    down_part = jnp.einsum("tn,snk->tsk", tokens, down_sent, preferred_element_type=jnp.float32)
    shrink_part = jnp.sum(jnp.where(in_slot[:, :, None], down_part, 0.0), axis=1)
    shrink = lax.psum(shrink_part, "tensor").astype(jnp.bfloat16)
    spread = jnp.where(in_slot[:, :, None], shrink[:, None, :], 0).reshape(tok_rows, adapter_slots * rank)
    prefix_pages = assemble(page_source, page_place, [store, *near, mirrored_store, *far])
    up = up_sent.reshape(adapter_slots * rank, q_cols)
    out = attend(query_base, spread, up, new_cache, prefix_pages, starts, ends)
    return (out, new_cache)


def solution(mesh):
    return jax.shard_map(
        on_device,
        mesh=mesh,
        in_specs=(
            P("dp", "tensor"),
            P(None, "tensor"),
            P(None, "tensor"),
            P("dp", "tensor", None),
            P("dp", None, "tensor"),
            P("dp", None, "tensor"),
            P("dp", None),
            P("dp", None),
            P("dp"),
            P("dp", None),
            P("dp"),
        ),
        out_specs=(P("dp", "tensor"), P("dp", "tensor")),
        check_vma=False,
    )
```

```python
import math

import jax
import jax.numpy as jnp
from jax import lax
from jax.experimental import pallas as pl
from jax.experimental.pallas import tpu as pltpu
from jax.sharding import PartitionSpec as P

HEAD_WIDTH = 128
ADP_CAP = 2
PAGE = 64
HITS = 4
MOST = 128
BLOCK = 32
TOGETHER = 4
HALVES = 2

ADAPTER_SCALE = 0.5
NEGATIVE = -1e30


def earlier_alike(owner):
    count = owner.shape[-1]
    ahead = jnp.arange(count, dtype=jnp.int32)[None, :] < jnp.arange(count, dtype=jnp.int32)[:, None]
    alike = owner[..., None, :] == owner[..., :, None]
    return jnp.sum((alike & ahead).astype(jnp.int32), axis=-1)


def asked_of(holder, owner, order, local, capacity):
    place = jnp.arange(capacity, dtype=jnp.int32)[None, :, None]
    match = (owner[:, None, :] == holder) & (order[:, None, :] == place)
    return jnp.sum(jnp.where(match, local[:, None, :], 0), axis=2)


def attention_steps(starts, ends, total):
    first = starts // BLOCK
    count = (ends - 1) // BLOCK - first + 1
    upto = jnp.cumsum(count)
    step = jnp.minimum(jnp.arange(total, dtype=jnp.int32), upto[-1] - 1)
    request = jnp.sum((upto[None, :] <= step[:, None]).astype(jnp.int32), axis=1)
    pick = request[:, None] == jnp.arange(starts.shape[0], dtype=jnp.int32)[None, :]

    def at(values):
        return jnp.sum(jnp.where(pick, values[None, :], 0), axis=1)

    block = at(first) + step - at(upto - count)
    return jnp.stack([request, block, at(starts), at(ends)])


def attention_kernel(steps_ref, spread_hbm, up_hbm, base_hbm, cache_hbm, pages_hbm, out_ref, query_ref, *rest):
    spread_ref, up_ref, base_ref, cache_ref, pages_ref, sems = rest
    pairs = [(spread_hbm, spread_ref), (up_hbm, up_ref), (base_hbm, base_ref), (cache_hbm, cache_ref), (pages_hbm, pages_ref)]
    copies = [pltpu.make_async_copy(*pair, sems.at[index]) for index, pair in enumerate(pairs)]
    for copy in copies:
        copy.start()
    rows_total, q_cols = base_ref.shape
    kv_heads = cache_ref.shape[1] // (2 * HEAD_WIDTH)
    group = q_cols // HEAD_WIDTH // kv_heads
    window = min(rows_total, MOST + BLOCK)
    sharp = HEAD_WIDTH ** -0.5 * math.log2(math.e)
    for copy in copies[:3]:
        copy.wait()

    def project(index, carry):
        cols = pl.ds(pl.multiple_of(index * 256, 256), 256)
        correction = jnp.dot(spread_ref[...], up_ref[:, cols], preferred_element_type=jnp.float32)
        query_ref[:, cols] = (base_ref[:, cols] + ADAPTER_SCALE * correction).astype(jnp.bfloat16)
        return carry

    lax.fori_loop(0, q_cols // 256, project, 0)

    for copy in copies[3:]:
        copy.wait()
    dims = (((1,), (1,)), ((), ()))

    def several(turn, carry):
        places = []
        for lane in range(TOGETHER):
            index = turn * TOGETHER + lane
            row = pl.multiple_of(steps_ref[1, index] * BLOCK, BLOCK)
            start = steps_ref[2, index]
            base = pl.multiple_of(jnp.minimum(start // BLOCK * BLOCK, rows_total - window), BLOCK)
            old = pl.ds(steps_ref[0, index] * HITS, HITS)
            places.append((row, pl.ds(base, window), old, base, start, steps_ref[3, index]))
        chains = [(place, head) for place in places for head in range(kv_heads)]
        scores = []
        for (row, new, old, base, start, _), head in chains:
            at = head * 2 * HEAD_WIDTH
            wide = head * group * HEAD_WIDTH
            q_at = row + lax.broadcasted_iota(jnp.int32, (group * BLOCK, window), 0) % BLOCK
            k_at = base + lax.broadcasted_iota(jnp.int32, (group * BLOCK, window), 1)
            visible = (k_at >= start) & (k_at <= q_at)
            rows_q = jnp.concatenate(
                [
                    query_ref[pl.ds(row, BLOCK), wide + g * HEAD_WIDTH : wide + (g + 1) * HEAD_WIDTH]
                    for g in range(group)
                ],
                axis=0,
            )
            old_k = pages_ref[old, :, at : at + HEAD_WIDTH].reshape(HITS * PAGE, HEAD_WIDTH)
            new_k = cache_ref[new, at : at + HEAD_WIDTH]
            old_s = lax.dot_general(rows_q, old_k, dims, preferred_element_type=jnp.float32)
            new_s = lax.dot_general(rows_q, new_k, dims, preferred_element_type=jnp.float32)
            scores.append((old_s, jnp.where(visible, new_s, NEGATIVE)))
        weights = []
        for old_s, new_s in scores:
            top = jnp.maximum(
                jnp.max(old_s, axis=1, keepdims=True), jnp.max(new_s, axis=1, keepdims=True)
            )
            old_e = jnp.exp2((old_s - top) * sharp)
            new_e = jnp.exp2((new_s - top) * sharp)
            total = jnp.sum(old_e, axis=1, keepdims=True) + jnp.sum(new_e, axis=1, keepdims=True)
            weights.append((old_e.astype(jnp.bfloat16), new_e.astype(jnp.bfloat16), total))
        results = []
        for ((_, new, old, _, _, _), head), (old_e, new_e, total) in zip(chains, weights):
            at = head * 2 * HEAD_WIDTH + HEAD_WIDTH
            old_v = pages_ref[old, :, at : at + HEAD_WIDTH].reshape(HITS * PAGE, HEAD_WIDTH)
            new_v = cache_ref[new, at : at + HEAD_WIDTH]
            summed = jnp.dot(old_e, old_v, preferred_element_type=jnp.float32)
            summed += jnp.dot(new_e, new_v, preferred_element_type=jnp.float32)
            results.append((summed / total).astype(jnp.bfloat16))
        for ((row, _, _, _, start, end), head), result in zip(chains, results):
            own_at = row + lax.broadcasted_iota(jnp.int32, (BLOCK, HEAD_WIDTH), 0)
            own = (own_at >= start) & (own_at < end)
            for g in range(group):
                col = (head * group + g) * HEAD_WIDTH
                cols = slice(col, col + HEAD_WIDTH)
                before = out_ref[pl.ds(row, BLOCK), cols]
                out_ref[pl.ds(row, BLOCK), cols] = jnp.where(own, result[g * BLOCK : (g + 1) * BLOCK], before)
        return carry

    lax.fori_loop(0, steps_ref.shape[1] // TOGETHER, several, 0)


def attend(query_base, spread, up, cache, pages, starts, ends):
    rows, q_cols = query_base.shape
    steps_total = -(-(rows // BLOCK + starts.shape[0] - 1) // TOGETHER) * TOGETHER
    steps = attention_steps(starts, ends, steps_total)
    return pl.pallas_call(
        attention_kernel,
        out_shape=jax.ShapeDtypeStruct((rows, q_cols), jnp.bfloat16),
        in_specs=[pl.BlockSpec(memory_space=pltpu.SMEM)] + [pl.BlockSpec(memory_space=pltpu.HBM)] * 5,
        out_specs=pl.BlockSpec(memory_space=pltpu.VMEM),
        scratch_shapes=[
            pltpu.VMEM((rows, q_cols), jnp.bfloat16),
            *[pltpu.VMEM(each.shape, each.dtype) for each in (spread, up, query_base, cache, pages)],
            pltpu.SemaphoreType.DMA((5,)),
        ],
        compiler_params=pltpu.CompilerParams(vmem_limit_bytes=48 * 1024 * 1024),
        cost_estimate=pl.CostEstimate(
            flops=4 * steps_total * BLOCK * q_cols * (HITS * PAGE + MOST + BLOCK) + 2 * spread.size * q_cols,
            bytes_accessed=4 * query_base.size + 2 * (2 * spread.size + up.size + cache.size + pages.size),
            transcendentals=0,
        ),
        name="attend",
    )(steps, spread, up, query_base, cache, pages)


def serve_kernel(asked_ref, store_ref, *refs):
    outs, sems = refs[:-1], refs[-1]
    for index, out in enumerate(outs):
        for place in range(out.shape[0]):
            page = asked_ref[index * out.shape[0] + place]
            pltpu.make_async_copy(store_ref.at[page], out.at[place], sems.at[index]).start()
    for index, out in enumerate(outs):
        pltpu.make_async_copy(out, out, sems.at[index]).wait()


def serve(asked, store):
    blocks, capacity = asked.shape
    shape = (capacity,) + store.shape[1:]
    return pl.pallas_call(
        serve_kernel,
        out_shape=[jax.ShapeDtypeStruct(shape, store.dtype)] * blocks,
        in_specs=[pl.BlockSpec(memory_space=pltpu.SMEM), pl.BlockSpec(memory_space=pltpu.HBM)],
        out_specs=[pl.BlockSpec(memory_space=pltpu.VMEM)] * blocks,
        scratch_shapes=[pltpu.SemaphoreType.DMA((blocks,))],
        compiler_params=pltpu.CompilerParams(vmem_limit_bytes=16 * 1024 * 1024),
        cost_estimate=pl.CostEstimate(
            flops=0, bytes_accessed=4 * blocks * math.prod(shape), transcendentals=0
        ),
        name="serve",
    )(asked.reshape(-1), store)


def assemble_kernel(source_ref, place_ref, *refs):
    out, sem = refs[-2:]
    half = (len(refs) - 2) // (1 + HALVES)
    near, far = refs[:half], refs[half:-2]
    width = far[0].shape[2]

    def one(index, carry):
        source = source_ref[index]
        place = place_ref[index]
        for number in range(half):

            @pl.when(source == number)
            def _():
                pltpu.make_async_copy(near[number].at[place], out.at[index], sem).start()

            @pl.when(source == half + number)
            def _():
                for part in range(HALVES):
                    columns = out.at[index, :, part * width : (part + 1) * width]
                    pltpu.make_async_copy(far[part * half + number].at[place], columns, sem).start()

        return carry

    lax.fori_loop(0, out.shape[0], one, 0)
    pltpu.make_async_copy(out, out, sem).wait()


def assemble(source, place, near, far):
    scalars = pl.BlockSpec(memory_space=pltpu.SMEM)
    sources = [*near, *far]
    shape = (source.shape[0],) + near[0].shape[1:]
    return pl.pallas_call(
        assemble_kernel,
        out_shape=jax.ShapeDtypeStruct(shape, near[0].dtype),
        in_specs=[scalars, scalars] + [pl.BlockSpec(memory_space=pltpu.HBM)] * len(sources),
        out_specs=pl.BlockSpec(memory_space=pltpu.VMEM),
        scratch_shapes=[pltpu.SemaphoreType.DMA],
        compiler_params=pltpu.CompilerParams(vmem_limit_bytes=16 * 1024 * 1024),
        cost_estimate=pl.CostEstimate(flops=0, bytes_accessed=4 * math.prod(shape), transcendentals=0),
        name="assemble",
    )(source, place, *sources)


def on_device(
    tokens,
    query_weight,
    keyvalue_weight,
    adapter_down_weight,
    adapter_up_weight,
    keyvalue_page_store,
    span_token_length,
    adapter_owner,
    adapter_local_index,
    page_owner,
    page_local_index,
):
    peers = lax.axis_size("dp")
    half = peers // 2
    me = lax.axis_index("dp")
    tok_rows = tokens.shape[0]
    q_cols = query_weight.shape[1]
    rank = adapter_down_weight.shape[2]
    adapter_slots = peers * ADP_CAP

    def swap(array, distance):
        return lax.ppermute(array, "dp", [(peer, peer ^ distance) for peer in range(peers)])

    page_count = page_local_index.shape[0]
    request_count = adapter_local_index.shape[0]
    raw = jnp.concatenate([page_owner[:, 0], page_local_index, adapter_owner[:, 0], adapter_local_index])
    everyone = lax.all_to_all(
        jnp.broadcast_to(raw[None], (peers, raw.shape[0])), "dp", split_axis=0, concat_axis=0, tiled=True
    )
    width = keyvalue_page_store.shape[2] // HALVES
    parts = [keyvalue_page_store[:, :, part * width : (part + 1) * width] for part in range(HALVES)]
    store, down_store, everyone, *parts = lax.optimization_barrier(
        (keyvalue_page_store, adapter_down_weight, everyone, *parts)
    )

    page_cap = max(2, 2 * page_count // peers)
    group = everyone[jnp.arange(half, dtype=jnp.int32) ^ me]
    group_owner = group[:, :page_count]
    group_local = group[:, page_count : 2 * page_count]
    group_order = earlier_alike(group_owner)
    near_asked = asked_of(me, group_owner, group_order, group_local, page_cap)
    far_asked = asked_of(me ^ half, group_owner, group_order, group_local, page_cap)
    all_owner = everyone[:, 2 * page_count : 2 * page_count + request_count]
    all_local = everyone[:, 2 * page_count + request_count :]
    adapter_asked = asked_of(me, all_owner, earlier_alike(all_owner), all_local, ADP_CAP).reshape(-1)
    adapter_pos = adapter_owner[:, 0] * ADP_CAP + earlier_alike(adapter_owner[:, 0])
    page_source = page_owner[:, 0] ^ me
    page_place = jnp.where(page_source % half == 0, page_local_index, earlier_alike(page_owner[:, 0]))

    near = serve(near_asked[1:], store)
    near = [swap(pages, i + 1) for i, pages in enumerate(near)]
    down_rows = down_store[adapter_asked]
    up_rows = adapter_up_weight[adapter_asked]

    piece = lax.all_gather(tokens, "tensor", axis=1, tiled=True)
    query_base = jnp.dot(piece, query_weight, preferred_element_type=jnp.float32)
    new_cache = jnp.dot(piece, keyvalue_weight, preferred_element_type=jnp.float32).astype(jnp.bfloat16)

    mirrored = []
    far = []
    for part in range(HALVES):
        mirrored.append(swap(parts[part], half))
        if part + 1 < HALVES:
            mirrored[part], parts[part + 1], down_rows = lax.optimization_barrier(
                (mirrored[part], parts[part + 1], down_rows)
            )
        far.append(serve(far_asked[1:], mirrored[part]))
    down_sent = lax.all_to_all(down_rows, "dp", split_axis=0, concat_axis=0, tiled=True)
    far = [[swap(pages, i + 1) for i, pages in enumerate(block)] for block in far[:-1]] + far[-1:]
    up_rows, down_sent, query_base, new_cache, far, near = lax.optimization_barrier(
        (up_rows, down_sent, query_base, new_cache, far, near)
    )
    up_sent = lax.all_to_all(up_rows, "dp", split_axis=0, concat_axis=0, tiled=True)
    far[-1] = [swap(pages, i + 1) for i, pages in enumerate(far[-1])]

    lengths = span_token_length[0]
    ends = jnp.cumsum(lengths)
    starts = ends - lengths
    steps = jnp.arange(tok_rows, dtype=jnp.int32)[:, None]
    member = (steps >= starts[None, :]) & (steps < ends[None, :])
    slot = jnp.sum(jnp.where(member, adapter_pos[None, :], 0), axis=1)
    in_slot = slot[:, None] == jnp.arange(adapter_slots, dtype=jnp.int32)[None, :]

    down_part = jnp.einsum("tn,snk->tsk", tokens, down_sent, preferred_element_type=jnp.float32)
    shrink_part = jnp.sum(jnp.where(in_slot[:, :, None], down_part, 0.0), axis=1)
    shrink = lax.psum(shrink_part, "tensor").astype(jnp.bfloat16)
    spread = jnp.where(in_slot[:, :, None], shrink[:, None, :], 0).reshape(tok_rows, adapter_slots * rank)
    far = [page for part in range(HALVES) for page in (mirrored[part], *far[part])]
    prefix_pages = assemble(page_source, page_place, [store, *near], far)
    up = up_sent.reshape(adapter_slots * rank, q_cols)
    out = attend(query_base, spread, up, new_cache, prefix_pages, starts, ends)
    return (out, new_cache)


def solution(mesh):
    return jax.shard_map(
        on_device,
        mesh=mesh,
        in_specs=(
            P("dp", "tensor"),
            P(None, "tensor"),
            P(None, "tensor"),
            P("dp", "tensor", None),
            P("dp", None, "tensor"),
            P("dp", None, "tensor"),
            P("dp", None),
            P("dp", None),
            P("dp"),
            P("dp", None),
            P("dp"),
        ),
        out_specs=(P("dp", "tensor"), P("dp", "tensor")),
        check_vma=False,
    )
```

```python
import math

import jax
import jax.numpy as jnp
from jax import lax
from jax.experimental import pallas as pl
from jax.experimental.pallas import tpu as pltpu
from jax.sharding import PartitionSpec as P

HEAD_WIDTH = 128
ADP_CAP = 2
PAGE = 64
HITS = 4
MOST = 128
BLOCK = 32
TOGETHER = 4
TILE = 256
PARTS = ((0, 48), (48, 64))
VMEM_GRANT = 60 * 1024 * 1024

ADAPTER_SCALE = 0.5
NEGATIVE = -1e30


def earlier_alike(owner):
    count = owner.shape[-1]
    ahead = jnp.arange(count, dtype=jnp.int32)[None, :] < jnp.arange(count, dtype=jnp.int32)[:, None]
    alike = owner[..., None, :] == owner[..., :, None]
    return jnp.sum((alike & ahead).astype(jnp.int32), axis=-1)


def asked_of(holder, owner, order, local, capacity):
    place = jnp.arange(capacity, dtype=jnp.int32)[None, :, None]
    match = (owner[:, None, :] == holder) & (order[:, None, :] == place)
    return jnp.sum(jnp.where(match, local[:, None, :], 0), axis=2)


def attention_steps(starts, ends, total):
    first = starts // BLOCK
    count = (ends - 1) // BLOCK - first + 1
    upto = jnp.cumsum(count)
    step = jnp.minimum(jnp.arange(total, dtype=jnp.int32), upto[-1] - 1)
    request = jnp.sum((upto[None, :] <= step[:, None]).astype(jnp.int32), axis=1)
    pick = request[:, None] == jnp.arange(starts.shape[0], dtype=jnp.int32)[None, :]

    def at(values):
        return jnp.sum(jnp.where(pick, values[None, :], 0), axis=1)

    block = at(first) + step - at(upto - count)
    return jnp.stack([request, block, at(starts), at(ends)])


def attention_kernel(steps_ref, spread_hbm, up_hbm, base_hbm, cache_hbm, pages_hbm, out_ref, query_ref, *rest):
    spread_ref, up_ref, base_ref, cache_ref, pages_ref, sems, tile_sems = rest

    def tile_copies(index):
        cols = pl.ds(pl.multiple_of(index * TILE, TILE), TILE)
        return (
            pltpu.make_async_copy(up_hbm.at[:, cols], up_ref.at[:, cols], tile_sems.at[0, index]),
            pltpu.make_async_copy(base_hbm.at[:, cols], base_ref.at[:, cols], tile_sems.at[1, index]),
        )

    pairs = [(spread_hbm, spread_ref), (cache_hbm, cache_ref), (pages_hbm, pages_ref)]
    copies = [pltpu.make_async_copy(*pair, sems.at[index]) for index, pair in enumerate(pairs)]
    copies[0].start()
    for index in range(base_ref.shape[1] // TILE):
        for copy in tile_copies(index):
            copy.start()
    for copy in copies[1:]:
        copy.start()
    rows_total, q_cols = base_ref.shape
    kv_heads = cache_ref.shape[1] // (2 * HEAD_WIDTH)
    group = q_cols // HEAD_WIDTH // kv_heads
    window = min(rows_total, MOST + BLOCK)
    sharp = HEAD_WIDTH ** -0.5 * math.log2(math.e)
    copies[0].wait()

    def project(index, carry):
        for copy in tile_copies(index):
            copy.wait()
        cols = pl.ds(pl.multiple_of(index * TILE, TILE), TILE)
        correction = jnp.dot(spread_ref[...], up_ref[:, cols], preferred_element_type=jnp.float32)
        query_ref[:, cols] = (base_ref[:, cols] + ADAPTER_SCALE * correction).astype(jnp.bfloat16)
        return carry

    lax.fori_loop(0, q_cols // TILE, project, 0)
    for copy in copies[1:]:
        copy.wait()
    dims = (((1,), (1,)), ((), ()))

    def several(turn, carry):
        places = []
        for lane in range(TOGETHER):
            index = turn * TOGETHER + lane
            row = pl.multiple_of(steps_ref[1, index] * BLOCK, BLOCK)
            start = steps_ref[2, index]
            base = pl.multiple_of(jnp.minimum(start // BLOCK * BLOCK, rows_total - window), BLOCK)
            old = pl.ds(steps_ref[0, index] * HITS, HITS)
            places.append((row, pl.ds(base, window), old, base, start, steps_ref[3, index]))
        chains = [(place, head) for place in places for head in range(kv_heads)]
        scores = []
        for (row, new, old, base, start, _), head in chains:
            at = head * 2 * HEAD_WIDTH
            wide = head * group * HEAD_WIDTH
            q_at = row + lax.broadcasted_iota(jnp.int32, (group * BLOCK, window), 0) % BLOCK
            k_at = base + lax.broadcasted_iota(jnp.int32, (group * BLOCK, window), 1)
            visible = (k_at >= start) & (k_at <= q_at)
            rows_q = jnp.concatenate(
                [
                    query_ref[pl.ds(row, BLOCK), wide + g * HEAD_WIDTH : wide + (g + 1) * HEAD_WIDTH]
                    for g in range(group)
                ],
                axis=0,
            )
            old_k = pages_ref[old, :, at : at + HEAD_WIDTH].reshape(HITS * PAGE, HEAD_WIDTH)
            new_k = cache_ref[new, at : at + HEAD_WIDTH]
            old_s = lax.dot_general(rows_q, old_k, dims, preferred_element_type=jnp.float32)
            new_s = lax.dot_general(rows_q, new_k, dims, preferred_element_type=jnp.float32)
            scores.append((old_s, jnp.where(visible, new_s, NEGATIVE)))
        weights = []
        for old_s, new_s in scores:
            top = jnp.maximum(
                jnp.max(old_s, axis=1, keepdims=True), jnp.max(new_s, axis=1, keepdims=True)
            )
            old_e = jnp.exp2((old_s - top) * sharp)
            new_e = jnp.exp2((new_s - top) * sharp)
            total = jnp.sum(old_e, axis=1, keepdims=True) + jnp.sum(new_e, axis=1, keepdims=True)
            weights.append((old_e.astype(jnp.bfloat16), new_e.astype(jnp.bfloat16), total))
        results = []
        for ((_, new, old, _, _, _), head), (old_e, new_e, total) in zip(chains, weights):
            at = head * 2 * HEAD_WIDTH + HEAD_WIDTH
            old_v = pages_ref[old, :, at : at + HEAD_WIDTH].reshape(HITS * PAGE, HEAD_WIDTH)
            new_v = cache_ref[new, at : at + HEAD_WIDTH]
            summed = jnp.dot(old_e, old_v, preferred_element_type=jnp.float32)
            summed += jnp.dot(new_e, new_v, preferred_element_type=jnp.float32)
            results.append((summed / total).astype(jnp.bfloat16))
        for ((row, _, _, _, start, end), head), result in zip(chains, results):
            own_at = row + lax.broadcasted_iota(jnp.int32, (BLOCK, HEAD_WIDTH), 0)
            own = (own_at >= start) & (own_at < end)
            for g in range(group):
                col = (head * group + g) * HEAD_WIDTH
                cols = slice(col, col + HEAD_WIDTH)
                before = out_ref[pl.ds(row, BLOCK), cols]
                out_ref[pl.ds(row, BLOCK), cols] = jnp.where(own, result[g * BLOCK : (g + 1) * BLOCK], before)
        return carry

    lax.fori_loop(0, steps_ref.shape[1] // TOGETHER, several, 0)


def attend(query_base, spread, up, cache, pages, starts, ends):
    rows, q_cols = query_base.shape
    steps_total = -(-(rows // BLOCK + starts.shape[0] - 1) // TOGETHER) * TOGETHER
    steps = attention_steps(starts, ends, steps_total)
    return pl.pallas_call(
        attention_kernel,
        out_shape=jax.ShapeDtypeStruct((rows, q_cols), jnp.bfloat16),
        in_specs=[pl.BlockSpec(memory_space=pltpu.SMEM)] + [pl.BlockSpec(memory_space=pltpu.HBM)] * 5,
        out_specs=pl.BlockSpec(memory_space=pltpu.VMEM),
        scratch_shapes=[
            pltpu.VMEM((rows, q_cols), jnp.bfloat16),
            *[pltpu.VMEM(each.shape, each.dtype) for each in (spread, up, query_base, cache, pages)],
            pltpu.SemaphoreType.DMA((3,)),
            pltpu.SemaphoreType.DMA((2, q_cols // TILE)),
        ],
        compiler_params=pltpu.CompilerParams(vmem_limit_bytes=VMEM_GRANT),
        cost_estimate=pl.CostEstimate(
            flops=4 * steps_total * BLOCK * q_cols * (HITS * PAGE + MOST + BLOCK) + 2 * spread.size * q_cols,
            bytes_accessed=4 * query_base.size + 2 * (2 * spread.size + up.size + cache.size + pages.size),
            transcendentals=0,
        ),
        name="attend",
    )(steps, spread, up, query_base, cache, pages)


def serve_kernel(asked_ref, store_ref, *refs):
    outs, sems = refs[:-1], refs[-1]
    for index, out in enumerate(outs):
        for place in range(out.shape[0]):
            page = asked_ref[index * out.shape[0] + place]
            pltpu.make_async_copy(store_ref.at[page], out.at[place], sems.at[index]).start()
    for index, out in enumerate(outs):
        pltpu.make_async_copy(out, out, sems.at[index]).wait()


def serve(asked, store):
    blocks, capacity = asked.shape
    shape = (capacity,) + store.shape[1:]
    return pl.pallas_call(
        serve_kernel,
        out_shape=[jax.ShapeDtypeStruct(shape, store.dtype)] * blocks,
        in_specs=[pl.BlockSpec(memory_space=pltpu.SMEM), pl.BlockSpec(memory_space=pltpu.HBM)],
        out_specs=[pl.BlockSpec(memory_space=pltpu.VMEM)] * blocks,
        scratch_shapes=[pltpu.SemaphoreType.DMA((blocks,))],
        compiler_params=pltpu.CompilerParams(vmem_limit_bytes=VMEM_GRANT),
        cost_estimate=pl.CostEstimate(
            flops=0, bytes_accessed=4 * blocks * math.prod(shape), transcendentals=0
        ),
        name="serve",
    )(asked.reshape(-1), store)


def assemble_kernel(source_ref, place_ref, *refs):
    out, sem = refs[-2:]
    half = (len(refs) - 2) // (1 + len(PARTS))
    near, far = refs[:half], refs[half:-2]

    def one(index, carry):
        source = source_ref[index]
        place = place_ref[index]
        for number in range(half):

            @pl.when(source == number)
            def _():
                pltpu.make_async_copy(near[number].at[place], out.at[index], sem).start()

            @pl.when(source == half + number)
            def _():
                for part, (first, end) in enumerate(PARTS):
                    rows = out.at[index, first:end]
                    pltpu.make_async_copy(far[part * half + number].at[place], rows, sem).start()

        return carry

    lax.fori_loop(0, out.shape[0], one, 0)
    pltpu.make_async_copy(out, out, sem).wait()


def assemble(source, place, near, far):
    scalars = pl.BlockSpec(memory_space=pltpu.SMEM)
    sources = [*near, *far]
    shape = (source.shape[0],) + near[0].shape[1:]
    return pl.pallas_call(
        assemble_kernel,
        out_shape=jax.ShapeDtypeStruct(shape, near[0].dtype),
        in_specs=[scalars, scalars] + [pl.BlockSpec(memory_space=pltpu.HBM)] * len(sources),
        out_specs=pl.BlockSpec(memory_space=pltpu.VMEM),
        scratch_shapes=[pltpu.SemaphoreType.DMA],
        compiler_params=pltpu.CompilerParams(vmem_limit_bytes=VMEM_GRANT),
        cost_estimate=pl.CostEstimate(flops=0, bytes_accessed=4 * math.prod(shape), transcendentals=0),
        name="assemble",
    )(source, place, *sources)


def on_device(
    tokens,
    query_weight,
    keyvalue_weight,
    adapter_down_weight,
    adapter_up_weight,
    keyvalue_page_store,
    span_token_length,
    adapter_owner,
    adapter_local_index,
    page_owner,
    page_local_index,
):
    peers = lax.axis_size("dp")
    half = peers // 2
    me = lax.axis_index("dp")
    tok_rows = tokens.shape[0]
    q_cols = query_weight.shape[1]
    rank = adapter_down_weight.shape[2]
    adapter_slots = peers * ADP_CAP

    def swap(array, distance):
        return lax.ppermute(array, "dp", [(peer, peer ^ distance) for peer in range(peers)])

    page_count = page_local_index.shape[0]
    request_count = adapter_local_index.shape[0]
    raw = jnp.concatenate([page_owner[:, 0], page_local_index, adapter_owner[:, 0], adapter_local_index])
    everyone = lax.all_to_all(
        jnp.broadcast_to(raw[None], (peers, raw.shape[0])), "dp", split_axis=0, concat_axis=0, tiled=True
    )
    parts = [keyvalue_page_store[:, first:end] for first, end in PARTS]
    store, down_store, everyone, *parts = lax.optimization_barrier(
        (keyvalue_page_store, adapter_down_weight, everyone, *parts)
    )

    page_cap = max(2, 2 * page_count // peers)
    group = everyone[jnp.arange(half, dtype=jnp.int32) ^ me]
    group_owner = group[:, :page_count]
    group_local = group[:, page_count : 2 * page_count]
    group_order = earlier_alike(group_owner)
    near_asked = asked_of(me, group_owner, group_order, group_local, page_cap)
    far_asked = asked_of(me ^ half, group_owner, group_order, group_local, page_cap)
    all_owner = everyone[:, 2 * page_count : 2 * page_count + request_count]
    all_local = everyone[:, 2 * page_count + request_count :]
    adapter_asked = asked_of(me, all_owner, earlier_alike(all_owner), all_local, ADP_CAP).reshape(-1)
    adapter_pos = adapter_owner[:, 0] * ADP_CAP + earlier_alike(adapter_owner[:, 0])
    page_source = page_owner[:, 0] ^ me
    page_place = jnp.where(page_source % half == 0, page_local_index, earlier_alike(page_owner[:, 0]))

    near = serve(near_asked[1:], store)
    near = [swap(pages, i + 1) for i, pages in enumerate(near)]
    down_rows = down_store[adapter_asked]
    up_rows = adapter_up_weight[adapter_asked]

    piece = lax.all_gather(tokens, "tensor", axis=1, tiled=True)
    query_base = jnp.dot(piece, query_weight, preferred_element_type=jnp.float32)
    new_cache = jnp.dot(piece, keyvalue_weight, preferred_element_type=jnp.float32).astype(jnp.bfloat16)

    mirrored = [swap(parts[0], half)]
    mirrored[0], parts[1], down_rows, near[:2], query_base, new_cache = lax.optimization_barrier(
        (mirrored[0], parts[1], down_rows, near[:2], query_base, new_cache)
    )
    mirrored.append(swap(parts[1], half))
    down_sent = lax.all_to_all(down_rows, "dp", split_axis=0, concat_axis=0, tiled=True)
    far = [serve(far_asked[1:], pool) for pool in mirrored]
    far[0] = [swap(pages, i + 1) for i, pages in enumerate(far[0])]
    up_rows, down_sent, far, near = lax.optimization_barrier((up_rows, down_sent, far, near))
    up_sent = lax.all_to_all(up_rows, "dp", split_axis=0, concat_axis=0, tiled=True)
    far[1] = [swap(pages, i + 1) for i, pages in enumerate(far[1])]

    lengths = span_token_length[0]
    ends = jnp.cumsum(lengths)
    starts = ends - lengths
    steps = jnp.arange(tok_rows, dtype=jnp.int32)[:, None]
    member = (steps >= starts[None, :]) & (steps < ends[None, :])
    slot = jnp.sum(jnp.where(member, adapter_pos[None, :], 0), axis=1)
    in_slot = slot[:, None] == jnp.arange(adapter_slots, dtype=jnp.int32)[None, :]

    down_part = jnp.einsum("tn,snk->tsk", tokens, down_sent, preferred_element_type=jnp.float32)
    shrink_part = jnp.sum(jnp.where(in_slot[:, :, None], down_part, 0.0), axis=1)
    shrink = lax.psum(shrink_part, "tensor").astype(jnp.bfloat16)
    spread = jnp.where(in_slot[:, :, None], shrink[:, None, :], 0).reshape(tok_rows, adapter_slots * rank)
    far = [page for part in range(len(PARTS)) for page in (mirrored[part], *far[part])]
    prefix_pages = assemble(page_source, page_place, [store, *near], far)
    up = up_sent.reshape(adapter_slots * rank, q_cols)
    out = attend(query_base, spread, up, new_cache, prefix_pages, starts, ends)
    return (out, new_cache)


def solution(mesh):
    return jax.shard_map(
        on_device,
        mesh=mesh,
        in_specs=(
            P("dp", "tensor"),
            P(None, "tensor"),
            P(None, "tensor"),
            P("dp", "tensor", None),
            P("dp", None, "tensor"),
            P("dp", None, "tensor"),
            P("dp", None),
            P("dp", None),
            P("dp"),
            P("dp", None),
            P("dp"),
        ),
        out_specs=(P("dp", "tensor"), P("dp", "tensor")),
        check_vma=False,
    )
```

```python
import math

import jax
import jax.numpy as jnp
from jax import lax
from jax.experimental import pallas as pl
from jax.experimental.pallas import tpu as pltpu
from jax.sharding import PartitionSpec as P

HEAD_WIDTH = 128
ADP_CAP = 2
PAGE = 64
HITS = 4
MOST = 128
BLOCK = 32
TOGETHER = 4
TILE = 256
PARTS = ((0, 48), (48, 64))
VMEM_GRANT = 60 * 1024 * 1024

ADAPTER_SCALE = 0.5
NEGATIVE = -1e30


def earlier_alike(owner):
    count = owner.shape[-1]
    ahead = jnp.arange(count, dtype=jnp.int32)[None, :] < jnp.arange(count, dtype=jnp.int32)[:, None]
    alike = owner[..., None, :] == owner[..., :, None]
    return jnp.sum((alike & ahead).astype(jnp.int32), axis=-1)


def asked_of(holder, owner, order, local, capacity):
    place = jnp.arange(capacity, dtype=jnp.int32)[None, :, None]
    match = (owner[:, None, :] == holder) & (order[:, None, :] == place)
    return jnp.sum(jnp.where(match, local[:, None, :], 0), axis=2)


def attention_steps(starts, ends, total):
    first = starts // BLOCK
    count = (ends - 1) // BLOCK - first + 1
    upto = jnp.cumsum(count)
    step = jnp.minimum(jnp.arange(total, dtype=jnp.int32), upto[-1] - 1)
    request = jnp.sum((upto[None, :] <= step[:, None]).astype(jnp.int32), axis=1)
    pick = request[:, None] == jnp.arange(starts.shape[0], dtype=jnp.int32)[None, :]

    def at(values):
        return jnp.sum(jnp.where(pick, values[None, :], 0), axis=1)

    block = at(first) + step - at(upto - count)
    return jnp.stack([request, block, at(starts), at(ends)])


def attention_kernel(steps_ref, spread_hbm, up_hbm, base_hbm, cache_hbm, pages_hbm, out_ref, query_ref, *rest):
    spread_ref, up_ref, base_ref, cache_ref, pages_ref, sems, tile_sems = rest

    def tile_copies(index):
        cols = pl.ds(pl.multiple_of(index * TILE, TILE), TILE)
        return (
            pltpu.make_async_copy(up_hbm.at[:, cols], up_ref.at[:, cols], tile_sems.at[0, index]),
            pltpu.make_async_copy(base_hbm.at[:, cols], base_ref.at[:, cols], tile_sems.at[1, index]),
        )

    pairs = [(spread_hbm, spread_ref), (cache_hbm, cache_ref), (pages_hbm, pages_ref)]
    copies = [pltpu.make_async_copy(*pair, sems.at[index]) for index, pair in enumerate(pairs)]
    copies[0].start()
    for index in range(base_ref.shape[1] // TILE):
        for copy in tile_copies(index):
            copy.start()
    for copy in copies[1:]:
        copy.start()
    rows_total, q_cols = base_ref.shape
    kv_heads = cache_ref.shape[1] // (2 * HEAD_WIDTH)
    group = q_cols // HEAD_WIDTH // kv_heads
    window = min(rows_total, MOST + BLOCK)
    sharp = HEAD_WIDTH ** -0.5 * math.log2(math.e)
    copies[0].wait()

    def project(index, carry):
        for copy in tile_copies(index):
            copy.wait()
        cols = pl.ds(pl.multiple_of(index * TILE, TILE), TILE)
        correction = jnp.dot(spread_ref[...], up_ref[:, cols], preferred_element_type=jnp.float32)
        query_ref[:, cols] = (base_ref[:, cols] + ADAPTER_SCALE * correction).astype(jnp.bfloat16)
        return carry

    lax.fori_loop(0, q_cols // TILE, project, 0)
    for copy in copies[1:]:
        copy.wait()
    dims = (((1,), (1,)), ((), ()))

    def several(turn, carry):
        places = []
        for lane in range(TOGETHER):
            index = turn * TOGETHER + lane
            row = pl.multiple_of(steps_ref[1, index] * BLOCK, BLOCK)
            start = steps_ref[2, index]
            base = pl.multiple_of(jnp.minimum(start // BLOCK * BLOCK, rows_total - window), BLOCK)
            old = pl.ds(steps_ref[0, index] * HITS, HITS)
            places.append((row, pl.ds(base, window), old, base, start, steps_ref[3, index]))
        chains = [(place, head) for place in places for head in range(kv_heads)]
        scores = []
        for (row, new, old, base, start, _), head in chains:
            at = head * 2 * HEAD_WIDTH
            wide = head * group * HEAD_WIDTH
            q_at = row + lax.broadcasted_iota(jnp.int32, (group * BLOCK, window), 0) % BLOCK
            k_at = base + lax.broadcasted_iota(jnp.int32, (group * BLOCK, window), 1)
            visible = (k_at >= start) & (k_at <= q_at)
            rows_q = jnp.concatenate(
                [
                    query_ref[pl.ds(row, BLOCK), wide + g * HEAD_WIDTH : wide + (g + 1) * HEAD_WIDTH]
                    for g in range(group)
                ],
                axis=0,
            )
            old_k = pages_ref[old, :, at : at + HEAD_WIDTH].reshape(HITS * PAGE, HEAD_WIDTH)
            new_k = cache_ref[new, at : at + HEAD_WIDTH]
            old_s = lax.dot_general(rows_q, old_k, dims, preferred_element_type=jnp.float32)
            new_s = lax.dot_general(rows_q, new_k, dims, preferred_element_type=jnp.float32)
            scores.append((old_s, jnp.where(visible, new_s, NEGATIVE)))
        weights = []
        for old_s, new_s in scores:
            top = jnp.maximum(
                jnp.max(old_s, axis=1, keepdims=True), jnp.max(new_s, axis=1, keepdims=True)
            )
            old_e = jnp.exp2((old_s - top) * sharp)
            new_e = jnp.exp2((new_s - top) * sharp)
            total = jnp.sum(old_e, axis=1, keepdims=True) + jnp.sum(new_e, axis=1, keepdims=True)
            weights.append((old_e.astype(jnp.bfloat16), new_e.astype(jnp.bfloat16), total))
        results = []
        for ((_, new, old, _, _, _), head), (old_e, new_e, total) in zip(chains, weights):
            at = head * 2 * HEAD_WIDTH + HEAD_WIDTH
            old_v = pages_ref[old, :, at : at + HEAD_WIDTH].reshape(HITS * PAGE, HEAD_WIDTH)
            new_v = cache_ref[new, at : at + HEAD_WIDTH]
            summed = jnp.dot(old_e, old_v, preferred_element_type=jnp.float32)
            summed += jnp.dot(new_e, new_v, preferred_element_type=jnp.float32)
            results.append((summed / total).astype(jnp.bfloat16))
        for ((row, _, _, _, start, end), head), result in zip(chains, results):
            own_at = row + lax.broadcasted_iota(jnp.int32, (BLOCK, HEAD_WIDTH), 0)
            own = (own_at >= start) & (own_at < end)
            for g in range(group):
                col = (head * group + g) * HEAD_WIDTH
                cols = slice(col, col + HEAD_WIDTH)
                before = out_ref[pl.ds(row, BLOCK), cols]
                out_ref[pl.ds(row, BLOCK), cols] = jnp.where(own, result[g * BLOCK : (g + 1) * BLOCK], before)
        return carry

    lax.fori_loop(0, steps_ref.shape[1] // TOGETHER, several, 0)


def attend(query_base, spread, up, cache, pages, starts, ends):
    rows, q_cols = query_base.shape
    steps_total = -(-(rows // BLOCK + starts.shape[0] - 1) // TOGETHER) * TOGETHER
    steps = attention_steps(starts, ends, steps_total)
    return pl.pallas_call(
        attention_kernel,
        out_shape=jax.ShapeDtypeStruct((rows, q_cols), jnp.bfloat16),
        in_specs=[pl.BlockSpec(memory_space=pltpu.SMEM)] + [pl.BlockSpec(memory_space=pltpu.HBM)] * 5,
        out_specs=pl.BlockSpec(memory_space=pltpu.VMEM),
        scratch_shapes=[
            pltpu.VMEM((rows, q_cols), jnp.bfloat16),
            *[pltpu.VMEM(each.shape, each.dtype) for each in (spread, up, query_base, cache, pages)],
            pltpu.SemaphoreType.DMA((3,)),
            pltpu.SemaphoreType.DMA((2, q_cols // TILE)),
        ],
        compiler_params=pltpu.CompilerParams(vmem_limit_bytes=VMEM_GRANT),
        cost_estimate=pl.CostEstimate(
            flops=4 * steps_total * BLOCK * q_cols * (HITS * PAGE + MOST + BLOCK) + 2 * spread.size * q_cols,
            bytes_accessed=4 * query_base.size + 2 * (2 * spread.size + up.size + cache.size + pages.size),
            transcendentals=0,
        ),
        name="attend",
    )(steps, spread, up, query_base, cache, pages)


def serve_kernel(asked_ref, store_ref, *refs):
    outs, sems = refs[:-1], refs[-1]
    for index, out in enumerate(outs):
        for place in range(out.shape[0]):
            page = asked_ref[index * out.shape[0] + place]
            pltpu.make_async_copy(store_ref.at[page], out.at[place], sems.at[index]).start()
    for index, out in enumerate(outs):
        pltpu.make_async_copy(out, out, sems.at[index]).wait()


def serve(asked, store):
    blocks, capacity = asked.shape
    shape = (capacity,) + store.shape[1:]
    return pl.pallas_call(
        serve_kernel,
        out_shape=[jax.ShapeDtypeStruct(shape, store.dtype)] * blocks,
        in_specs=[pl.BlockSpec(memory_space=pltpu.SMEM), pl.BlockSpec(memory_space=pltpu.HBM)],
        out_specs=[pl.BlockSpec(memory_space=pltpu.VMEM)] * blocks,
        scratch_shapes=[pltpu.SemaphoreType.DMA((blocks,))],
        compiler_params=pltpu.CompilerParams(vmem_limit_bytes=VMEM_GRANT),
        cost_estimate=pl.CostEstimate(
            flops=0, bytes_accessed=4 * blocks * math.prod(shape), transcendentals=0
        ),
        name="serve",
    )(asked.reshape(-1), store)


def assemble_kernel(source_ref, place_ref, *refs):
    out, sem = refs[-2:]
    half = (len(refs) - 2) // (1 + len(PARTS))
    near, far = refs[:half], refs[half:-2]

    def one(index, carry):
        source = source_ref[index]
        place = place_ref[index]
        for number in range(half):

            @pl.when(source == number)
            def _():
                pltpu.make_async_copy(near[number].at[place], out.at[index], sem).start()

            @pl.when(source == half + number)
            def _():
                for part, (first, end) in enumerate(PARTS):
                    rows = out.at[index, first:end]
                    pltpu.make_async_copy(far[part * half + number].at[place], rows, sem).start()

        return carry

    lax.fori_loop(0, out.shape[0], one, 0)
    pltpu.make_async_copy(out, out, sem).wait()


def assemble(source, place, near, far):
    scalars = pl.BlockSpec(memory_space=pltpu.SMEM)
    sources = [*near, *far]
    shape = (source.shape[0],) + near[0].shape[1:]
    return pl.pallas_call(
        assemble_kernel,
        out_shape=jax.ShapeDtypeStruct(shape, near[0].dtype),
        in_specs=[scalars, scalars] + [pl.BlockSpec(memory_space=pltpu.HBM)] * len(sources),
        out_specs=pl.BlockSpec(memory_space=pltpu.VMEM),
        scratch_shapes=[pltpu.SemaphoreType.DMA],
        compiler_params=pltpu.CompilerParams(vmem_limit_bytes=VMEM_GRANT),
        cost_estimate=pl.CostEstimate(flops=0, bytes_accessed=4 * math.prod(shape), transcendentals=0),
        name="assemble",
    )(source, place, *sources)


def on_device(
    tokens,
    query_weight,
    keyvalue_weight,
    adapter_down_weight,
    adapter_up_weight,
    keyvalue_page_store,
    span_token_length,
    adapter_owner,
    adapter_local_index,
    page_owner,
    page_local_index,
):
    peers = lax.axis_size("dp")
    half = peers // 2
    me = lax.axis_index("dp")
    tok_rows = tokens.shape[0]
    q_cols = query_weight.shape[1]
    rank = adapter_down_weight.shape[2]
    adapter_slots = peers * ADP_CAP

    def swap(array, distance):
        return lax.ppermute(array, "dp", [(peer, peer ^ distance) for peer in range(peers)])

    page_count = page_local_index.shape[0]
    request_count = adapter_local_index.shape[0]
    raw = jnp.concatenate([page_owner[:, 0], page_local_index, adapter_owner[:, 0], adapter_local_index])
    everyone = lax.all_to_all(
        jnp.broadcast_to(raw[None], (peers, raw.shape[0])), "dp", split_axis=0, concat_axis=0, tiled=True
    )
    parts = [keyvalue_page_store[:, first:end] for first, end in PARTS]
    store, down_store, everyone, *parts = lax.optimization_barrier(
        (keyvalue_page_store, adapter_down_weight, everyone, *parts)
    )

    page_cap = max(2, 2 * page_count // peers)
    group = everyone[jnp.arange(half, dtype=jnp.int32) ^ me]
    group_owner = group[:, :page_count]
    group_local = group[:, page_count : 2 * page_count]
    group_order = earlier_alike(group_owner)
    near_asked = asked_of(me, group_owner, group_order, group_local, page_cap)
    far_asked = asked_of(me ^ half, group_owner, group_order, group_local, page_cap)
    all_owner = everyone[:, 2 * page_count : 2 * page_count + request_count]
    all_local = everyone[:, 2 * page_count + request_count :]
    adapter_asked = asked_of(me, all_owner, earlier_alike(all_owner), all_local, ADP_CAP).reshape(-1)
    adapter_pos = adapter_owner[:, 0] * ADP_CAP + earlier_alike(adapter_owner[:, 0])
    page_source = page_owner[:, 0] ^ me
    page_place = jnp.where(page_source % half == 0, page_local_index, earlier_alike(page_owner[:, 0]))

    near = serve(near_asked[1:], store)
    near = [swap(pages, i + 1) for i, pages in enumerate(near)]
    down_rows = down_store[adapter_asked]
    up_rows = adapter_up_weight[adapter_asked]

    piece = lax.all_gather(tokens, "tensor", axis=1, tiled=True)
    query_base = jnp.dot(piece, query_weight, preferred_element_type=jnp.float32)
    new_cache = jnp.dot(piece, keyvalue_weight, preferred_element_type=jnp.float32).astype(jnp.bfloat16)

    mirrored = [swap(parts[0], half)]
    mirrored[0], parts[1], near, query_base, new_cache = lax.optimization_barrier(
        (mirrored[0], parts[1], near, query_base, new_cache)
    )
    mirrored.append(swap(parts[1], half))
    far = [serve(far_asked[1:], pool) for pool in mirrored]
    down_rows, far[0] = lax.optimization_barrier((down_rows, far[0]))
    down_sent = lax.all_to_all(down_rows, "dp", split_axis=0, concat_axis=0, tiled=True)
    far = [[swap(pages, i + 1) for i, pages in enumerate(block)] for block in far]
    up_rows, down_sent, far = lax.optimization_barrier((up_rows, down_sent, far))
    up_sent = lax.all_to_all(up_rows, "dp", split_axis=0, concat_axis=0, tiled=True)

    lengths = span_token_length[0]
    ends = jnp.cumsum(lengths)
    starts = ends - lengths
    steps = jnp.arange(tok_rows, dtype=jnp.int32)[:, None]
    member = (steps >= starts[None, :]) & (steps < ends[None, :])
    slot = jnp.sum(jnp.where(member, adapter_pos[None, :], 0), axis=1)
    in_slot = slot[:, None] == jnp.arange(adapter_slots, dtype=jnp.int32)[None, :]

    down_part = jnp.einsum("tn,snk->tsk", tokens, down_sent, preferred_element_type=jnp.float32)
    shrink_part = jnp.sum(jnp.where(in_slot[:, :, None], down_part, 0.0), axis=1)
    shrink = lax.psum(shrink_part, "tensor").astype(jnp.bfloat16)
    spread = jnp.where(in_slot[:, :, None], shrink[:, None, :], 0).reshape(tok_rows, adapter_slots * rank)
    far = [page for part in range(len(PARTS)) for page in (mirrored[part], *far[part])]
    prefix_pages = assemble(page_source, page_place, [store, *near], far)
    up = up_sent.reshape(adapter_slots * rank, q_cols)
    out = attend(query_base, spread, up, new_cache, prefix_pages, starts, ends)
    return (out, new_cache)


def solution(mesh):
    return jax.shard_map(
        on_device,
        mesh=mesh,
        in_specs=(
            P("dp", "tensor"),
            P(None, "tensor"),
            P(None, "tensor"),
            P("dp", "tensor", None),
            P("dp", None, "tensor"),
            P("dp", None, "tensor"),
            P("dp", None),
            P("dp", None),
            P("dp"),
            P("dp", None),
            P("dp"),
        ),
        out_specs=(P("dp", "tensor"), P("dp", "tensor")),
        check_vma=False,
    )
```

```python
import math

import jax
import jax.numpy as jnp
from jax import lax
from jax.experimental import pallas as pl
from jax.experimental.pallas import tpu as pltpu
from jax.sharding import PartitionSpec as P

HEAD_WIDTH = 128
ADP_CAP = 2
PAGE = 64
HITS = 4
MOST = 128
BLOCK = 32
TOGETHER = 4
TILE = 256
VMEM_GRANT = 60 * 1024 * 1024

ADAPTER_SCALE = 0.5
NEGATIVE = -1e30


def earlier_alike(owner):
    count = owner.shape[-1]
    ahead = jnp.arange(count, dtype=jnp.int32)[None, :] < jnp.arange(count, dtype=jnp.int32)[:, None]
    alike = owner[..., None, :] == owner[..., :, None]
    return jnp.sum((alike & ahead).astype(jnp.int32), axis=-1)


def asked_of(holder, owner, order, local, capacity):
    place = jnp.arange(capacity, dtype=jnp.int32)[None, :, None]
    match = (owner[:, None, :] == holder) & (order[:, None, :] == place)
    return jnp.sum(jnp.where(match, local[:, None, :], 0), axis=2)


def attention_steps(starts, ends, total):
    first = starts // BLOCK
    count = (ends - 1) // BLOCK - first + 1
    upto = jnp.cumsum(count)
    step = jnp.minimum(jnp.arange(total, dtype=jnp.int32), upto[-1] - 1)
    request = jnp.sum((upto[None, :] <= step[:, None]).astype(jnp.int32), axis=1)
    pick = request[:, None] == jnp.arange(starts.shape[0], dtype=jnp.int32)[None, :]

    def at(values):
        return jnp.sum(jnp.where(pick, values[None, :], 0), axis=1)

    block = at(first) + step - at(upto - count)
    return jnp.stack([request, block, at(starts), at(ends)])


def attention_kernel(steps_ref, spread_hbm, up_hbm, base_hbm, cache_hbm, pages_hbm, out_ref, query_ref, *rest):
    spread_ref, up_ref, base_ref, cache_ref, pages_ref, sems, tile_sems = rest

    def tile_copies(index):
        cols = pl.ds(pl.multiple_of(index * TILE, TILE), TILE)
        return (
            pltpu.make_async_copy(up_hbm.at[:, cols], up_ref.at[:, cols], tile_sems.at[0, index]),
            pltpu.make_async_copy(base_hbm.at[:, cols], base_ref.at[:, cols], tile_sems.at[1, index]),
        )

    pairs = [(spread_hbm, spread_ref), (cache_hbm, cache_ref), (pages_hbm, pages_ref)]
    copies = [pltpu.make_async_copy(*pair, sems.at[index]) for index, pair in enumerate(pairs)]
    copies[0].start()
    for index in range(base_ref.shape[1] // TILE):
        for copy in tile_copies(index):
            copy.start()
    for copy in copies[1:]:
        copy.start()
    rows_total, q_cols = base_ref.shape
    kv_heads = cache_ref.shape[1] // (2 * HEAD_WIDTH)
    group = q_cols // HEAD_WIDTH // kv_heads
    window = min(rows_total, MOST + BLOCK)
    sharp = HEAD_WIDTH ** -0.5 * math.log2(math.e)
    copies[0].wait()

    def project(index, carry):
        for copy in tile_copies(index):
            copy.wait()
        cols = pl.ds(pl.multiple_of(index * TILE, TILE), TILE)
        correction = jnp.dot(spread_ref[...], up_ref[:, cols], preferred_element_type=jnp.float32)
        query_ref[:, cols] = (base_ref[:, cols] + ADAPTER_SCALE * correction).astype(jnp.bfloat16)
        return carry

    lax.fori_loop(0, q_cols // TILE, project, 0)
    for copy in copies[1:]:
        copy.wait()
    dims = (((1,), (1,)), ((), ()))

    def several(turn, carry):
        places = []
        for lane in range(TOGETHER):
            index = turn * TOGETHER + lane
            row = pl.multiple_of(steps_ref[1, index] * BLOCK, BLOCK)
            start = steps_ref[2, index]
            base = pl.multiple_of(jnp.minimum(start // BLOCK * BLOCK, rows_total - window), BLOCK)
            old = pl.ds(steps_ref[0, index] * HITS, HITS)
            places.append((row, pl.ds(base, window), old, base, start, steps_ref[3, index]))
        chains = [(place, head) for place in places for head in range(kv_heads)]
        scores = []
        for (row, new, old, base, start, _), head in chains:
            at = head * 2 * HEAD_WIDTH
            wide = head * group * HEAD_WIDTH
            q_at = row + lax.broadcasted_iota(jnp.int32, (group * BLOCK, window), 0) % BLOCK
            k_at = base + lax.broadcasted_iota(jnp.int32, (group * BLOCK, window), 1)
            visible = (k_at >= start) & (k_at <= q_at)
            rows_q = jnp.concatenate(
                [
                    query_ref[pl.ds(row, BLOCK), wide + g * HEAD_WIDTH : wide + (g + 1) * HEAD_WIDTH]
                    for g in range(group)
                ],
                axis=0,
            )
            old_k = pages_ref[old, :, at : at + HEAD_WIDTH].reshape(HITS * PAGE, HEAD_WIDTH)
            new_k = cache_ref[new, at : at + HEAD_WIDTH]
            old_s = lax.dot_general(rows_q, old_k, dims, preferred_element_type=jnp.float32)
            new_s = lax.dot_general(rows_q, new_k, dims, preferred_element_type=jnp.float32)
            scores.append((old_s, jnp.where(visible, new_s, NEGATIVE)))
        weights = []
        for old_s, new_s in scores:
            top = jnp.maximum(
                jnp.max(old_s, axis=1, keepdims=True), jnp.max(new_s, axis=1, keepdims=True)
            )
            old_e = jnp.exp2((old_s - top) * sharp)
            new_e = jnp.exp2((new_s - top) * sharp)
            total = jnp.sum(old_e, axis=1, keepdims=True) + jnp.sum(new_e, axis=1, keepdims=True)
            weights.append((old_e.astype(jnp.bfloat16), new_e.astype(jnp.bfloat16), total))
        results = []
        for ((_, new, old, _, _, _), head), (old_e, new_e, total) in zip(chains, weights):
            at = head * 2 * HEAD_WIDTH + HEAD_WIDTH
            old_v = pages_ref[old, :, at : at + HEAD_WIDTH].reshape(HITS * PAGE, HEAD_WIDTH)
            new_v = cache_ref[new, at : at + HEAD_WIDTH]
            summed = jnp.dot(old_e, old_v, preferred_element_type=jnp.float32)
            summed += jnp.dot(new_e, new_v, preferred_element_type=jnp.float32)
            results.append((summed / total).astype(jnp.bfloat16))
        for ((row, _, _, _, start, end), head), result in zip(chains, results):
            own_at = row + lax.broadcasted_iota(jnp.int32, (BLOCK, HEAD_WIDTH), 0)
            own = (own_at >= start) & (own_at < end)
            for g in range(group):
                col = (head * group + g) * HEAD_WIDTH
                cols = slice(col, col + HEAD_WIDTH)
                before = out_ref[pl.ds(row, BLOCK), cols]
                out_ref[pl.ds(row, BLOCK), cols] = jnp.where(own, result[g * BLOCK : (g + 1) * BLOCK], before)
        return carry

    lax.fori_loop(0, steps_ref.shape[1] // TOGETHER, several, 0)


def attend(query_base, spread, up, cache, pages, starts, ends):
    rows, q_cols = query_base.shape
    steps_total = -(-(rows // BLOCK + starts.shape[0] - 1) // TOGETHER) * TOGETHER
    steps = attention_steps(starts, ends, steps_total)
    return pl.pallas_call(
        attention_kernel,
        out_shape=jax.ShapeDtypeStruct((rows, q_cols), jnp.bfloat16),
        in_specs=[pl.BlockSpec(memory_space=pltpu.SMEM)] + [pl.BlockSpec(memory_space=pltpu.HBM)] * 5,
        out_specs=pl.BlockSpec(memory_space=pltpu.VMEM),
        scratch_shapes=[
            pltpu.VMEM((rows, q_cols), jnp.bfloat16),
            *[pltpu.VMEM(each.shape, each.dtype) for each in (spread, up, query_base, cache, pages)],
            pltpu.SemaphoreType.DMA((3,)),
            pltpu.SemaphoreType.DMA((2, q_cols // TILE)),
        ],
        compiler_params=pltpu.CompilerParams(vmem_limit_bytes=VMEM_GRANT),
        cost_estimate=pl.CostEstimate(
            flops=4 * steps_total * BLOCK * q_cols * (HITS * PAGE + MOST + BLOCK) + 2 * spread.size * q_cols,
            bytes_accessed=4 * query_base.size + 2 * (2 * spread.size + up.size + cache.size + pages.size),
            transcendentals=0,
        ),
        name="attend",
    )(steps, spread, up, query_base, cache, pages)


def serve_kernel(asked_ref, store_ref, *refs):
    outs, sems = refs[:-1], refs[-1]
    for index, out in enumerate(outs):
        for place in range(out.shape[0]):
            page = asked_ref[index * out.shape[0] + place]
            pltpu.make_async_copy(store_ref.at[page], out.at[place], sems.at[index]).start()
    for index, out in enumerate(outs):
        pltpu.make_async_copy(out, out, sems.at[index]).wait()


def serve(asked, store):
    blocks, capacity = asked.shape
    shape = (capacity,) + store.shape[1:]
    return pl.pallas_call(
        serve_kernel,
        out_shape=[jax.ShapeDtypeStruct(shape, store.dtype)] * blocks,
        in_specs=[pl.BlockSpec(memory_space=pltpu.SMEM), pl.BlockSpec(memory_space=pltpu.HBM)],
        out_specs=[pl.BlockSpec(memory_space=pltpu.VMEM)] * blocks,
        scratch_shapes=[pltpu.SemaphoreType.DMA((blocks,))],
        compiler_params=pltpu.CompilerParams(vmem_limit_bytes=VMEM_GRANT),
        cost_estimate=pl.CostEstimate(
            flops=0, bytes_accessed=4 * blocks * math.prod(shape), transcendentals=0
        ),
        name="serve",
    )(asked.reshape(-1), store)


def assemble_kernel(source_ref, place_ref, *refs):
    sources, out, sem = refs[:-2], refs[-2], refs[-1]

    def one(index, carry):
        source = source_ref[index]
        place = place_ref[index]
        for number, ref in enumerate(sources):

            @pl.when(source == number)
            def _():
                pltpu.make_async_copy(ref.at[place], out.at[index], sem).start()

        return carry

    lax.fori_loop(0, out.shape[0], one, 0)
    pltpu.make_async_copy(out, out, sem).wait()


def assemble(source, place, sources):
    scalars = pl.BlockSpec(memory_space=pltpu.SMEM)
    shape = (source.shape[0],) + sources[0].shape[1:]
    return pl.pallas_call(
        assemble_kernel,
        out_shape=jax.ShapeDtypeStruct(shape, sources[0].dtype),
        in_specs=[scalars, scalars] + [pl.BlockSpec(memory_space=pltpu.HBM)] * len(sources),
        out_specs=pl.BlockSpec(memory_space=pltpu.VMEM),
        scratch_shapes=[pltpu.SemaphoreType.DMA],
        compiler_params=pltpu.CompilerParams(vmem_limit_bytes=VMEM_GRANT),
        cost_estimate=pl.CostEstimate(flops=0, bytes_accessed=4 * math.prod(shape), transcendentals=0),
        name="assemble",
    )(source, place, *sources)


def on_device(
    tokens,
    query_weight,
    keyvalue_weight,
    adapter_down_weight,
    adapter_up_weight,
    keyvalue_page_store,
    span_token_length,
    adapter_owner,
    adapter_local_index,
    page_owner,
    page_local_index,
):
    peers = lax.axis_size("dp")
    half = peers // 2
    me = lax.axis_index("dp")
    tok_rows = tokens.shape[0]
    q_cols = query_weight.shape[1]
    rank = adapter_down_weight.shape[2]
    adapter_slots = peers * ADP_CAP

    def swap(array, distance):
        return lax.ppermute(array, "dp", [(peer, peer ^ distance) for peer in range(peers)])

    page_count = page_local_index.shape[0]
    request_count = adapter_local_index.shape[0]
    raw = jnp.concatenate([page_owner[:, 0], page_local_index, adapter_owner[:, 0], adapter_local_index])
    everyone = lax.all_to_all(
        jnp.broadcast_to(raw[None], (peers, raw.shape[0])), "dp", split_axis=0, concat_axis=0, tiled=True
    )
    store, down_store, everyone = lax.optimization_barrier((keyvalue_page_store, adapter_down_weight, everyone))
    mirrored_store = swap(store, half)

    page_cap = max(2, 2 * page_count // peers)
    group = everyone[jnp.arange(half, dtype=jnp.int32) ^ me]
    group_owner = group[:, :page_count]
    group_local = group[:, page_count : 2 * page_count]
    group_order = earlier_alike(group_owner)
    near_asked = asked_of(me, group_owner, group_order, group_local, page_cap)
    far_asked = asked_of(me ^ half, group_owner, group_order, group_local, page_cap)
    all_owner = everyone[:, 2 * page_count : 2 * page_count + request_count]
    all_local = everyone[:, 2 * page_count + request_count :]
    adapter_asked = asked_of(me, all_owner, earlier_alike(all_owner), all_local, ADP_CAP).reshape(-1)
    adapter_pos = adapter_owner[:, 0] * ADP_CAP + earlier_alike(adapter_owner[:, 0])
    page_source = page_owner[:, 0] ^ me
    page_place = jnp.where(page_source % half == 0, page_local_index, earlier_alike(page_owner[:, 0]))

    near = list(serve(near_asked[1:], store))
    near = [swap(pages, i + 1) for i, pages in enumerate(near)]
    down_rows = down_store[adapter_asked]
    up_rows = adapter_up_weight[adapter_asked]

    piece = lax.all_gather(tokens, "tensor", axis=1, tiled=True)
    query_base = jnp.dot(piece, query_weight, preferred_element_type=jnp.float32)
    new_cache = jnp.dot(piece, keyvalue_weight, preferred_element_type=jnp.float32).astype(jnp.bfloat16)

    down_rows, mirrored_store, query_base, new_cache, near = lax.optimization_barrier(
        (down_rows, mirrored_store, query_base, new_cache, near)
    )
    down_sent = lax.all_to_all(down_rows, "dp", split_axis=0, concat_axis=0, tiled=True)
    far = list(serve(far_asked[1:], mirrored_store))
    far = [swap(pages, i + 1) for i, pages in enumerate(far[:-1])] + far[-1:]
    up_rows, down_sent, far = lax.optimization_barrier((up_rows, down_sent, far))
    up_sent = lax.all_to_all(up_rows, "dp", split_axis=0, concat_axis=0, tiled=True)
    far[-1] = swap(far[-1], half - 1)

    lengths = span_token_length[0]
    ends = jnp.cumsum(lengths)
    starts = ends - lengths
    steps = jnp.arange(tok_rows, dtype=jnp.int32)[:, None]
    member = (steps >= starts[None, :]) & (steps < ends[None, :])
    slot = jnp.sum(jnp.where(member, adapter_pos[None, :], 0), axis=1)
    in_slot = slot[:, None] == jnp.arange(adapter_slots, dtype=jnp.int32)[None, :]

    down_part = jnp.einsum("tn,snk->tsk", tokens, down_sent, preferred_element_type=jnp.float32)
    shrink_part = jnp.sum(jnp.where(in_slot[:, :, None], down_part, 0.0), axis=1)
    shrink = lax.psum(shrink_part, "tensor").astype(jnp.bfloat16)
    spread = jnp.where(in_slot[:, :, None], shrink[:, None, :], 0).reshape(tok_rows, adapter_slots * rank)
    prefix_pages = assemble(page_source, page_place, [store, *near, mirrored_store, *far])
    up = up_sent.reshape(adapter_slots * rank, q_cols)
    out = attend(query_base, spread, up, new_cache, prefix_pages, starts, ends)
    return (out, new_cache)


def solution(mesh):
    return jax.shard_map(
        on_device,
        mesh=mesh,
        in_specs=(
            P("dp", "tensor"),
            P(None, "tensor"),
            P(None, "tensor"),
            P("dp", "tensor", None),
            P("dp", None, "tensor"),
            P("dp", None, "tensor"),
            P("dp", None),
            P("dp", None),
            P("dp"),
            P("dp", None),
            P("dp"),
        ),
        out_specs=(P("dp", "tensor"), P("dp", "tensor")),
        check_vma=False,
    )
```

```python
import math

import jax
import jax.numpy as jnp
from jax import lax
from jax.experimental import pallas as pl
from jax.experimental.pallas import tpu as pltpu
from jax.sharding import PartitionSpec as P

HEAD_WIDTH = 128
ADP_CAP = 2
PAGE = 64
HITS = 4
MOST = 128
BLOCK = 32
TOGETHER = 4
TILE = 256
VMEM_GRANT = 60 * 1024 * 1024

ADAPTER_SCALE = 0.5
NEGATIVE = -1e30


def earlier_alike(owner):
    count = owner.shape[-1]
    ahead = jnp.arange(count, dtype=jnp.int32)[None, :] < jnp.arange(count, dtype=jnp.int32)[:, None]
    alike = owner[..., None, :] == owner[..., :, None]
    return jnp.sum((alike & ahead).astype(jnp.int32), axis=-1)


def asked_of(holder, owner, order, local, capacity):
    place = jnp.arange(capacity, dtype=jnp.int32)[None, :, None]
    match = (owner[:, None, :] == holder) & (order[:, None, :] == place)
    return jnp.sum(jnp.where(match, local[:, None, :], 0), axis=2)


def attention_steps(starts, ends, total):
    first = starts // BLOCK
    count = (ends - 1) // BLOCK - first + 1
    upto = jnp.cumsum(count)
    step = jnp.minimum(jnp.arange(total, dtype=jnp.int32), upto[-1] - 1)
    request = jnp.sum((upto[None, :] <= step[:, None]).astype(jnp.int32), axis=1)
    pick = request[:, None] == jnp.arange(starts.shape[0], dtype=jnp.int32)[None, :]

    def at(values):
        return jnp.sum(jnp.where(pick, values[None, :], 0), axis=1)

    block = at(first) + step - at(upto - count)
    return jnp.stack([request, block, at(starts), at(ends)])


def attention_kernel(steps_ref, spread_hbm, up_hbm, base_hbm, cache_hbm, pages_hbm, out_ref, query_ref, *rest):
    spread_ref, up_ref, base_ref, cache_ref, pages_ref, sems, tile_sems = rest

    def tile_copies(index):
        cols = pl.ds(pl.multiple_of(index * TILE, TILE), TILE)
        return (
            pltpu.make_async_copy(up_hbm.at[:, cols], up_ref.at[:, cols], tile_sems.at[0, index]),
            pltpu.make_async_copy(base_hbm.at[:, cols], base_ref.at[:, cols], tile_sems.at[1, index]),
        )

    pairs = [(spread_hbm, spread_ref), (cache_hbm, cache_ref), (pages_hbm, pages_ref)]
    copies = [pltpu.make_async_copy(*pair, sems.at[index]) for index, pair in enumerate(pairs)]
    copies[0].start()
    for index in range(base_ref.shape[1] // TILE):
        for copy in tile_copies(index):
            copy.start()
    for copy in copies[1:]:
        copy.start()
    rows_total, q_cols = base_ref.shape
    kv_heads = cache_ref.shape[1] // (2 * HEAD_WIDTH)
    group = q_cols // HEAD_WIDTH // kv_heads
    window = min(rows_total, MOST + BLOCK)
    sharp = HEAD_WIDTH ** -0.5 * math.log2(math.e)
    copies[0].wait()

    def project(index, carry):
        for copy in tile_copies(index):
            copy.wait()
        cols = pl.ds(pl.multiple_of(index * TILE, TILE), TILE)
        correction = jnp.dot(spread_ref[...], up_ref[:, cols], preferred_element_type=jnp.float32)
        query_ref[:, cols] = (base_ref[:, cols] + ADAPTER_SCALE * correction).astype(jnp.bfloat16)
        return carry

    lax.fori_loop(0, q_cols // TILE, project, 0)
    for copy in copies[1:]:
        copy.wait()
    dims = (((1,), (1,)), ((), ()))

    def several(turn, carry):
        places = []
        for lane in range(TOGETHER):
            index = turn * TOGETHER + lane
            row = pl.multiple_of(steps_ref[1, index] * BLOCK, BLOCK)
            start = steps_ref[2, index]
            base = pl.multiple_of(jnp.minimum(start // BLOCK * BLOCK, rows_total - window), BLOCK)
            old = pl.ds(steps_ref[0, index] * HITS, HITS)
            places.append((row, pl.ds(base, window), old, base, start, steps_ref[3, index]))
        chains = [(place, head) for place in places for head in range(kv_heads)]
        scores = []
        for (row, new, old, base, start, _), head in chains:
            at = head * 2 * HEAD_WIDTH
            wide = head * group * HEAD_WIDTH
            q_at = row + lax.broadcasted_iota(jnp.int32, (group * BLOCK, window), 0) % BLOCK
            k_at = base + lax.broadcasted_iota(jnp.int32, (group * BLOCK, window), 1)
            visible = (k_at >= start) & (k_at <= q_at)
            rows_q = jnp.concatenate(
                [
                    query_ref[pl.ds(row, BLOCK), wide + g * HEAD_WIDTH : wide + (g + 1) * HEAD_WIDTH]
                    for g in range(group)
                ],
                axis=0,
            )
            old_k = pages_ref[old, :, at : at + HEAD_WIDTH].reshape(HITS * PAGE, HEAD_WIDTH)
            new_k = cache_ref[new, at : at + HEAD_WIDTH]
            old_s = lax.dot_general(rows_q, old_k, dims, preferred_element_type=jnp.float32)
            new_s = lax.dot_general(rows_q, new_k, dims, preferred_element_type=jnp.float32)
            scores.append((old_s, jnp.where(visible, new_s, NEGATIVE)))
        weights = []
        for old_s, new_s in scores:
            top = jnp.maximum(
                jnp.max(old_s, axis=1, keepdims=True), jnp.max(new_s, axis=1, keepdims=True)
            )
            old_e = jnp.exp2((old_s - top) * sharp)
            new_e = jnp.exp2((new_s - top) * sharp)
            total = jnp.sum(old_e, axis=1, keepdims=True) + jnp.sum(new_e, axis=1, keepdims=True)
            weights.append((old_e.astype(jnp.bfloat16), new_e.astype(jnp.bfloat16), total))
        results = []
        for ((_, new, old, _, _, _), head), (old_e, new_e, total) in zip(chains, weights):
            at = head * 2 * HEAD_WIDTH + HEAD_WIDTH
            old_v = pages_ref[old, :, at : at + HEAD_WIDTH].reshape(HITS * PAGE, HEAD_WIDTH)
            new_v = cache_ref[new, at : at + HEAD_WIDTH]
            summed = jnp.dot(old_e, old_v, preferred_element_type=jnp.float32)
            summed += jnp.dot(new_e, new_v, preferred_element_type=jnp.float32)
            results.append((summed / total).astype(jnp.bfloat16))
        for ((row, _, _, _, start, end), head), result in zip(chains, results):
            own_at = row + lax.broadcasted_iota(jnp.int32, (BLOCK, HEAD_WIDTH), 0)
            own = (own_at >= start) & (own_at < end)
            for g in range(group):
                col = (head * group + g) * HEAD_WIDTH
                cols = slice(col, col + HEAD_WIDTH)
                before = out_ref[pl.ds(row, BLOCK), cols]
                out_ref[pl.ds(row, BLOCK), cols] = jnp.where(own, result[g * BLOCK : (g + 1) * BLOCK], before)
        return carry

    lax.fori_loop(0, steps_ref.shape[1] // TOGETHER, several, 0)


def attend(query_base, spread, up, cache, pages, starts, ends):
    rows, q_cols = query_base.shape
    steps_total = -(-(rows // BLOCK + starts.shape[0] - 1) // TOGETHER) * TOGETHER
    steps = attention_steps(starts, ends, steps_total)
    return pl.pallas_call(
        attention_kernel,
        out_shape=jax.ShapeDtypeStruct((rows, q_cols), jnp.bfloat16),
        in_specs=[pl.BlockSpec(memory_space=pltpu.SMEM)] + [pl.BlockSpec(memory_space=pltpu.HBM)] * 5,
        out_specs=pl.BlockSpec(memory_space=pltpu.VMEM),
        scratch_shapes=[
            pltpu.VMEM((rows, q_cols), jnp.bfloat16),
            *[pltpu.VMEM(each.shape, each.dtype) for each in (spread, up, query_base, cache, pages)],
            pltpu.SemaphoreType.DMA((3,)),
            pltpu.SemaphoreType.DMA((2, q_cols // TILE)),
        ],
        compiler_params=pltpu.CompilerParams(vmem_limit_bytes=VMEM_GRANT),
        cost_estimate=pl.CostEstimate(
            flops=4 * steps_total * BLOCK * q_cols * (HITS * PAGE + MOST + BLOCK) + 2 * spread.size * q_cols,
            bytes_accessed=4 * query_base.size + 2 * (2 * spread.size + up.size + cache.size + pages.size),
            transcendentals=0,
        ),
        name="attend",
    )(steps, spread, up, query_base, cache, pages)


def serve_kernel(asked_ref, store_ref, *refs):
    outs, sems = refs[:-1], refs[-1]
    for index, out in enumerate(outs):
        for place in range(out.shape[0]):
            page = asked_ref[index * out.shape[0] + place]
            pltpu.make_async_copy(store_ref.at[page], out.at[place], sems.at[index]).start()
    for index, out in enumerate(outs):
        pltpu.make_async_copy(out, out, sems.at[index]).wait()


def serve(asked, store):
    blocks, capacity = asked.shape
    shape = (capacity,) + store.shape[1:]
    return pl.pallas_call(
        serve_kernel,
        out_shape=[jax.ShapeDtypeStruct(shape, store.dtype)] * blocks,
        in_specs=[pl.BlockSpec(memory_space=pltpu.SMEM), pl.BlockSpec(memory_space=pltpu.HBM)],
        out_specs=[pl.BlockSpec(memory_space=pltpu.VMEM)] * blocks,
        scratch_shapes=[pltpu.SemaphoreType.DMA((blocks,))],
        compiler_params=pltpu.CompilerParams(vmem_limit_bytes=VMEM_GRANT),
        cost_estimate=pl.CostEstimate(
            flops=0, bytes_accessed=4 * blocks * math.prod(shape), transcendentals=0
        ),
        name="serve",
    )(asked.reshape(-1), store)


def assemble_kernel(source_ref, place_ref, *refs):
    sources, out, sem = refs[:-2], refs[-2], refs[-1]

    def one(index, carry):
        source = source_ref[index]
        place = place_ref[index]
        for number, ref in enumerate(sources):

            @pl.when(source == number)
            def _():
                pltpu.make_async_copy(ref.at[place], out.at[index], sem).start()

        return carry

    lax.fori_loop(0, out.shape[0], one, 0)
    pltpu.make_async_copy(out, out, sem).wait()


def assemble(source, place, sources):
    scalars = pl.BlockSpec(memory_space=pltpu.SMEM)
    shape = (source.shape[0],) + sources[0].shape[1:]
    return pl.pallas_call(
        assemble_kernel,
        out_shape=jax.ShapeDtypeStruct(shape, sources[0].dtype),
        in_specs=[scalars, scalars] + [pl.BlockSpec(memory_space=pltpu.HBM)] * len(sources),
        out_specs=pl.BlockSpec(memory_space=pltpu.VMEM),
        scratch_shapes=[pltpu.SemaphoreType.DMA],
        compiler_params=pltpu.CompilerParams(vmem_limit_bytes=VMEM_GRANT),
        cost_estimate=pl.CostEstimate(flops=0, bytes_accessed=4 * math.prod(shape), transcendentals=0),
        name="assemble",
    )(source, place, *sources)


def on_device(
    tokens,
    query_weight,
    keyvalue_weight,
    adapter_down_weight,
    adapter_up_weight,
    keyvalue_page_store,
    span_token_length,
    adapter_owner,
    adapter_local_index,
    page_owner,
    page_local_index,
):
    peers = lax.axis_size("dp")
    half = peers // 2
    me = lax.axis_index("dp")
    tok_rows = tokens.shape[0]
    q_cols = query_weight.shape[1]
    rank = adapter_down_weight.shape[2]
    adapter_slots = peers * ADP_CAP

    def swap(array, distance):
        return lax.ppermute(array, "dp", [(peer, peer ^ distance) for peer in range(peers)])

    page_count = page_local_index.shape[0]
    request_count = adapter_local_index.shape[0]
    raw = jnp.concatenate([page_owner[:, 0], page_local_index, adapter_owner[:, 0], adapter_local_index])
    tile = jnp.pad(raw, (0, 8 * 128 - raw.shape[0])).reshape(8, 128)
    everyone = lax.all_gather(tile, "dp", axis=0, tiled=True).reshape(peers, 8 * 128)
    mirrored_store = swap(keyvalue_page_store, half)

    page_cap = max(2, 2 * page_count // peers)
    group = everyone[jnp.arange(half, dtype=jnp.int32) ^ me]
    group_owner = group[:, :page_count]
    group_local = group[:, page_count : 2 * page_count]
    group_order = earlier_alike(group_owner)
    near_asked = asked_of(me, group_owner, group_order, group_local, page_cap)
    far_asked = asked_of(me ^ half, group_owner, group_order, group_local, page_cap)
    all_owner = everyone[:, 2 * page_count : 2 * page_count + request_count]
    all_local = everyone[:, 2 * page_count + request_count : raw.shape[0]]
    adapter_asked = asked_of(me, all_owner, earlier_alike(all_owner), all_local, ADP_CAP).reshape(-1)
    adapter_pos = adapter_owner[:, 0] * ADP_CAP + earlier_alike(adapter_owner[:, 0])
    page_source = page_owner[:, 0] ^ me
    page_place = jnp.where(page_source % half == 0, page_local_index, earlier_alike(page_owner[:, 0]))

    near = list(serve(near_asked[1:], keyvalue_page_store))
    near = [swap(pages, i + 1) for i, pages in enumerate(near)]
    down_rows = adapter_down_weight[adapter_asked]
    up_rows = adapter_up_weight[adapter_asked]

    piece = lax.all_gather(tokens, "tensor", axis=1, tiled=True)
    query_base = jnp.dot(piece, query_weight, preferred_element_type=jnp.float32)
    new_cache = jnp.dot(piece, keyvalue_weight, preferred_element_type=jnp.float32).astype(jnp.bfloat16)

    down_rows, mirrored_store, query_base, new_cache, near = lax.optimization_barrier(
        (down_rows, mirrored_store, query_base, new_cache, near)
    )
    down_sent = lax.all_to_all(down_rows, "dp", split_axis=0, concat_axis=0, tiled=True)
    far = list(serve(far_asked[1:], mirrored_store))
    far = [swap(pages, i + 1) for i, pages in enumerate(far[:-1])] + far[-1:]
    up_rows, down_sent, far = lax.optimization_barrier((up_rows, down_sent, far))
    up_sent = lax.all_to_all(up_rows, "dp", split_axis=0, concat_axis=0, tiled=True)
    far[-1] = swap(far[-1], half - 1)

    lengths = span_token_length[0]
    ends = jnp.cumsum(lengths)
    starts = ends - lengths
    steps = jnp.arange(tok_rows, dtype=jnp.int32)[:, None]
    member = (steps >= starts[None, :]) & (steps < ends[None, :])
    slot = jnp.sum(jnp.where(member, adapter_pos[None, :], 0), axis=1)
    in_slot = slot[:, None] == jnp.arange(adapter_slots, dtype=jnp.int32)[None, :]

    down_part = jnp.einsum("tn,snk->tsk", tokens, down_sent, preferred_element_type=jnp.float32)
    shrink_part = jnp.sum(jnp.where(in_slot[:, :, None], down_part, 0.0), axis=1)
    shrink = lax.psum(shrink_part, "tensor").astype(jnp.bfloat16)
    spread = jnp.where(in_slot[:, :, None], shrink[:, None, :], 0).reshape(tok_rows, adapter_slots * rank)
    prefix_pages = assemble(page_source, page_place, [keyvalue_page_store, *near, mirrored_store, *far])
    up = up_sent.reshape(adapter_slots * rank, q_cols)
    out = attend(query_base, spread, up, new_cache, prefix_pages, starts, ends)
    return (out, new_cache)


def solution(mesh):
    return jax.shard_map(
        on_device,
        mesh=mesh,
        in_specs=(
            P("dp", "tensor"),
            P(None, "tensor"),
            P(None, "tensor"),
            P("dp", "tensor", None),
            P("dp", None, "tensor"),
            P("dp", None, "tensor"),
            P("dp", None),
            P("dp", None),
            P("dp"),
            P("dp", None),
            P("dp"),
        ),
        out_specs=(P("dp", "tensor"), P("dp", "tensor")),
        check_vma=False,
    )
```

```python
import functools
import math

import jax
import jax.numpy as jnp
from jax import lax
from jax.experimental import pallas as pl
from jax.experimental.pallas import tpu as pltpu
from jax.sharding import PartitionSpec as P

HEAD_WIDTH = 128
ADP_CAP = 2
PAGE = 64
HITS = 4
MOST = 128
BLOCK = 32
TOGETHER = 4
TILE = 256
VMEM_GRANT = 60 * 1024 * 1024

ADAPTER_SCALE = 0.5
NEGATIVE = -1e30


def earlier_alike(owner):
    count = owner.shape[-1]
    ahead = jnp.arange(count, dtype=jnp.int32)[None, :] < jnp.arange(count, dtype=jnp.int32)[:, None]
    alike = owner[..., None, :] == owner[..., :, None]
    return jnp.sum((alike & ahead).astype(jnp.int32), axis=-1)


def asked_of(holder, owner, order, local, capacity):
    place = jnp.arange(capacity, dtype=jnp.int32)[None, :, None]
    match = (owner[:, None, :] == holder) & (order[:, None, :] == place)
    return jnp.sum(jnp.where(match, local[:, None, :], 0), axis=2)


def attention_steps(starts, ends, total):
    first = starts // BLOCK
    count = (ends - 1) // BLOCK - first + 1
    upto = jnp.cumsum(count)
    step = jnp.minimum(jnp.arange(total, dtype=jnp.int32), upto[-1] - 1)
    request = jnp.sum((upto[None, :] <= step[:, None]).astype(jnp.int32), axis=1)
    pick = request[:, None] == jnp.arange(starts.shape[0], dtype=jnp.int32)[None, :]

    def at(values):
        return jnp.sum(jnp.where(pick, values[None, :], 0), axis=1)

    block = at(first) + step - at(upto - count)
    return jnp.stack([request, block, at(starts), at(ends)])


def attention_kernel(steps_ref, spread_hbm, up_hbm, base_hbm, cache_hbm, pages_hbm, out_ref, query_ref, *rest):
    spread_ref, up_ref, base_ref, cache_ref, pages_ref, sems, tile_sems = rest

    def tile_copies(index):
        cols = pl.ds(pl.multiple_of(index * TILE, TILE), TILE)
        return (
            pltpu.make_async_copy(up_hbm.at[:, cols], up_ref.at[:, cols], tile_sems.at[0, index]),
            pltpu.make_async_copy(base_hbm.at[:, cols], base_ref.at[:, cols], tile_sems.at[1, index]),
        )

    pairs = [(spread_hbm, spread_ref), (cache_hbm, cache_ref), (pages_hbm, pages_ref)]
    copies = [pltpu.make_async_copy(*pair, sems.at[index]) for index, pair in enumerate(pairs)]
    copies[0].start()
    for index in range(base_ref.shape[1] // TILE):
        for copy in tile_copies(index):
            copy.start()
    for copy in copies[1:]:
        copy.start()
    rows_total, q_cols = base_ref.shape
    kv_heads = cache_ref.shape[1] // (2 * HEAD_WIDTH)
    group = q_cols // HEAD_WIDTH // kv_heads
    window = min(rows_total, MOST + BLOCK)
    sharp = HEAD_WIDTH ** -0.5 * math.log2(math.e)
    copies[0].wait()

    def project(index, carry):
        for copy in tile_copies(index):
            copy.wait()
        cols = pl.ds(pl.multiple_of(index * TILE, TILE), TILE)
        correction = jnp.dot(spread_ref[...], up_ref[:, cols], preferred_element_type=jnp.float32)
        query_ref[:, cols] = (base_ref[:, cols] + ADAPTER_SCALE * correction).astype(jnp.bfloat16)
        return carry

    lax.fori_loop(0, q_cols // TILE, project, 0)
    for copy in copies[1:]:
        copy.wait()
    dims = (((1,), (1,)), ((), ()))

    def several(turn, carry):
        places = []
        for lane in range(TOGETHER):
            index = turn * TOGETHER + lane
            row = pl.multiple_of(steps_ref[1, index] * BLOCK, BLOCK)
            start = steps_ref[2, index]
            base = pl.multiple_of(jnp.minimum(start // BLOCK * BLOCK, rows_total - window), BLOCK)
            old = pl.ds(steps_ref[0, index] * HITS, HITS)
            places.append((row, pl.ds(base, window), old, base, start, steps_ref[3, index]))
        chains = [(place, head) for place in places for head in range(kv_heads)]
        scores = []
        for (row, new, old, base, start, _), head in chains:
            at = head * 2 * HEAD_WIDTH
            wide = head * group * HEAD_WIDTH
            q_at = row + lax.broadcasted_iota(jnp.int32, (group * BLOCK, window), 0) % BLOCK
            k_at = base + lax.broadcasted_iota(jnp.int32, (group * BLOCK, window), 1)
            visible = (k_at >= start) & (k_at <= q_at)
            rows_q = jnp.concatenate(
                [
                    query_ref[pl.ds(row, BLOCK), wide + g * HEAD_WIDTH : wide + (g + 1) * HEAD_WIDTH]
                    for g in range(group)
                ],
                axis=0,
            )
            old_k = pages_ref[old, :, at : at + HEAD_WIDTH].reshape(HITS * PAGE, HEAD_WIDTH)
            new_k = cache_ref[new, at : at + HEAD_WIDTH]
            old_s = lax.dot_general(rows_q, old_k, dims, preferred_element_type=jnp.float32)
            new_s = lax.dot_general(rows_q, new_k, dims, preferred_element_type=jnp.float32)
            scores.append((old_s, jnp.where(visible, new_s, NEGATIVE)))
        weights = []
        for old_s, new_s in scores:
            top = jnp.maximum(
                jnp.max(old_s, axis=1, keepdims=True), jnp.max(new_s, axis=1, keepdims=True)
            )
            old_e = jnp.exp2((old_s - top) * sharp)
            new_e = jnp.exp2((new_s - top) * sharp)
            total = jnp.sum(old_e, axis=1, keepdims=True) + jnp.sum(new_e, axis=1, keepdims=True)
            weights.append((old_e.astype(jnp.bfloat16), new_e.astype(jnp.bfloat16), total))
        results = []
        for ((_, new, old, _, _, _), head), (old_e, new_e, total) in zip(chains, weights):
            at = head * 2 * HEAD_WIDTH + HEAD_WIDTH
            old_v = pages_ref[old, :, at : at + HEAD_WIDTH].reshape(HITS * PAGE, HEAD_WIDTH)
            new_v = cache_ref[new, at : at + HEAD_WIDTH]
            summed = jnp.dot(old_e, old_v, preferred_element_type=jnp.float32)
            summed += jnp.dot(new_e, new_v, preferred_element_type=jnp.float32)
            results.append((summed / total).astype(jnp.bfloat16))
        for ((row, _, _, _, start, end), head), result in zip(chains, results):
            own_at = row + lax.broadcasted_iota(jnp.int32, (BLOCK, HEAD_WIDTH), 0)
            own = (own_at >= start) & (own_at < end)
            for g in range(group):
                col = (head * group + g) * HEAD_WIDTH
                cols = slice(col, col + HEAD_WIDTH)
                before = out_ref[pl.ds(row, BLOCK), cols]
                out_ref[pl.ds(row, BLOCK), cols] = jnp.where(own, result[g * BLOCK : (g + 1) * BLOCK], before)
        return carry

    lax.fori_loop(0, steps_ref.shape[1] // TOGETHER, several, 0)


def attend(query_base, spread, up, cache, pages, starts, ends):
    rows, q_cols = query_base.shape
    steps_total = -(-(rows // BLOCK + starts.shape[0] - 1) // TOGETHER) * TOGETHER
    steps = attention_steps(starts, ends, steps_total)
    return pl.pallas_call(
        attention_kernel,
        out_shape=jax.ShapeDtypeStruct((rows, q_cols), jnp.bfloat16),
        in_specs=[pl.BlockSpec(memory_space=pltpu.SMEM)] + [pl.BlockSpec(memory_space=pltpu.HBM)] * 5,
        out_specs=pl.BlockSpec(memory_space=pltpu.VMEM),
        scratch_shapes=[
            pltpu.VMEM((rows, q_cols), jnp.bfloat16),
            *[pltpu.VMEM(each.shape, each.dtype) for each in (spread, up, query_base, cache, pages)],
            pltpu.SemaphoreType.DMA((3,)),
            pltpu.SemaphoreType.DMA((2, q_cols // TILE)),
        ],
        compiler_params=pltpu.CompilerParams(vmem_limit_bytes=VMEM_GRANT),
        cost_estimate=pl.CostEstimate(
            flops=4 * steps_total * BLOCK * q_cols * (HITS * PAGE + MOST + BLOCK) + 2 * spread.size * q_cols,
            bytes_accessed=4 * query_base.size + 2 * (2 * spread.size + up.size + cache.size + pages.size),
            transcendentals=0,
        ),
        name="attend",
    )(steps, spread, up, query_base, cache, pages)


def serve_kernel(pieces, asked_ref, store_ref, *refs):
    outs, sems = refs[:-1], refs[-1]
    for number, ((block, first, end), out) in enumerate(zip(pieces, outs)):
        for place in range(out.shape[0]):
            page = asked_ref[block * out.shape[0] + place]
            rows = store_ref.at[page, first:end]
            pltpu.make_async_copy(rows, out.at[place], sems.at[number]).start()
    for number, out in enumerate(outs):
        pltpu.make_async_copy(out, out, sems.at[number]).wait()


def serve(asked, store, pieces):
    capacity = asked.shape[1]
    shapes = [(capacity, end - first, store.shape[2]) for _, first, end in pieces]
    return pl.pallas_call(
        functools.partial(serve_kernel, pieces),
        out_shape=[jax.ShapeDtypeStruct(shape, store.dtype) for shape in shapes],
        in_specs=[pl.BlockSpec(memory_space=pltpu.SMEM), pl.BlockSpec(memory_space=pltpu.HBM)],
        out_specs=[pl.BlockSpec(memory_space=pltpu.VMEM)] * len(pieces),
        scratch_shapes=[pltpu.SemaphoreType.DMA((len(pieces),))],
        compiler_params=pltpu.CompilerParams(vmem_limit_bytes=VMEM_GRANT),
        cost_estimate=pl.CostEstimate(
            flops=0, bytes_accessed=4 * sum(math.prod(shape) for shape in shapes), transcendentals=0
        ),
        name="serve",
    )(asked.reshape(-1), store)


def assemble_kernel(pieces, source_ref, place_ref, *refs):
    out, sem = refs[-2:]

    def one(index, carry):
        source = source_ref[index]
        place = place_ref[index]
        for number in range(max(block for block, _, _ in pieces) + 1):

            @pl.when(source == number)
            def _():
                for (block, first, end), ref in zip(pieces, refs):
                    if block == number:
                        pltpu.make_async_copy(ref.at[place], out.at[index, first:end], sem).start()

        return carry

    lax.fori_loop(0, out.shape[0], one, 0)
    pltpu.make_async_copy(out, out, sem).wait()


def assemble(source, place, arrays, pieces):
    scalars = pl.BlockSpec(memory_space=pltpu.SMEM)
    shape = (source.shape[0],) + arrays[0].shape[1:]
    return pl.pallas_call(
        functools.partial(assemble_kernel, pieces),
        out_shape=jax.ShapeDtypeStruct(shape, arrays[0].dtype),
        in_specs=[scalars, scalars] + [pl.BlockSpec(memory_space=pltpu.HBM)] * len(arrays),
        out_specs=pl.BlockSpec(memory_space=pltpu.VMEM),
        scratch_shapes=[pltpu.SemaphoreType.DMA],
        compiler_params=pltpu.CompilerParams(vmem_limit_bytes=VMEM_GRANT),
        cost_estimate=pl.CostEstimate(flops=0, bytes_accessed=4 * math.prod(shape), transcendentals=0),
        name="assemble",
    )(source, place, *arrays)


def on_device(
    tokens,
    query_weight,
    keyvalue_weight,
    adapter_down_weight,
    adapter_up_weight,
    keyvalue_page_store,
    span_token_length,
    adapter_owner,
    adapter_local_index,
    page_owner,
    page_local_index,
):
    peers = lax.axis_size("dp")
    half = peers // 2
    me = lax.axis_index("dp")
    tok_rows = tokens.shape[0]
    q_cols = query_weight.shape[1]
    rank = adapter_down_weight.shape[2]
    adapter_slots = peers * ADP_CAP

    def swap(array, distance):
        return lax.ppermute(array, "dp", [(peer, peer ^ distance) for peer in range(peers)])

    page_count = page_local_index.shape[0]
    request_count = adapter_local_index.shape[0]
    raw = jnp.concatenate([page_owner[:, 0], page_local_index, adapter_owner[:, 0], adapter_local_index])
    everyone = lax.all_to_all(
        jnp.broadcast_to(raw[None], (peers, raw.shape[0])), "dp", split_axis=0, concat_axis=0, tiled=True
    )
    store, down_store, everyone = lax.optimization_barrier((keyvalue_page_store, adapter_down_weight, everyone))
    mirrored_store = swap(store, half)

    page_cap = max(2, 2 * page_count // peers)
    group = everyone[jnp.arange(half, dtype=jnp.int32) ^ me]
    group_owner = group[:, :page_count]
    group_local = group[:, page_count : 2 * page_count]
    group_order = earlier_alike(group_owner)
    near_asked = asked_of(me, group_owner, group_order, group_local, page_cap)
    far_asked = asked_of(me ^ half, group_owner, group_order, group_local, page_cap)
    all_owner = everyone[:, 2 * page_count : 2 * page_count + request_count]
    all_local = everyone[:, 2 * page_count + request_count :]
    adapter_asked = asked_of(me, all_owner, earlier_alike(all_owner), all_local, ADP_CAP).reshape(-1)
    adapter_pos = adapter_owner[:, 0] * ADP_CAP + earlier_alike(adapter_owner[:, 0])
    page_source = page_owner[:, 0] ^ me
    page_place = jnp.where(page_source % half == 0, page_local_index, earlier_alike(page_owner[:, 0]))

    page = keyvalue_page_store.shape[1]
    near_pieces = [(block, 0, page) for block in range(half - 1)]
    near = serve(near_asked[1:], store, near_pieces)
    near = [swap(pages, block + 1) for pages, (block, _, _) in zip(near, near_pieces)]
    down_rows = down_store[adapter_asked]
    up_rows = adapter_up_weight[adapter_asked]

    piece = lax.all_gather(tokens, "tensor", axis=1, tiled=True)
    query_base = jnp.dot(piece, query_weight, preferred_element_type=jnp.float32)
    new_cache = jnp.dot(piece, keyvalue_weight, preferred_element_type=jnp.float32).astype(jnp.bfloat16)

    down_rows, mirrored_store, query_base, new_cache, near = lax.optimization_barrier(
        (down_rows, mirrored_store, query_base, new_cache, near)
    )
    down_sent = lax.all_to_all(down_rows, "dp", split_axis=0, concat_axis=0, tiled=True)
    far_pieces = near_pieces[:-1] + [(half - 2, 0, page // 2), (half - 2, page // 2, page)]
    far = list(serve(far_asked[1:], mirrored_store, far_pieces))
    far[:-1] = [swap(pages, block + 1) for pages, (block, _, _) in zip(far[:-1], far_pieces)]
    up_rows, down_sent, far = lax.optimization_barrier((up_rows, down_sent, far))
    up_sent = lax.all_to_all(up_rows, "dp", split_axis=0, concat_axis=0, tiled=True)
    far[-1] = swap(far[-1], half - 1)

    lengths = span_token_length[0]
    ends = jnp.cumsum(lengths)
    starts = ends - lengths
    steps = jnp.arange(tok_rows, dtype=jnp.int32)[:, None]
    member = (steps >= starts[None, :]) & (steps < ends[None, :])
    slot = jnp.sum(jnp.where(member, adapter_pos[None, :], 0), axis=1)
    in_slot = slot[:, None] == jnp.arange(adapter_slots, dtype=jnp.int32)[None, :]

    down_part = jnp.einsum("tn,snk->tsk", tokens, down_sent, preferred_element_type=jnp.float32)
    shrink_part = jnp.sum(jnp.where(in_slot[:, :, None], down_part, 0.0), axis=1)
    shrink = lax.psum(shrink_part, "tensor").astype(jnp.bfloat16)
    spread = jnp.where(in_slot[:, :, None], shrink[:, None, :], 0).reshape(tok_rows, adapter_slots * rank)
    pieces = [(0, 0, page)]
    pieces += [(block + 1, first, end) for block, first, end in near_pieces]
    pieces += [(half, 0, page)]
    pieces += [(half + block + 1, first, end) for block, first, end in far_pieces]
    prefix_pages = assemble(page_source, page_place, [store, *near, mirrored_store, *far], pieces)
    up = up_sent.reshape(adapter_slots * rank, q_cols)
    out = attend(query_base, spread, up, new_cache, prefix_pages, starts, ends)
    return (out, new_cache)


def solution(mesh):
    return jax.shard_map(
        on_device,
        mesh=mesh,
        in_specs=(
            P("dp", "tensor"),
            P(None, "tensor"),
            P(None, "tensor"),
            P("dp", "tensor", None),
            P("dp", None, "tensor"),
            P("dp", None, "tensor"),
            P("dp", None),
            P("dp", None),
            P("dp"),
            P("dp", None),
            P("dp"),
        ),
        out_specs=(P("dp", "tensor"), P("dp", "tensor")),
        check_vma=False,
    )
```

```python
import functools
import math

import jax
import jax.numpy as jnp
from jax import lax
from jax.experimental import pallas as pl
from jax.experimental.pallas import tpu as pltpu
from jax.sharding import PartitionSpec as P

HEAD_WIDTH = 128
ADP_CAP = 2
HITS = 4
MOST = 128
BLOCK = 32
TOGETHER = 4
TILE = 256
VMEM_GRANT = 60 * 1024 * 1024

ADAPTER_SCALE = 0.5
NEGATIVE = -1e30


def earlier_alike(owner):
    count = owner.shape[-1]
    ahead = jnp.arange(count, dtype=jnp.int32)[None, :] < jnp.arange(count, dtype=jnp.int32)[:, None]
    alike = owner[..., None, :] == owner[..., :, None]
    return jnp.sum((alike & ahead).astype(jnp.int32), axis=-1)


def asked_of(holder, owner, order, local, capacity):
    place = jnp.arange(capacity, dtype=jnp.int32)[None, :, None]
    match = (owner[:, None, :] == holder) & (order[:, None, :] == place)
    return jnp.sum(jnp.where(match, local[:, None, :], 0), axis=2)


def attention_steps(starts, ends, total):
    first = starts // BLOCK
    count = (ends - 1) // BLOCK - first + 1
    upto = jnp.cumsum(count)
    step = jnp.minimum(jnp.arange(total, dtype=jnp.int32), upto[-1] - 1)
    request = jnp.sum((upto[None, :] <= step[:, None]).astype(jnp.int32), axis=1)
    pick = request[:, None] == jnp.arange(starts.shape[0], dtype=jnp.int32)[None, :]

    def at(values):
        return jnp.sum(jnp.where(pick, values[None, :], 0), axis=1)

    block = at(first) + step - at(upto - count)
    return jnp.stack([request, block, at(starts), at(ends)])


def attention_kernel(steps_ref, spread_hbm, up_any, base_hbm, fresh_hbm, pages_hbm, out_ref, query_ref, *rest):
    spread_ref, up_ref, base_ref, cache_ref, sems, tile_sems = rest
    q_cols = base_ref.shape[1]
    kv_heads = cache_ref.shape[2] // (2 * HEAD_WIDTH)
    group = q_cols // HEAD_WIDTH // kv_heads
    held = pages_hbm.shape[1]
    sharp = HEAD_WIDTH ** -0.5 * math.log2(math.e)

    def tile_copies(index):
        cols = pl.ds(pl.multiple_of(index * TILE, TILE), TILE)
        return (
            pltpu.make_async_copy(up_any.at[:, cols], up_ref.at[:, cols], tile_sems.at[0, index]),
            pltpu.make_async_copy(base_hbm.at[:, cols], base_ref.at[:, cols], tile_sems.at[1, index]),
        )

    copies = [
        pltpu.make_async_copy(spread_hbm, spread_ref, sems.at[0]),
        pltpu.make_async_copy(pages_hbm, cache_ref.at[:, :held], sems.at[1]),
        pltpu.make_async_copy(fresh_hbm, cache_ref.at[:, held:], sems.at[2]),
    ]
    copies[0].start()
    for index in range(q_cols // TILE):
        for copy in tile_copies(index):
            copy.start()
    for copy in copies[1:]:
        copy.start()
    copies[0].wait()

    def project(index, carry):
        for copy in tile_copies(index):
            copy.wait()
        cols = pl.ds(pl.multiple_of(index * TILE, TILE), TILE)
        correction = jnp.dot(spread_ref[...], up_ref[:, cols], preferred_element_type=jnp.float32)
        query_ref[:, cols] = (base_ref[:, cols] + ADAPTER_SCALE * correction).astype(jnp.bfloat16)
        return carry

    lax.fori_loop(0, q_cols // TILE, project, 0)
    for copy in copies[1:]:
        copy.wait()
    dims = (((1,), (1,)), ((), ()))
    q_at = lax.broadcasted_iota(jnp.int32, (group * BLOCK, MOST), 0) % BLOCK
    ahead = lax.broadcasted_iota(jnp.int32, (group * BLOCK, MOST), 1) - q_at
    own_at = lax.broadcasted_iota(jnp.int32, (BLOCK, HEAD_WIDTH), 0)

    def several(turn, carry):
        places = []
        for lane in range(TOGETHER):
            index = turn * TOGETHER + lane
            row = pl.multiple_of(steps_ref[1, index] * BLOCK, BLOCK)
            places.append((steps_ref[0, index], row, steps_ref[2, index], steps_ref[3, index]))
        chains = [(place, head) for place in places for head in range(kv_heads)]
        scores = []
        for (request, row, start, _), head in chains:
            at = head * 2 * HEAD_WIDTH
            wide = head * group * HEAD_WIDTH
            rows_q = jnp.concatenate(
                [
                    query_ref[pl.ds(row, BLOCK), wide + g * HEAD_WIDTH : wide + (g + 1) * HEAD_WIDTH]
                    for g in range(group)
                ],
                axis=0,
            )
            keys = cache_ref[request, :, at : at + HEAD_WIDTH]
            score = lax.dot_general(rows_q, keys, dims, preferred_element_type=jnp.float32)
            scores.append((score[:, :held], jnp.where(ahead <= row - start, score[:, held:], NEGATIVE)))
        weights = []
        for old_s, new_s in scores:
            top = jnp.maximum(
                jnp.max(old_s, axis=1, keepdims=True), jnp.max(new_s, axis=1, keepdims=True)
            )
            old_e = jnp.exp2((old_s - top) * sharp)
            new_e = jnp.exp2((new_s - top) * sharp)
            total = jnp.sum(old_e, axis=1, keepdims=True) + jnp.sum(new_e, axis=1, keepdims=True)
            weights.append((jnp.concatenate([old_e, new_e], axis=1).astype(jnp.bfloat16), total))
        results = []
        for ((request, _, _, _), head), (weight, total) in zip(chains, weights):
            at = head * 2 * HEAD_WIDTH + HEAD_WIDTH
            values = cache_ref[request, :, at : at + HEAD_WIDTH]
            summed = jnp.dot(weight, values, preferred_element_type=jnp.float32)
            results.append((summed / total).astype(jnp.bfloat16))
        for ((_, row, start, end), head), result in zip(chains, results):
            own = (own_at >= start - row) & (own_at < end - row)
            for g in range(group):
                col = (head * group + g) * HEAD_WIDTH
                cols = slice(col, col + HEAD_WIDTH)
                before = out_ref[pl.ds(row, BLOCK), cols]
                out_ref[pl.ds(row, BLOCK), cols] = jnp.where(own, result[g * BLOCK : (g + 1) * BLOCK], before)
        return carry

    lax.fori_loop(0, steps_ref.shape[1] // TOGETHER, several, 0)


def attend(query_base, spread, up, fresh, pages, starts, ends):
    rows, q_cols = query_base.shape
    requests, held, kv_cols = pages.shape
    steps_total = -(-(rows // BLOCK + requests - 1) // TOGETHER) * TOGETHER
    steps = attention_steps(starts, ends, steps_total)
    hbm = pl.BlockSpec(memory_space=pltpu.HBM)
    return pl.pallas_call(
        attention_kernel,
        out_shape=jax.ShapeDtypeStruct((rows, q_cols), jnp.bfloat16),
        in_specs=[pl.BlockSpec(memory_space=pltpu.SMEM), hbm, pl.BlockSpec(memory_space=pl.ANY), hbm, hbm, hbm],
        out_specs=pl.BlockSpec(memory_space=pltpu.VMEM),
        scratch_shapes=[
            pltpu.VMEM((rows, q_cols), jnp.bfloat16),
            *[pltpu.VMEM(each.shape, each.dtype) for each in (spread, up, query_base)],
            pltpu.VMEM((requests, held + MOST, kv_cols), pages.dtype),
            pltpu.SemaphoreType.DMA((3,)),
            pltpu.SemaphoreType.DMA((2, q_cols // TILE)),
        ],
        compiler_params=pltpu.CompilerParams(vmem_limit_bytes=VMEM_GRANT),
        cost_estimate=pl.CostEstimate(
            flops=4 * steps_total * BLOCK * q_cols * (held + MOST) + 2 * spread.size * q_cols,
            bytes_accessed=4 * query_base.size + 2 * (2 * spread.size + up.size + fresh.size + pages.size),
            transcendentals=0,
        ),
        name="attend",
    )(steps, spread, up, query_base, fresh, pages)


def serve_kernel(pieces, asked_ref, store_ref, *refs):
    outs, sems = refs[:-1], refs[-1]
    for number, ((block, first, end), out) in enumerate(zip(pieces, outs)):
        for place in range(out.shape[0]):
            page = asked_ref[block * out.shape[0] + place]
            rows = store_ref.at[page, first:end]
            pltpu.make_async_copy(rows, out.at[place], sems.at[number]).start()
    for number, out in enumerate(outs):
        pltpu.make_async_copy(out, out, sems.at[number]).wait()


def serve(asked, store, pieces):
    capacity = asked.shape[1]
    shapes = [(capacity, end - first, store.shape[2]) for _, first, end in pieces]
    return pl.pallas_call(
        functools.partial(serve_kernel, pieces),
        out_shape=[jax.ShapeDtypeStruct(shape, store.dtype) for shape in shapes],
        in_specs=[pl.BlockSpec(memory_space=pltpu.SMEM), pl.BlockSpec(memory_space=pltpu.HBM)],
        out_specs=[pl.BlockSpec(memory_space=pltpu.VMEM)] * len(pieces),
        scratch_shapes=[pltpu.SemaphoreType.DMA((len(pieces),))],
        compiler_params=pltpu.CompilerParams(vmem_limit_bytes=VMEM_GRANT),
        cost_estimate=pl.CostEstimate(
            flops=0, bytes_accessed=4 * sum(math.prod(shape) for shape in shapes), transcendentals=0
        ),
        name="serve",
    )(asked.reshape(-1), store)


def assemble_kernel(pieces, source_ref, place_ref, *refs):
    out, sem = refs[-2:]

    def one(index, carry):
        source = source_ref[index]
        place = place_ref[index]
        for number in range(max(block for block, _, _ in pieces) + 1):

            @pl.when(source == number)
            def _():
                for (block, first, end), ref in zip(pieces, refs):
                    if block == number:
                        pltpu.make_async_copy(ref.at[place], out.at[index, first:end], sem).start()

        return carry

    lax.fori_loop(0, out.shape[0], one, 0)
    pltpu.make_async_copy(out, out, sem).wait()


def assemble(source, place, arrays, pieces):
    scalars = pl.BlockSpec(memory_space=pltpu.SMEM)
    shape = (source.shape[0],) + arrays[0].shape[1:]
    return pl.pallas_call(
        functools.partial(assemble_kernel, pieces),
        out_shape=jax.ShapeDtypeStruct(shape, arrays[0].dtype),
        in_specs=[scalars, scalars] + [pl.BlockSpec(memory_space=pltpu.HBM)] * len(arrays),
        out_specs=pl.BlockSpec(memory_space=pltpu.VMEM),
        scratch_shapes=[pltpu.SemaphoreType.DMA],
        compiler_params=pltpu.CompilerParams(vmem_limit_bytes=VMEM_GRANT),
        cost_estimate=pl.CostEstimate(flops=0, bytes_accessed=4 * math.prod(shape), transcendentals=0),
        name="assemble",
    )(source, place, *arrays)


def on_device(
    tokens,
    query_weight,
    keyvalue_weight,
    adapter_down_weight,
    adapter_up_weight,
    keyvalue_page_store,
    span_token_length,
    adapter_owner,
    adapter_local_index,
    page_owner,
    page_local_index,
):
    peers = lax.axis_size("dp")
    half = peers // 2
    me = lax.axis_index("dp")
    tok_rows = tokens.shape[0]
    q_cols = query_weight.shape[1]
    rank = adapter_down_weight.shape[2]
    adapter_slots = peers * ADP_CAP

    def swap(array, distance):
        return lax.ppermute(array, "dp", [(peer, peer ^ distance) for peer in range(peers)])

    page_count = page_local_index.shape[0]
    request_count = adapter_local_index.shape[0]
    raw = jnp.concatenate([page_owner[:, 0], page_local_index, adapter_owner[:, 0], adapter_local_index])
    everyone = lax.all_to_all(
        jnp.broadcast_to(raw[None], (peers, raw.shape[0])), "dp", split_axis=0, concat_axis=0, tiled=True
    )
    page = keyvalue_page_store.shape[1]
    parts = [(0, page // 4), (page // 4, page)]
    pools = [keyvalue_page_store[:, first:end] for first, end in parts]
    store, down_store, everyone, pools = lax.optimization_barrier(
        (keyvalue_page_store, adapter_down_weight, everyone, pools)
    )

    page_cap = max(2, 2 * page_count // peers)
    group = everyone[jnp.arange(half, dtype=jnp.int32) ^ me]
    group_owner = group[:, :page_count]
    group_local = group[:, page_count : 2 * page_count]
    group_order = earlier_alike(group_owner)
    near_asked = asked_of(me, group_owner, group_order, group_local, page_cap)
    far_asked = asked_of(me ^ half, group_owner, group_order, group_local, page_cap)
    all_owner = everyone[:, 2 * page_count : 2 * page_count + request_count]
    all_local = everyone[:, 2 * page_count + request_count :]
    adapter_asked = asked_of(me, all_owner, earlier_alike(all_owner), all_local, ADP_CAP).reshape(-1)
    adapter_pos = adapter_owner[:, 0] * ADP_CAP + earlier_alike(adapter_owner[:, 0])
    page_source = page_owner[:, 0] ^ me
    page_place = jnp.where(page_source % half == 0, page_local_index, earlier_alike(page_owner[:, 0]))

    pools[1], near_asked, far_asked = lax.optimization_barrier((pools[1], near_asked, far_asked))
    mirrored = [swap(pool, half) for pool in pools]
    near_pieces = [(block, 0, page) for block in range(half - 1)]
    near = serve(near_asked[1:], store, near_pieces)
    near = [swap(pages, block + 1) for pages, (block, _, _) in zip(near, near_pieces)]
    down_rows = down_store[adapter_asked]
    up_rows = adapter_up_weight[adapter_asked]

    piece = lax.all_gather(tokens, "tensor", axis=1, tiled=True)
    query_base = jnp.dot(piece, query_weight, preferred_element_type=jnp.float32)
    new_cache = jnp.dot(piece, keyvalue_weight, preferred_element_type=jnp.float32).astype(jnp.bfloat16)

    def far_blocks(part):
        first, end = parts[part]
        pages = serve(far_asked[1:], mirrored[part], [(block, 0, end - first) for block in range(half - 1)])
        return [swap(block, number + 1) for number, block in enumerate(pages)]

    far = [far_blocks(0)]
    down_rows, mirrored, query_base, new_cache, near, far = lax.optimization_barrier(
        (down_rows, mirrored, query_base, new_cache, near, far)
    )
    down_sent = lax.all_to_all(down_rows, "dp", split_axis=0, concat_axis=0, tiled=True)
    far.append(far_blocks(1))
    up_rows, down_sent, far = lax.optimization_barrier((up_rows, down_sent, far))
    up_sent = lax.all_to_all(up_rows, "dp", split_axis=0, concat_axis=0, tiled=True)

    lengths = span_token_length[0]
    ends = jnp.cumsum(lengths)
    starts = ends - lengths
    steps = jnp.arange(tok_rows, dtype=jnp.int32)[:, None]
    member = (steps >= starts[None, :]) & (steps < ends[None, :])
    slot = jnp.sum(jnp.where(member, adapter_pos[None, :], 0), axis=1)
    in_slot = slot[:, None] == jnp.arange(adapter_slots, dtype=jnp.int32)[None, :]

    down_part = jnp.einsum("tn,snk->tsk", tokens, down_sent, preferred_element_type=jnp.float32)
    shrink_part = jnp.sum(jnp.where(in_slot[:, :, None], down_part, 0.0), axis=1)
    shrink = lax.psum(shrink_part, "tensor").astype(jnp.bfloat16)
    spread = jnp.where(in_slot[:, :, None], shrink[:, None, :], 0).reshape(tok_rows, adapter_slots * rank)
    pieces = [(0, 0, page)] + [(block + 1, first, end) for block, first, end in near_pieces]
    arrays = [store, *near]
    for part, (first, end) in enumerate(parts):
        pieces += [(half + block, first, end) for block in range(half)]
        arrays += [mirrored[part], *far[part]]
    prefix_pages = assemble(page_source, page_place, arrays, pieces).reshape(request_count, HITS * page, -1)

    place = starts[:, None] + jnp.arange(MOST, dtype=jnp.int32)[None, :]
    pick = (place.reshape(-1, 1) == jnp.arange(tok_rows, dtype=jnp.int32)[None, :]).astype(jnp.bfloat16)
    fresh = jnp.dot(pick, new_cache, preferred_element_type=jnp.float32).astype(jnp.bfloat16)
    fresh = fresh.reshape(request_count, MOST, -1)
    up = up_sent.reshape(adapter_slots * rank, q_cols)
    out = attend(query_base, spread, up, fresh, prefix_pages, starts, ends)
    return (out, new_cache)


def solution(mesh):
    return jax.shard_map(
        on_device,
        mesh=mesh,
        in_specs=(
            P("dp", "tensor"),
            P(None, "tensor"),
            P(None, "tensor"),
            P("dp", "tensor", None),
            P("dp", None, "tensor"),
            P("dp", None, "tensor"),
            P("dp", None),
            P("dp", None),
            P("dp"),
            P("dp", None),
            P("dp"),
        ),
        out_specs=(P("dp", "tensor"), P("dp", "tensor")),
        check_vma=False,
    )
```

```python
import functools
import math

import jax
import jax.numpy as jnp
from jax import lax
from jax.experimental import pallas as pl
from jax.experimental.pallas import tpu as pltpu
from jax.sharding import PartitionSpec as P

HEAD_WIDTH = 128
ADP_CAP = 2
HITS = 4
MOST = 128
BLOCK = 32
TOGETHER = 4
TILE = 256
VMEM_GRANT = 60 * 1024 * 1024

ADAPTER_SCALE = 0.5
NEGATIVE = -1e30


def earlier_alike(owner):
    count = owner.shape[-1]
    ahead = jnp.arange(count, dtype=jnp.int32)[None, :] < jnp.arange(count, dtype=jnp.int32)[:, None]
    alike = owner[..., None, :] == owner[..., :, None]
    return jnp.sum((alike & ahead).astype(jnp.int32), axis=-1)


def asked_of(holder, owner, order, local, capacity):
    place = jnp.arange(capacity, dtype=jnp.int32)[None, :, None]
    match = (owner[:, None, :] == holder) & (order[:, None, :] == place)
    return jnp.sum(jnp.where(match, local[:, None, :], 0), axis=2)


def attention_steps(starts, ends, total):
    first = starts // BLOCK
    count = (ends - 1) // BLOCK - first + 1
    upto = jnp.cumsum(count)
    step = jnp.minimum(jnp.arange(total, dtype=jnp.int32), upto[-1] - 1)
    request = jnp.sum((upto[None, :] <= step[:, None]).astype(jnp.int32), axis=1)
    pick = request[:, None] == jnp.arange(starts.shape[0], dtype=jnp.int32)[None, :]

    def at(values):
        return jnp.sum(jnp.where(pick, values[None, :], 0), axis=1)

    block = at(first) + step - at(upto - count)
    return jnp.stack([request, block, at(starts), at(ends)])


def attention_kernel(
    last, steps_ref, source_ref, place_ref, spread_hbm, up_any, base_hbm, fresh_hbm, pages_hbm, last_hbm, *rest
):
    out_ref, query_ref, spread_ref, up_ref, base_ref, cache_ref, sems, tile_sems = rest
    q_cols = base_ref.shape[1]
    kv_heads = cache_ref.shape[2] // (2 * HEAD_WIDTH)
    group = q_cols // HEAD_WIDTH // kv_heads
    page = pages_hbm.shape[1]
    held = HITS * page
    sharp = HEAD_WIDTH ** -0.5 * math.log2(math.e)

    def tile_copies(index):
        cols = pl.ds(pl.multiple_of(index * TILE, TILE), TILE)
        return (
            pltpu.make_async_copy(up_any.at[:, cols], up_ref.at[:, cols], tile_sems.at[0, index]),
            pltpu.make_async_copy(base_hbm.at[:, cols], base_ref.at[:, cols], tile_sems.at[1, index]),
        )

    def fetch(index, carry):
        rows = pl.ds(pl.multiple_of(index % HITS * page, page), page)
        to = cache_ref.at[index // HITS, rows]
        late = source_ref[index] == last

        @pl.when(late)
        def _():
            pltpu.make_async_copy(last_hbm.at[place_ref[index]], to, sems.at[1]).start()

        @pl.when(jnp.logical_not(late))
        def _():
            pltpu.make_async_copy(pages_hbm.at[index], to, sems.at[1]).start()

        return carry

    spread_copy = pltpu.make_async_copy(spread_hbm, spread_ref, sems.at[0])
    fresh_copy = pltpu.make_async_copy(fresh_hbm, cache_ref.at[:, held:], sems.at[2])
    spread_copy.start()
    for index in range(q_cols // TILE):
        for copy in tile_copies(index):
            copy.start()
    fresh_copy.start()
    lax.fori_loop(0, pages_hbm.shape[0], fetch, 0)
    spread_copy.wait()

    def project(index, carry):
        for copy in tile_copies(index):
            copy.wait()
        cols = pl.ds(pl.multiple_of(index * TILE, TILE), TILE)
        correction = jnp.dot(spread_ref[...], up_ref[:, cols], preferred_element_type=jnp.float32)
        query_ref[:, cols] = (base_ref[:, cols] + ADAPTER_SCALE * correction).astype(jnp.bfloat16)
        return carry

    lax.fori_loop(0, q_cols // TILE, project, 0)
    fresh_copy.wait()
    prefix = cache_ref.at[:, :held]
    pltpu.make_async_copy(prefix, prefix, sems.at[1]).wait()
    dims = (((1,), (1,)), ((), ()))
    q_at = lax.broadcasted_iota(jnp.int32, (group * BLOCK, MOST), 0) % BLOCK
    ahead = lax.broadcasted_iota(jnp.int32, (group * BLOCK, MOST), 1) - q_at
    own_at = lax.broadcasted_iota(jnp.int32, (BLOCK, HEAD_WIDTH), 0)

    def several(turn, carry):
        places = []
        for lane in range(TOGETHER):
            index = turn * TOGETHER + lane
            row = pl.multiple_of(steps_ref[1, index] * BLOCK, BLOCK)
            places.append((steps_ref[0, index], row, steps_ref[2, index], steps_ref[3, index]))
        chains = [(place, head) for place in places for head in range(kv_heads)]
        scores = []
        for (request, row, start, _), head in chains:
            at = head * 2 * HEAD_WIDTH
            wide = head * group * HEAD_WIDTH
            rows_q = jnp.concatenate(
                [
                    query_ref[pl.ds(row, BLOCK), wide + g * HEAD_WIDTH : wide + (g + 1) * HEAD_WIDTH]
                    for g in range(group)
                ],
                axis=0,
            )
            keys = cache_ref[request, :, at : at + HEAD_WIDTH]
            score = lax.dot_general(rows_q, keys, dims, preferred_element_type=jnp.float32)
            scores.append((score[:, :held], jnp.where(ahead <= row - start, score[:, held:], NEGATIVE)))
        weights = []
        for old_s, new_s in scores:
            top = jnp.maximum(
                jnp.max(old_s, axis=1, keepdims=True), jnp.max(new_s, axis=1, keepdims=True)
            )
            old_e = jnp.exp2((old_s - top) * sharp)
            new_e = jnp.exp2((new_s - top) * sharp)
            total = jnp.sum(old_e, axis=1, keepdims=True) + jnp.sum(new_e, axis=1, keepdims=True)
            weights.append((jnp.concatenate([old_e, new_e], axis=1).astype(jnp.bfloat16), total))
        results = []
        for ((request, _, _, _), head), (weight, total) in zip(chains, weights):
            at = head * 2 * HEAD_WIDTH + HEAD_WIDTH
            values = cache_ref[request, :, at : at + HEAD_WIDTH]
            summed = jnp.dot(weight, values, preferred_element_type=jnp.float32)
            results.append((summed / total).astype(jnp.bfloat16))
        for ((_, row, start, end), head), result in zip(chains, results):
            own = (own_at >= start - row) & (own_at < end - row)
            for g in range(group):
                col = (head * group + g) * HEAD_WIDTH
                cols = slice(col, col + HEAD_WIDTH)
                before = out_ref[pl.ds(row, BLOCK), cols]
                out_ref[pl.ds(row, BLOCK), cols] = jnp.where(own, result[g * BLOCK : (g + 1) * BLOCK], before)
        return carry

    lax.fori_loop(0, steps_ref.shape[1] // TOGETHER, several, 0)


def attend(query_base, spread, up, fresh, pages, last_pages, source, place, last, starts, ends):
    rows, q_cols = query_base.shape
    requests = fresh.shape[0]
    keys = HITS * pages.shape[1] + MOST
    steps_total = -(-(rows // BLOCK + requests - 1) // TOGETHER) * TOGETHER
    steps = attention_steps(starts, ends, steps_total)
    hbm = pl.BlockSpec(memory_space=pltpu.HBM)
    scalars = pl.BlockSpec(memory_space=pltpu.SMEM)
    return pl.pallas_call(
        functools.partial(attention_kernel, last),
        out_shape=jax.ShapeDtypeStruct((rows, q_cols), jnp.bfloat16),
        in_specs=[scalars] * 3 + [hbm] * 6,
        out_specs=pl.BlockSpec(memory_space=pltpu.VMEM),
        scratch_shapes=[
            pltpu.VMEM((rows, q_cols), jnp.bfloat16),
            *[pltpu.VMEM(each.shape, each.dtype) for each in (spread, up, query_base)],
            pltpu.VMEM((requests, keys, pages.shape[2]), pages.dtype),
            pltpu.SemaphoreType.DMA((3,)),
            pltpu.SemaphoreType.DMA((2, q_cols // TILE)),
        ],
        compiler_params=pltpu.CompilerParams(vmem_limit_bytes=VMEM_GRANT),
        cost_estimate=pl.CostEstimate(
            flops=4 * steps_total * BLOCK * q_cols * keys + 2 * spread.size * q_cols,
            bytes_accessed=4 * query_base.size + 2 * (2 * spread.size + up.size + fresh.size + pages.size),
            transcendentals=0,
        ),
        name="attend",
    )(steps, source, place, spread, up, query_base, fresh, pages, last_pages)


def serve_kernel(asked_ref, store_ref, *refs):
    outs, sems = refs[:-1], refs[-1]
    for index, out in enumerate(outs):
        for place in range(out.shape[0]):
            page = asked_ref[index * out.shape[0] + place]
            pltpu.make_async_copy(store_ref.at[page], out.at[place], sems.at[index]).start()
    for index, out in enumerate(outs):
        pltpu.make_async_copy(out, out, sems.at[index]).wait()


def serve(asked, store):
    blocks, capacity = asked.shape
    shape = (capacity,) + store.shape[1:]
    return pl.pallas_call(
        serve_kernel,
        out_shape=[jax.ShapeDtypeStruct(shape, store.dtype)] * blocks,
        in_specs=[pl.BlockSpec(memory_space=pltpu.SMEM), pl.BlockSpec(memory_space=pl.ANY)],
        out_specs=[pl.BlockSpec(memory_space=pltpu.VMEM)] * blocks,
        scratch_shapes=[pltpu.SemaphoreType.DMA((blocks,))],
        compiler_params=pltpu.CompilerParams(vmem_limit_bytes=VMEM_GRANT),
        cost_estimate=pl.CostEstimate(
            flops=0, bytes_accessed=4 * blocks * math.prod(shape), transcendentals=0
        ),
        name="serve",
    )(asked.reshape(-1), store)


def assemble_kernel(source_ref, place_ref, *refs):
    sources, out, sem = refs[:-2], refs[-2], refs[-1]

    def one(index, carry):
        source = source_ref[index]
        place = place_ref[index]
        for number, ref in enumerate(sources):

            @pl.when(source == number)
            def _():
                pltpu.make_async_copy(ref.at[place], out.at[index], sem).start()

        @pl.when(source == len(sources))
        def _():
            pltpu.make_async_copy(sources[0].at[0], out.at[index], sem).start()

        return carry

    lax.fori_loop(0, out.shape[0], one, 0)
    pltpu.make_async_copy(out, out, sem).wait()


def assemble(source, place, sources):
    scalars = pl.BlockSpec(memory_space=pltpu.SMEM)
    shape = (source.shape[0],) + sources[0].shape[1:]
    return pl.pallas_call(
        assemble_kernel,
        out_shape=jax.ShapeDtypeStruct(shape, sources[0].dtype),
        in_specs=[scalars, scalars] + [pl.BlockSpec(memory_space=pltpu.HBM)] * len(sources),
        out_specs=pl.BlockSpec(memory_space=pltpu.VMEM),
        scratch_shapes=[pltpu.SemaphoreType.DMA],
        compiler_params=pltpu.CompilerParams(vmem_limit_bytes=VMEM_GRANT),
        cost_estimate=pl.CostEstimate(flops=0, bytes_accessed=4 * math.prod(shape), transcendentals=0),
        name="assemble",
    )(source, place, *sources)


def on_device(
    tokens,
    query_weight,
    keyvalue_weight,
    adapter_down_weight,
    adapter_up_weight,
    keyvalue_page_store,
    span_token_length,
    adapter_owner,
    adapter_local_index,
    page_owner,
    page_local_index,
):
    peers = lax.axis_size("dp")
    half = peers // 2
    me = lax.axis_index("dp")
    tok_rows = tokens.shape[0]
    q_cols = query_weight.shape[1]
    rank = adapter_down_weight.shape[2]
    adapter_slots = peers * ADP_CAP

    def swap(array, distance):
        return lax.ppermute(array, "dp", [(peer, peer ^ distance) for peer in range(peers)])

    page_count = page_local_index.shape[0]
    request_count = adapter_local_index.shape[0]
    raw = jnp.concatenate([page_owner[:, 0], page_local_index, adapter_owner[:, 0], adapter_local_index])
    everyone = lax.all_to_all(
        jnp.broadcast_to(raw[None], (peers, raw.shape[0])), "dp", split_axis=0, concat_axis=0, tiled=True
    )
    store, down_store, everyone = lax.optimization_barrier((keyvalue_page_store, adapter_down_weight, everyone))
    mirrored_store = swap(store, half)

    page_cap = max(2, 2 * page_count // peers)
    group = everyone[jnp.arange(half, dtype=jnp.int32) ^ me]
    group_owner = group[:, :page_count]
    group_local = group[:, page_count : 2 * page_count]
    group_order = earlier_alike(group_owner)
    near_asked = asked_of(me, group_owner, group_order, group_local, page_cap)
    far_asked = asked_of(me ^ half, group_owner, group_order, group_local, page_cap)
    all_owner = everyone[:, 2 * page_count : 2 * page_count + request_count]
    all_local = everyone[:, 2 * page_count + request_count :]
    adapter_asked = asked_of(me, all_owner, earlier_alike(all_owner), all_local, ADP_CAP).reshape(-1)
    adapter_pos = adapter_owner[:, 0] * ADP_CAP + earlier_alike(adapter_owner[:, 0])
    page_source = page_owner[:, 0] ^ me
    page_place = jnp.where(page_source % half == 0, page_local_index, earlier_alike(page_owner[:, 0]))

    near = [swap(pages, i + 1) for i, pages in enumerate(serve(near_asked[1:], store))]
    down_rows = down_store[adapter_asked]
    up_rows = adapter_up_weight[adapter_asked]

    piece = lax.all_gather(tokens, "tensor", axis=1, tiled=True)
    query_base = jnp.dot(piece, query_weight, preferred_element_type=jnp.float32)
    new_cache = jnp.dot(piece, keyvalue_weight, preferred_element_type=jnp.float32).astype(jnp.bfloat16)

    down_rows, mirrored_store, query_base, new_cache, near = lax.optimization_barrier(
        (down_rows, mirrored_store, query_base, new_cache, near)
    )
    down_sent = lax.all_to_all(down_rows, "dp", split_axis=0, concat_axis=0, tiled=True)
    far = list(serve(far_asked[1:], mirrored_store))
    far = [swap(pages, i + 1) for i, pages in enumerate(far[:-1])] + far[-1:]
    up_rows, down_sent, far = lax.optimization_barrier((up_rows, down_sent, far))
    up_sent = lax.all_to_all(up_rows, "dp", split_axis=0, concat_axis=0, tiled=True)
    far[-1] = swap(far[-1], half - 1)

    lengths = span_token_length[0]
    ends = jnp.cumsum(lengths)
    starts = ends - lengths
    steps = jnp.arange(tok_rows, dtype=jnp.int32)[:, None]
    member = (steps >= starts[None, :]) & (steps < ends[None, :])
    slot = jnp.sum(jnp.where(member, adapter_pos[None, :], 0), axis=1)
    in_slot = slot[:, None] == jnp.arange(adapter_slots, dtype=jnp.int32)[None, :]

    down_part = jnp.einsum("tn,snk->tsk", tokens, down_sent, preferred_element_type=jnp.float32)
    shrink_part = jnp.sum(jnp.where(in_slot[:, :, None], down_part, 0.0), axis=1)
    shrink = lax.psum(shrink_part, "tensor").astype(jnp.bfloat16)
    spread = jnp.where(in_slot[:, :, None], shrink[:, None, :], 0).reshape(tok_rows, adapter_slots * rank)
    prefix_pages = assemble(page_source, page_place, [store, *near, mirrored_store, *far[:-1]])

    taken = starts[:, None] + jnp.arange(MOST, dtype=jnp.int32)[None, :]
    pick = (taken.reshape(-1, 1) == jnp.arange(tok_rows, dtype=jnp.int32)[None, :]).astype(jnp.bfloat16)
    fresh = jnp.dot(pick, new_cache, preferred_element_type=jnp.float32).astype(jnp.bfloat16)
    fresh = fresh.reshape(request_count, MOST, -1)
    up = up_sent.reshape(adapter_slots * rank, q_cols)
    out = attend(
        query_base, spread, up, fresh, prefix_pages, far[-1], page_source, page_place, peers - 1, starts, ends
    )
    return (out, new_cache)


def solution(mesh):
    return jax.shard_map(
        on_device,
        mesh=mesh,
        in_specs=(
            P("dp", "tensor"),
            P(None, "tensor"),
            P(None, "tensor"),
            P("dp", "tensor", None),
            P("dp", None, "tensor"),
            P("dp", None, "tensor"),
            P("dp", None),
            P("dp", None),
            P("dp"),
            P("dp", None),
            P("dp"),
        ),
        out_specs=(P("dp", "tensor"), P("dp", "tensor")),
        check_vma=False,
    )
```

```python
import functools
import math

import jax
import jax.numpy as jnp
from jax import lax
from jax.experimental import pallas as pl
from jax.experimental.pallas import tpu as pltpu
from jax.sharding import PartitionSpec as P

HEAD_WIDTH = 128
ADP_CAP = 2
HITS = 4
MOST = 128
BLOCK = 32
TOGETHER = 4
TILE = 256
VMEM_GRANT = 60 * 1024 * 1024
SMALL_GRANT = 16 * 1024 * 1024

ADAPTER_SCALE = 0.5
NEGATIVE = -1e30


def earlier_alike(owner):
    count = owner.shape[-1]
    ahead = jnp.arange(count, dtype=jnp.int32)[None, :] < jnp.arange(count, dtype=jnp.int32)[:, None]
    alike = owner[..., None, :] == owner[..., :, None]
    return jnp.sum((alike & ahead).astype(jnp.int32), axis=-1)


def asked_of(holder, owner, order, local, capacity):
    place = jnp.arange(capacity, dtype=jnp.int32)[None, :, None]
    match = (owner[:, None, :] == holder) & (order[:, None, :] == place)
    return jnp.sum(jnp.where(match, local[:, None, :], 0), axis=2)


def attention_steps(starts, ends, total):
    first = starts // BLOCK
    count = (ends - 1) // BLOCK - first + 1
    upto = jnp.cumsum(count)
    step = jnp.minimum(jnp.arange(total, dtype=jnp.int32), upto[-1] - 1)
    request = jnp.sum((upto[None, :] <= step[:, None]).astype(jnp.int32), axis=1)
    pick = request[:, None] == jnp.arange(starts.shape[0], dtype=jnp.int32)[None, :]

    def at(values):
        return jnp.sum(jnp.where(pick, values[None, :], 0), axis=1)

    block = at(first) + step - at(upto - count)
    return jnp.stack([request, block, at(starts), at(ends)])


def attention_kernel(
    last, steps_ref, source_ref, place_ref, spread_hbm, up_any, base_hbm, fresh_hbm, pages_hbm, last_hbm, *rest
):
    out_ref, query_ref, spread_ref, up_ref, base_ref, cache_ref, sems, tile_sems = rest
    q_cols = base_ref.shape[1]
    kv_heads = cache_ref.shape[2] // (2 * HEAD_WIDTH)
    group = q_cols // HEAD_WIDTH // kv_heads
    page = pages_hbm.shape[1]
    held = HITS * page
    sharp = HEAD_WIDTH ** -0.5 * math.log2(math.e)

    def tile_copies(index):
        cols = pl.ds(pl.multiple_of(index * TILE, TILE), TILE)
        return (
            pltpu.make_async_copy(up_any.at[:, cols], up_ref.at[:, cols], tile_sems.at[0, index]),
            pltpu.make_async_copy(base_hbm.at[:, cols], base_ref.at[:, cols], tile_sems.at[1, index]),
        )

    def fetch(index, carry):
        rows = pl.ds(pl.multiple_of(index % HITS * page, page), page)
        to = cache_ref.at[index // HITS, rows]
        late = source_ref[index] == last

        @pl.when(late)
        def _():
            pltpu.make_async_copy(last_hbm.at[place_ref[index]], to, sems.at[1]).start()

        @pl.when(jnp.logical_not(late))
        def _():
            pltpu.make_async_copy(pages_hbm.at[index], to, sems.at[1]).start()

        return carry

    spread_copy = pltpu.make_async_copy(spread_hbm, spread_ref, sems.at[0])
    fresh_copy = pltpu.make_async_copy(fresh_hbm, cache_ref.at[:, held:], sems.at[2])
    spread_copy.start()
    for index in range(q_cols // TILE):
        for copy in tile_copies(index):
            copy.start()
    fresh_copy.start()
    lax.fori_loop(0, pages_hbm.shape[0], fetch, 0)
    spread_copy.wait()

    def project(index, carry):
        for copy in tile_copies(index):
            copy.wait()
        cols = pl.ds(pl.multiple_of(index * TILE, TILE), TILE)
        correction = jnp.dot(spread_ref[...], up_ref[:, cols], preferred_element_type=jnp.float32)
        query_ref[:, cols] = (base_ref[:, cols] + ADAPTER_SCALE * correction).astype(jnp.bfloat16)
        return carry

    lax.fori_loop(0, q_cols // TILE, project, 0)
    fresh_copy.wait()
    prefix = cache_ref.at[:, :held]
    pltpu.make_async_copy(prefix, prefix, sems.at[1]).wait()
    dims = (((1,), (1,)), ((), ()))
    tall = group * BLOCK
    q_at = lax.broadcasted_iota(jnp.int32, (kv_heads * tall, MOST), 0) % BLOCK
    ahead = lax.broadcasted_iota(jnp.int32, (kv_heads * tall, MOST), 1) - q_at
    own_at = lax.broadcasted_iota(jnp.int32, (BLOCK, HEAD_WIDTH), 0)
    blank = jnp.zeros((tall, HEAD_WIDTH), jnp.bfloat16)

    def side_by_side(request, offset):
        columns = [(2 * head + offset) * HEAD_WIDTH for head in range(kv_heads)]
        return jnp.concatenate([cache_ref[request, :, col : col + HEAD_WIDTH] for col in columns], axis=1)

    def queries(row):
        heads = []
        for head in range(kv_heads):
            columns = [(head * group + g) * HEAD_WIDTH for g in range(group)]
            own = jnp.concatenate([query_ref[pl.ds(row, BLOCK), col : col + HEAD_WIDTH] for col in columns], axis=0)
            heads.append(jnp.concatenate([own if other == head else blank for other in range(kv_heads)], axis=1))
        return jnp.concatenate(heads, axis=0)

    def several(turn, carry):
        places = []
        for lane in range(TOGETHER):
            index = turn * TOGETHER + lane
            row = pl.multiple_of(steps_ref[1, index] * BLOCK, BLOCK)
            places.append((steps_ref[0, index], row, steps_ref[2, index], steps_ref[3, index]))
        scores = []
        for request, row, start, _ in places:
            score = lax.dot_general(queries(row), side_by_side(request, 0), dims, preferred_element_type=jnp.float32)
            scores.append((score[:, :held], jnp.where(ahead <= row - start, score[:, held:], NEGATIVE)))
        weights = []
        for old_s, new_s in scores:
            top = jnp.maximum(
                jnp.max(old_s, axis=1, keepdims=True), jnp.max(new_s, axis=1, keepdims=True)
            )
            old_e = jnp.exp2((old_s - top) * sharp)
            new_e = jnp.exp2((new_s - top) * sharp)
            total = jnp.sum(old_e, axis=1, keepdims=True) + jnp.sum(new_e, axis=1, keepdims=True)
            weights.append((jnp.concatenate([old_e, new_e], axis=1).astype(jnp.bfloat16), total))
        results = []
        for (request, _, _, _), (weight, total) in zip(places, weights):
            summed = jnp.dot(weight, side_by_side(request, 1), preferred_element_type=jnp.float32)
            results.append((summed, total))
        for (_, row, start, end), (summed, total) in zip(places, results):
            own = (own_at >= start - row) & (own_at < end - row)
            for head in range(kv_heads):
                rows = slice(head * tall, (head + 1) * tall)
                result = summed[rows, head * HEAD_WIDTH : (head + 1) * HEAD_WIDTH] / total[rows]
                result = result.astype(jnp.bfloat16)
                for g in range(group):
                    col = (head * group + g) * HEAD_WIDTH
                    cols = slice(col, col + HEAD_WIDTH)
                    before = out_ref[pl.ds(row, BLOCK), cols]
                    out_ref[pl.ds(row, BLOCK), cols] = jnp.where(own, result[g * BLOCK : (g + 1) * BLOCK], before)
        return carry

    lax.fori_loop(0, steps_ref.shape[1] // TOGETHER, several, 0)


def attend(query_base, spread, up, fresh, pages, last_pages, source, place, last, starts, ends):
    rows, q_cols = query_base.shape
    requests = fresh.shape[0]
    keys = HITS * pages.shape[1] + MOST
    steps_total = -(-(rows // BLOCK + requests - 1) // TOGETHER) * TOGETHER
    steps = attention_steps(starts, ends, steps_total)
    hbm = pl.BlockSpec(memory_space=pltpu.HBM)
    scalars = pl.BlockSpec(memory_space=pltpu.SMEM)
    return pl.pallas_call(
        functools.partial(attention_kernel, last),
        out_shape=jax.ShapeDtypeStruct((rows, q_cols), jnp.bfloat16),
        in_specs=[scalars] * 3 + [hbm] * 6,
        out_specs=pl.BlockSpec(memory_space=pltpu.VMEM),
        scratch_shapes=[
            pltpu.VMEM((rows, q_cols), jnp.bfloat16),
            *[pltpu.VMEM(each.shape, each.dtype) for each in (spread, up, query_base)],
            pltpu.VMEM((requests, keys, pages.shape[2]), pages.dtype),
            pltpu.SemaphoreType.DMA((3,)),
            pltpu.SemaphoreType.DMA((2, q_cols // TILE)),
        ],
        compiler_params=pltpu.CompilerParams(vmem_limit_bytes=VMEM_GRANT),
        cost_estimate=pl.CostEstimate(
            flops=4 * steps_total * BLOCK * q_cols * keys + 2 * spread.size * q_cols,
            bytes_accessed=4 * query_base.size + 2 * (2 * spread.size + up.size + fresh.size + pages.size),
            transcendentals=0,
        ),
        name="attend",
    )(steps, source, place, spread, up, query_base, fresh, pages, last_pages)


def serve_kernel(asked_ref, store_ref, *refs):
    outs, sems = refs[:-1], refs[-1]
    for index, out in enumerate(outs):
        for place in range(out.shape[0]):
            page = asked_ref[index * out.shape[0] + place]
            pltpu.make_async_copy(store_ref.at[page], out.at[place], sems.at[index]).start()
    for index, out in enumerate(outs):
        pltpu.make_async_copy(out, out, sems.at[index]).wait()


def serve(asked, store, grant):
    blocks, capacity = asked.shape
    shape = (capacity,) + store.shape[1:]
    return pl.pallas_call(
        serve_kernel,
        out_shape=[jax.ShapeDtypeStruct(shape, store.dtype)] * blocks,
        in_specs=[pl.BlockSpec(memory_space=pltpu.SMEM), pl.BlockSpec(memory_space=pl.ANY)],
        out_specs=[pl.BlockSpec(memory_space=pltpu.VMEM)] * blocks,
        scratch_shapes=[pltpu.SemaphoreType.DMA((blocks,))],
        compiler_params=pltpu.CompilerParams(vmem_limit_bytes=grant),
        cost_estimate=pl.CostEstimate(
            flops=0, bytes_accessed=4 * blocks * math.prod(shape), transcendentals=0
        ),
        name="serve",
    )(asked.reshape(-1), store)


def assemble_kernel(source_ref, place_ref, *refs):
    sources, out, sem = refs[:-2], refs[-2], refs[-1]

    def one(index, carry):
        source = source_ref[index]
        place = place_ref[index]
        for number, ref in enumerate(sources):

            @pl.when(source == number)
            def _():
                pltpu.make_async_copy(ref.at[place], out.at[index], sem).start()

        @pl.when(source == len(sources))
        def _():
            pltpu.make_async_copy(sources[0].at[0], out.at[index], sem).start()

        return carry

    lax.fori_loop(0, out.shape[0], one, 0)
    pltpu.make_async_copy(out, out, sem).wait()


def assemble(source, place, sources):
    scalars = pl.BlockSpec(memory_space=pltpu.SMEM)
    shape = (source.shape[0],) + sources[0].shape[1:]
    return pl.pallas_call(
        assemble_kernel,
        out_shape=jax.ShapeDtypeStruct(shape, sources[0].dtype),
        in_specs=[scalars, scalars] + [pl.BlockSpec(memory_space=pltpu.HBM)] * len(sources),
        out_specs=pl.BlockSpec(memory_space=pltpu.VMEM),
        scratch_shapes=[pltpu.SemaphoreType.DMA],
        compiler_params=pltpu.CompilerParams(vmem_limit_bytes=VMEM_GRANT),
        cost_estimate=pl.CostEstimate(flops=0, bytes_accessed=4 * math.prod(shape), transcendentals=0),
        name="assemble",
    )(source, place, *sources)


def on_device(
    tokens,
    query_weight,
    keyvalue_weight,
    adapter_down_weight,
    adapter_up_weight,
    keyvalue_page_store,
    span_token_length,
    adapter_owner,
    adapter_local_index,
    page_owner,
    page_local_index,
):
    peers = lax.axis_size("dp")
    half = peers // 2
    me = lax.axis_index("dp")
    tok_rows = tokens.shape[0]
    q_cols = query_weight.shape[1]
    rank = adapter_down_weight.shape[2]
    adapter_slots = peers * ADP_CAP

    def swap(array, distance):
        return lax.ppermute(array, "dp", [(peer, peer ^ distance) for peer in range(peers)])

    page_count = page_local_index.shape[0]
    request_count = adapter_local_index.shape[0]
    raw = jnp.concatenate([page_owner[:, 0], page_local_index, adapter_owner[:, 0], adapter_local_index])
    everyone = lax.all_to_all(
        jnp.broadcast_to(raw[None], (peers, raw.shape[0])), "dp", split_axis=0, concat_axis=0, tiled=True
    )
    store, down_store, everyone = lax.optimization_barrier((keyvalue_page_store, adapter_down_weight, everyone))
    mirrored_store = swap(store, half)

    page_cap = max(2, 2 * page_count // peers)
    group = everyone[jnp.arange(half, dtype=jnp.int32) ^ me]
    group_owner = group[:, :page_count]
    group_local = group[:, page_count : 2 * page_count]
    group_order = earlier_alike(group_owner)
    near_asked = asked_of(me, group_owner, group_order, group_local, page_cap)
    far_asked = asked_of(me ^ half, group_owner, group_order, group_local, page_cap)
    all_owner = everyone[:, 2 * page_count : 2 * page_count + request_count]
    all_local = everyone[:, 2 * page_count + request_count :]
    adapter_asked = asked_of(me, all_owner, earlier_alike(all_owner), all_local, ADP_CAP).reshape(-1)
    adapter_pos = adapter_owner[:, 0] * ADP_CAP + earlier_alike(adapter_owner[:, 0])
    page_source = page_owner[:, 0] ^ me
    page_place = jnp.where(page_source % half == 0, page_local_index, earlier_alike(page_owner[:, 0]))

    near = [swap(pages, i + 1) for i, pages in enumerate(serve(near_asked[1:], store, VMEM_GRANT))]
    down_rows = down_store[adapter_asked]
    up_rows = adapter_up_weight[adapter_asked]

    piece = lax.all_gather(tokens, "tensor", axis=1, tiled=True)
    query_base = jnp.dot(piece, query_weight, preferred_element_type=jnp.float32)
    new_cache = jnp.dot(piece, keyvalue_weight, preferred_element_type=jnp.float32).astype(jnp.bfloat16)

    down_rows, mirrored_store, query_base, new_cache, near = lax.optimization_barrier(
        (down_rows, mirrored_store, query_base, new_cache, near)
    )
    down_sent = lax.all_to_all(down_rows, "dp", split_axis=0, concat_axis=0, tiled=True)
    far = list(serve(far_asked[1:], mirrored_store, SMALL_GRANT))
    far = [swap(pages, i + 1) for i, pages in enumerate(far[:-1])] + far[-1:]
    up_rows, down_sent, far = lax.optimization_barrier((up_rows, down_sent, far))
    up_sent = lax.all_to_all(up_rows, "dp", split_axis=0, concat_axis=0, tiled=True)
    far[-1] = swap(far[-1], half - 1)

    lengths = span_token_length[0]
    ends = jnp.cumsum(lengths)
    starts = ends - lengths
    steps = jnp.arange(tok_rows, dtype=jnp.int32)[:, None]
    member = (steps >= starts[None, :]) & (steps < ends[None, :])
    slot = jnp.sum(jnp.where(member, adapter_pos[None, :], 0), axis=1)
    in_slot = slot[:, None] == jnp.arange(adapter_slots, dtype=jnp.int32)[None, :]

    down_part = jnp.einsum("tn,snk->tsk", tokens, down_sent, preferred_element_type=jnp.float32)
    shrink_part = jnp.sum(jnp.where(in_slot[:, :, None], down_part, 0.0), axis=1)
    shrink = lax.psum(shrink_part, "tensor").astype(jnp.bfloat16)
    spread = jnp.where(in_slot[:, :, None], shrink[:, None, :], 0).reshape(tok_rows, adapter_slots * rank)
    prefix_pages = assemble(page_source, page_place, [store, *near, mirrored_store, *far[:-1]])

    taken = starts[:, None] + jnp.arange(MOST, dtype=jnp.int32)[None, :]
    pick = (taken.reshape(-1, 1) == jnp.arange(tok_rows, dtype=jnp.int32)[None, :]).astype(jnp.bfloat16)
    fresh = jnp.dot(pick, new_cache, preferred_element_type=jnp.float32).astype(jnp.bfloat16)
    fresh = fresh.reshape(request_count, MOST, -1)
    up = up_sent.reshape(adapter_slots * rank, q_cols)
    out = attend(
        query_base, spread, up, fresh, prefix_pages, far[-1], page_source, page_place, peers - 1, starts, ends
    )
    return (out, new_cache)


def solution(mesh):
    return jax.shard_map(
        on_device,
        mesh=mesh,
        in_specs=(
            P("dp", "tensor"),
            P(None, "tensor"),
            P(None, "tensor"),
            P("dp", "tensor", None),
            P("dp", None, "tensor"),
            P("dp", None, "tensor"),
            P("dp", None),
            P("dp", None),
            P("dp"),
            P("dp", None),
            P("dp"),
        ),
        out_specs=(P("dp", "tensor"), P("dp", "tensor")),
        check_vma=False,
    )
```

```python
import functools
import math

import jax
import jax.numpy as jnp
from jax import lax
from jax.experimental import pallas as pl
from jax.experimental.pallas import tpu as pltpu
from jax.sharding import PartitionSpec as P

HEAD_WIDTH = 128
ADP_CAP = 2
HITS = 4
MOST = 128
BLOCK = 32
TOGETHER = 4
TILE = 256
VMEM_GRANT = 60 * 1024 * 1024
SMALL_GRANT = 16 * 1024 * 1024

ADAPTER_SCALE = 0.5
NEGATIVE = -1e30


def earlier_alike(owner):
    count = owner.shape[-1]
    ahead = jnp.arange(count, dtype=jnp.int32)[None, :] < jnp.arange(count, dtype=jnp.int32)[:, None]
    alike = owner[..., None, :] == owner[..., :, None]
    return jnp.sum((alike & ahead).astype(jnp.int32), axis=-1)


def asked_of(holder, owner, order, local, capacity):
    place = jnp.arange(capacity, dtype=jnp.int32)[None, :, None]
    match = (owner[:, None, :] == holder) & (order[:, None, :] == place)
    return jnp.sum(jnp.where(match, local[:, None, :], 0), axis=2)


def attention_steps(starts, ends, total):
    first = starts // BLOCK
    count = (ends - 1) // BLOCK - first + 1
    upto = jnp.cumsum(count)
    step = jnp.minimum(jnp.arange(total, dtype=jnp.int32), upto[-1] - 1)
    request = jnp.sum((upto[None, :] <= step[:, None]).astype(jnp.int32), axis=1)
    pick = request[:, None] == jnp.arange(starts.shape[0], dtype=jnp.int32)[None, :]

    def at(values):
        return jnp.sum(jnp.where(pick, values[None, :], 0), axis=1)

    block = at(first) + step - at(upto - count)
    return jnp.stack([request, block, at(starts), at(ends)])


def attention_kernel(
    last, steps_ref, source_ref, place_ref, spread_hbm, up_any, base_hbm, fresh_hbm, pages_hbm, last_hbm, *rest
):
    out_ref, query_ref, spread_ref, up_ref, base_ref, cache_ref, sems, tile_sems = rest
    q_cols = base_ref.shape[1]
    kv_heads = cache_ref.shape[2] // (2 * HEAD_WIDTH)
    group = q_cols // HEAD_WIDTH // kv_heads
    page = pages_hbm.shape[1]
    held = HITS * page
    sharp = HEAD_WIDTH ** -0.5 * math.log2(math.e)

    def tile_copies(index):
        cols = pl.ds(pl.multiple_of(index * TILE, TILE), TILE)
        return (
            pltpu.make_async_copy(up_any.at[:, cols], up_ref.at[:, cols], tile_sems.at[0, index]),
            pltpu.make_async_copy(base_hbm.at[:, cols], base_ref.at[:, cols], tile_sems.at[1, index]),
        )

    def fetch(index, carry):
        rows = pl.ds(pl.multiple_of(index % HITS * page, page), page)
        to = cache_ref.at[index // HITS, rows]
        late = source_ref[index] == last

        @pl.when(late)
        def _():
            pltpu.make_async_copy(last_hbm.at[place_ref[index]], to, sems.at[1]).start()

        @pl.when(jnp.logical_not(late))
        def _():
            pltpu.make_async_copy(pages_hbm.at[index], to, sems.at[1]).start()

        return carry

    spread_copy = pltpu.make_async_copy(spread_hbm, spread_ref, sems.at[0])
    fresh_copy = pltpu.make_async_copy(fresh_hbm, cache_ref.at[:, held:], sems.at[2])
    spread_copy.start()
    for index in range(q_cols // TILE):
        for copy in tile_copies(index):
            copy.start()
    fresh_copy.start()
    lax.fori_loop(0, pages_hbm.shape[0], fetch, 0)
    spread_copy.wait()

    def project(index, carry):
        for copy in tile_copies(index):
            copy.wait()
        cols = pl.ds(pl.multiple_of(index * TILE, TILE), TILE)
        correction = jnp.dot(spread_ref[...], up_ref[:, cols], preferred_element_type=jnp.float32)
        query_ref[:, cols] = (base_ref[:, cols] + ADAPTER_SCALE * correction).astype(jnp.bfloat16)
        return carry

    lax.fori_loop(0, q_cols // TILE, project, 0)
    fresh_copy.wait()
    prefix = cache_ref.at[:, :held]
    pltpu.make_async_copy(prefix, prefix, sems.at[1]).wait()
    dims = (((1,), (1,)), ((), ()))
    tall = group * BLOCK
    q_at = lax.broadcasted_iota(jnp.int32, (kv_heads * tall, MOST), 0) % BLOCK
    ahead = lax.broadcasted_iota(jnp.int32, (kv_heads * tall, MOST), 1) - q_at
    own_at = lax.broadcasted_iota(jnp.int32, (BLOCK, HEAD_WIDTH), 0)
    blank = jnp.zeros((tall, HEAD_WIDTH), jnp.bfloat16)

    def side_by_side(request, offset):
        columns = [(2 * head + offset) * HEAD_WIDTH for head in range(kv_heads)]
        return jnp.concatenate([cache_ref[request, :, col : col + HEAD_WIDTH] for col in columns], axis=1)

    def queries(row):
        heads = []
        for head in range(kv_heads):
            columns = [(head * group + g) * HEAD_WIDTH for g in range(group)]
            own = jnp.concatenate([query_ref[pl.ds(row, BLOCK), col : col + HEAD_WIDTH] for col in columns], axis=0)
            heads.append(jnp.concatenate([own if other == head else blank for other in range(kv_heads)], axis=1))
        return jnp.concatenate(heads, axis=0)

    def several(turn, carry):
        places = []
        for lane in range(TOGETHER):
            index = turn * TOGETHER + lane
            row = pl.multiple_of(steps_ref[1, index] * BLOCK, BLOCK)
            places.append((steps_ref[0, index], row, steps_ref[2, index], steps_ref[3, index]))
        scores = []
        for request, row, start, _ in places:
            score = lax.dot_general(queries(row), side_by_side(request, 0), dims, preferred_element_type=jnp.float32)
            scores.append((score[:, :held], jnp.where(ahead <= row - start, score[:, held:], NEGATIVE)))
        weights = []
        for old_s, new_s in scores:
            top = jnp.maximum(
                jnp.max(old_s, axis=1, keepdims=True), jnp.max(new_s, axis=1, keepdims=True)
            )
            old_e = jnp.exp2((old_s - top) * sharp)
            new_e = jnp.exp2((new_s - top) * sharp)
            total = jnp.sum(old_e, axis=1, keepdims=True) + jnp.sum(new_e, axis=1, keepdims=True)
            weights.append((jnp.concatenate([old_e, new_e], axis=1).astype(jnp.bfloat16), total))
        results = []
        for (request, _, _, _), (weight, total) in zip(places, weights):
            summed = jnp.dot(weight, side_by_side(request, 1), preferred_element_type=jnp.float32)
            results.append((summed, total))
        for (_, row, start, end), (summed, total) in zip(places, results):
            own = (own_at >= start - row) & (own_at < end - row)
            for head in range(kv_heads):
                rows = slice(head * tall, (head + 1) * tall)
                result = summed[rows, head * HEAD_WIDTH : (head + 1) * HEAD_WIDTH] / total[rows]
                result = result.astype(jnp.bfloat16)
                for g in range(group):
                    col = (head * group + g) * HEAD_WIDTH
                    cols = slice(col, col + HEAD_WIDTH)
                    before = out_ref[pl.ds(row, BLOCK), cols]
                    out_ref[pl.ds(row, BLOCK), cols] = jnp.where(own, result[g * BLOCK : (g + 1) * BLOCK], before)
        return carry

    lax.fori_loop(0, steps_ref.shape[1] // TOGETHER, several, 0)


def attend(query_base, spread, up, fresh, pages, last_pages, source, place, last, starts, ends):
    rows, q_cols = query_base.shape
    requests = fresh.shape[0]
    keys = HITS * pages.shape[1] + MOST
    steps_total = -(-(rows // BLOCK + requests - 1) // TOGETHER) * TOGETHER
    steps = attention_steps(starts, ends, steps_total)
    hbm = pl.BlockSpec(memory_space=pltpu.HBM)
    scalars = pl.BlockSpec(memory_space=pltpu.SMEM)
    return pl.pallas_call(
        functools.partial(attention_kernel, last),
        out_shape=jax.ShapeDtypeStruct((rows, q_cols), jnp.bfloat16),
        in_specs=[scalars] * 3 + [hbm] * 6,
        out_specs=pl.BlockSpec(memory_space=pltpu.VMEM),
        scratch_shapes=[
            pltpu.VMEM((rows, q_cols), jnp.bfloat16),
            *[pltpu.VMEM(each.shape, each.dtype) for each in (spread, up, query_base)],
            pltpu.VMEM((requests, keys, pages.shape[2]), pages.dtype),
            pltpu.SemaphoreType.DMA((3,)),
            pltpu.SemaphoreType.DMA((2, q_cols // TILE)),
        ],
        compiler_params=pltpu.CompilerParams(vmem_limit_bytes=VMEM_GRANT),
        cost_estimate=pl.CostEstimate(
            flops=4 * steps_total * BLOCK * q_cols * keys + 2 * spread.size * q_cols,
            bytes_accessed=4 * query_base.size + 2 * (2 * spread.size + up.size + fresh.size + pages.size),
            transcendentals=0,
        ),
        name="attend",
    )(steps, source, place, spread, up, query_base, fresh, pages, last_pages)


def serve_kernel(asked_ref, store_ref, *refs):
    outs, sems = refs[:-1], refs[-1]
    for index, out in enumerate(outs):
        for place in range(out.shape[0]):
            page = asked_ref[index * out.shape[0] + place]
            pltpu.make_async_copy(store_ref.at[page], out.at[place], sems.at[index]).start()
    for index, out in enumerate(outs):
        pltpu.make_async_copy(out, out, sems.at[index]).wait()


def serve(asked, store, grant):
    blocks, capacity = asked.shape
    shape = (capacity,) + store.shape[1:]
    return pl.pallas_call(
        serve_kernel,
        out_shape=[jax.ShapeDtypeStruct(shape, store.dtype)] * blocks,
        in_specs=[pl.BlockSpec(memory_space=pltpu.SMEM), pl.BlockSpec(memory_space=pl.ANY)],
        out_specs=[pl.BlockSpec(memory_space=pltpu.VMEM)] * blocks,
        scratch_shapes=[pltpu.SemaphoreType.DMA((blocks,))],
        compiler_params=pltpu.CompilerParams(vmem_limit_bytes=grant),
        cost_estimate=pl.CostEstimate(
            flops=0, bytes_accessed=4 * blocks * math.prod(shape), transcendentals=0
        ),
        name="serve",
    )(asked.reshape(-1), store)


def serve_both_kernel(asked_ref, adapters_ref, store_ref, down_ref, *refs):
    outs, sems = refs[:-1], refs[-1]
    columns = store_ref.shape[2]
    cuts = down_ref.shape[2] // columns
    pages = outs[0].shape[0] - ADP_CAP * cuts
    for index, out in enumerate(outs):
        for place in range(pages):
            page = asked_ref[index * pages + place]
            pltpu.make_async_copy(store_ref.at[page], out.at[place], sems.at[index]).start()
        for number in range(ADP_CAP):
            factor = down_ref.at[adapters_ref[index * ADP_CAP + number]]
            for cut in range(cuts):
                cols = factor.at[:, cut * columns : (cut + 1) * columns]
                pltpu.make_async_copy(cols, out.at[pages + number * cuts + cut], sems.at[index]).start()
    for index, out in enumerate(outs):
        pltpu.make_async_copy(out, out, sems.at[index]).wait()


def serve_both(asked, adapters, store, down):
    blocks, capacity = asked.shape
    shape = (capacity + ADP_CAP * (down.shape[2] // store.shape[2]),) + store.shape[1:]
    scalars = pl.BlockSpec(memory_space=pltpu.SMEM)
    return pl.pallas_call(
        serve_both_kernel,
        out_shape=[jax.ShapeDtypeStruct(shape, store.dtype)] * blocks,
        in_specs=[scalars, scalars, pl.BlockSpec(memory_space=pltpu.HBM), pl.BlockSpec(memory_space=pltpu.HBM)],
        out_specs=[pl.BlockSpec(memory_space=pltpu.VMEM)] * blocks,
        scratch_shapes=[pltpu.SemaphoreType.DMA((blocks,))],
        compiler_params=pltpu.CompilerParams(vmem_limit_bytes=VMEM_GRANT),
        cost_estimate=pl.CostEstimate(
            flops=0, bytes_accessed=4 * blocks * math.prod(shape), transcendentals=0
        ),
        name="serve_both",
    )(asked.reshape(-1), adapters.reshape(-1), store, down)


def assemble_kernel(source_ref, place_ref, *refs):
    sources, out, sem = refs[:-2], refs[-2], refs[-1]

    def one(index, carry):
        source = source_ref[index]
        place = place_ref[index]
        for number, ref in enumerate(sources):

            @pl.when(source == number)
            def _():
                pltpu.make_async_copy(ref.at[place], out.at[index], sem).start()

        @pl.when(source == len(sources))
        def _():
            pltpu.make_async_copy(sources[0].at[0], out.at[index], sem).start()

        return carry

    lax.fori_loop(0, out.shape[0], one, 0)
    pltpu.make_async_copy(out, out, sem).wait()


def assemble(source, place, sources):
    scalars = pl.BlockSpec(memory_space=pltpu.SMEM)
    shape = (source.shape[0],) + sources[0].shape[1:]
    return pl.pallas_call(
        assemble_kernel,
        out_shape=jax.ShapeDtypeStruct(shape, sources[0].dtype),
        in_specs=[scalars, scalars] + [pl.BlockSpec(memory_space=pltpu.HBM)] * len(sources),
        out_specs=pl.BlockSpec(memory_space=pltpu.VMEM),
        scratch_shapes=[pltpu.SemaphoreType.DMA],
        compiler_params=pltpu.CompilerParams(vmem_limit_bytes=VMEM_GRANT),
        cost_estimate=pl.CostEstimate(flops=0, bytes_accessed=4 * math.prod(shape), transcendentals=0),
        name="assemble",
    )(source, place, *sources)


def on_device(
    tokens,
    query_weight,
    keyvalue_weight,
    adapter_down_weight,
    adapter_up_weight,
    keyvalue_page_store,
    span_token_length,
    adapter_owner,
    adapter_local_index,
    page_owner,
    page_local_index,
):
    peers = lax.axis_size("dp")
    half = peers // 2
    me = lax.axis_index("dp")
    tok_rows = tokens.shape[0]
    q_cols = query_weight.shape[1]
    rank = adapter_down_weight.shape[2]
    adapter_slots = peers * ADP_CAP

    def swap(array, distance):
        return lax.ppermute(array, "dp", [(peer, peer ^ distance) for peer in range(peers)])

    page_count = page_local_index.shape[0]
    request_count = adapter_local_index.shape[0]
    raw = jnp.concatenate([page_owner[:, 0], page_local_index, adapter_owner[:, 0], adapter_local_index])
    everyone = lax.all_to_all(
        jnp.broadcast_to(raw[None], (peers, raw.shape[0])), "dp", split_axis=0, concat_axis=0, tiled=True
    )
    down_store = jnp.swapaxes(adapter_down_weight, 1, 2)
    store, down_store, everyone = lax.optimization_barrier((keyvalue_page_store, down_store, everyone))
    mirrored_store = swap(store, half)

    page_cap = max(2, 2 * page_count // peers)
    group = everyone[jnp.arange(half, dtype=jnp.int32) ^ me]
    group_owner = group[:, :page_count]
    group_local = group[:, page_count : 2 * page_count]
    group_order = earlier_alike(group_owner)
    near_asked = asked_of(me, group_owner, group_order, group_local, page_cap)
    far_asked = asked_of(me ^ half, group_owner, group_order, group_local, page_cap)
    all_owner = everyone[:, 2 * page_count : 2 * page_count + request_count]
    all_local = everyone[:, 2 * page_count + request_count :]
    adapter_asked = asked_of(me, all_owner, earlier_alike(all_owner), all_local, ADP_CAP)
    adapter_near = adapter_asked[jnp.arange(peers, dtype=jnp.int32) ^ me]
    adapter_order = earlier_alike(adapter_owner[:, 0])
    down_pos = (adapter_owner[:, 0] ^ me) * ADP_CAP + adapter_order
    up_pos = adapter_owner[:, 0] * ADP_CAP + adapter_order
    page_source = page_owner[:, 0] ^ me
    page_place = jnp.where(page_source % half == 0, page_local_index, earlier_alike(page_owner[:, 0]))

    near = serve_both(near_asked[1:], adapter_near[1:half], store, down_store)
    near = [swap(pages, i + 1) for i, pages in enumerate(near)]
    own_down, *cross = serve(jnp.concatenate([adapter_near[:1], adapter_near[half:]]), down_store, VMEM_GRANT)
    up_rows = adapter_up_weight[adapter_asked.reshape(-1)]

    piece = lax.all_gather(tokens, "tensor", axis=1, tiled=True)
    query_base = jnp.dot(piece, query_weight, preferred_element_type=jnp.float32)
    new_cache = jnp.dot(piece, keyvalue_weight, preferred_element_type=jnp.float32).astype(jnp.bfloat16)

    cross, mirrored_store, query_base, new_cache, near = lax.optimization_barrier(
        (cross, mirrored_store, query_base, new_cache, near)
    )
    cross = [swap(rows, half + i) for i, rows in enumerate(cross)]
    far = serve(far_asked[1:], mirrored_store, SMALL_GRANT)
    far = [swap(pages, i + 1) for i, pages in enumerate(far)]
    up_rows, cross, far = lax.optimization_barrier((up_rows, cross, far))
    up_sent = lax.all_to_all(up_rows, "dp", split_axis=0, concat_axis=0, tiled=True)

    lengths = span_token_length[0]
    ends = jnp.cumsum(lengths)
    starts = ends - lengths
    steps = jnp.arange(tok_rows, dtype=jnp.int32)[:, None]
    member = (steps >= starts[None, :]) & (steps < ends[None, :])

    def in_slot(position):
        slot = jnp.sum(jnp.where(member, position[None, :], 0), axis=1)
        return slot[:, None] == jnp.arange(adapter_slots, dtype=jnp.int32)[None, :]

    def joined(pieces):
        cut = pieces.reshape(ADP_CAP, -1, rank, pieces.shape[2])
        return jnp.swapaxes(cut, 1, 2).reshape(ADP_CAP, rank, tokens.shape[1])

    near_down = [joined(block[page_cap:]) for block in near]
    down_sent = jnp.concatenate([own_down, *near_down, *cross], axis=0)
    down_part = jnp.einsum("tn,skn->tsk", tokens, down_sent, preferred_element_type=jnp.float32)
    shrink_part = jnp.sum(jnp.where(in_slot(down_pos)[:, :, None], down_part, 0.0), axis=1)
    shrink = lax.psum(shrink_part, "tensor").astype(jnp.bfloat16)
    spread = jnp.where(in_slot(up_pos)[:, :, None], shrink[:, None, :], 0).reshape(tok_rows, adapter_slots * rank)
    prefix_pages = assemble(page_source, page_place, [store, *near, mirrored_store, *far[:-1]])

    taken = starts[:, None] + jnp.arange(MOST, dtype=jnp.int32)[None, :]
    pick = (taken.reshape(-1, 1) == jnp.arange(tok_rows, dtype=jnp.int32)[None, :]).astype(jnp.bfloat16)
    fresh = jnp.dot(pick, new_cache, preferred_element_type=jnp.float32).astype(jnp.bfloat16)
    fresh = fresh.reshape(request_count, MOST, -1)
    up = up_sent.reshape(adapter_slots * rank, q_cols)
    out = attend(
        query_base, spread, up, fresh, prefix_pages, far[-1], page_source, page_place, peers - 1, starts, ends
    )
    return (out, new_cache)


def solution(mesh):
    return jax.shard_map(
        on_device,
        mesh=mesh,
        in_specs=(
            P("dp", "tensor"),
            P(None, "tensor"),
            P(None, "tensor"),
            P("dp", "tensor", None),
            P("dp", None, "tensor"),
            P("dp", None, "tensor"),
            P("dp", None),
            P("dp", None),
            P("dp"),
            P("dp", None),
            P("dp"),
        ),
        out_specs=(P("dp", "tensor"), P("dp", "tensor")),
        check_vma=False,
    )
```

```python
import functools
import math

import jax
import jax.numpy as jnp
from jax import lax
from jax.experimental import pallas as pl
from jax.experimental.pallas import tpu as pltpu
from jax.sharding import PartitionSpec as P

HEAD_WIDTH = 128
ADP_CAP = 2
HITS = 4
MOST = 128
BLOCK = 32
TOGETHER = 4
TILE = 256
VMEM_GRANT = 60 * 1024 * 1024
SMALL_GRANT = 16 * 1024 * 1024

ADAPTER_SCALE = 0.5
NEGATIVE = -1e30


def earlier_alike(owner):
    count = owner.shape[-1]
    ahead = jnp.arange(count, dtype=jnp.int32)[None, :] < jnp.arange(count, dtype=jnp.int32)[:, None]
    alike = owner[..., None, :] == owner[..., :, None]
    return jnp.sum((alike & ahead).astype(jnp.int32), axis=-1)


def asked_of(holder, owner, order, local, capacity):
    place = jnp.arange(capacity, dtype=jnp.int32)[None, :, None]
    match = (owner[:, None, :] == holder) & (order[:, None, :] == place)
    return jnp.sum(jnp.where(match, local[:, None, :], 0), axis=2)


def attention_steps(starts, ends, total):
    first = starts // BLOCK
    count = (ends - 1) // BLOCK - first + 1
    upto = jnp.cumsum(count)
    step = jnp.minimum(jnp.arange(total, dtype=jnp.int32), upto[-1] - 1)
    request = jnp.sum((upto[None, :] <= step[:, None]).astype(jnp.int32), axis=1)
    pick = request[:, None] == jnp.arange(starts.shape[0], dtype=jnp.int32)[None, :]

    def at(values):
        return jnp.sum(jnp.where(pick, values[None, :], 0), axis=1)

    block = at(first) + step - at(upto - count)
    return jnp.stack([request, block, at(starts), at(ends)])


def attention_kernel(
    last, steps_ref, source_ref, place_ref, spread_hbm, up_any, base_hbm, fresh_hbm, pages_hbm, last_hbm, *rest
):
    out_ref, query_ref, spread_ref, up_ref, base_ref, cache_ref, spread_sem, group_sems, tile_sems = rest
    q_cols = base_ref.shape[1]
    kv_heads = cache_ref.shape[2] // (2 * HEAD_WIDTH)
    group = q_cols // HEAD_WIDTH // kv_heads
    page = pages_hbm.shape[1]
    held = HITS * page
    groups = cache_ref.shape[0] // TOGETHER
    sharp = HEAD_WIDTH ** -0.5 * math.log2(math.e)

    def tile_copies(index):
        cols = pl.ds(pl.multiple_of(index * TILE, TILE), TILE)
        return (
            pltpu.make_async_copy(up_any.at[:, cols], up_ref.at[:, cols], tile_sems.at[0, index]),
            pltpu.make_async_copy(base_hbm.at[:, cols], base_ref.at[:, cols], tile_sems.at[1, index]),
        )

    def fetch(index, carry):
        rows = pl.ds(pl.multiple_of(index % HITS * page, page), page)
        to = cache_ref.at[index // HITS, rows]
        sem = group_sems.at[index // (HITS * TOGETHER)]
        late = source_ref[index] == last

        @pl.when(late)
        def _():
            pltpu.make_async_copy(last_hbm.at[place_ref[index]], to, sem).start()

        @pl.when(jnp.logical_not(late))
        def _():
            pltpu.make_async_copy(pages_hbm.at[index], to, sem).start()

        return carry

    spread_copy = pltpu.make_async_copy(spread_hbm, spread_ref, spread_sem)
    spread_copy.start()
    for index in range(q_cols // TILE):
        for copy in tile_copies(index):
            copy.start()
    for index in range(groups):
        rows = pl.ds(index * TOGETHER, TOGETHER)
        pltpu.make_async_copy(fresh_hbm.at[rows], cache_ref.at[rows, held:], group_sems.at[index]).start()
    lax.fori_loop(0, pages_hbm.shape[0], fetch, 0)
    spread_copy.wait()

    def project(index, carry):
        for copy in tile_copies(index):
            copy.wait()
        cols = pl.ds(pl.multiple_of(index * TILE, TILE), TILE)
        correction = jnp.dot(spread_ref[...], up_ref[:, cols], preferred_element_type=jnp.float32)
        query_ref[:, cols] = (base_ref[:, cols] + ADAPTER_SCALE * correction).astype(jnp.bfloat16)
        return carry

    lax.fori_loop(0, q_cols // TILE, project, 0)
    dims = (((1,), (1,)), ((), ()))
    tall = group * BLOCK
    q_at = lax.broadcasted_iota(jnp.int32, (kv_heads * tall, MOST), 0) % BLOCK
    ahead = lax.broadcasted_iota(jnp.int32, (kv_heads * tall, MOST), 1) - q_at
    own_at = lax.broadcasted_iota(jnp.int32, (BLOCK, HEAD_WIDTH), 0)
    blank = jnp.zeros((tall, HEAD_WIDTH), jnp.bfloat16)

    def side_by_side(request, offset):
        columns = [(2 * head + offset) * HEAD_WIDTH for head in range(kv_heads)]
        return jnp.concatenate([cache_ref[request, :, col : col + HEAD_WIDTH] for col in columns], axis=1)

    def queries(row):
        heads = []
        for head in range(kv_heads):
            columns = [(head * group + g) * HEAD_WIDTH for g in range(group)]
            own = jnp.concatenate([query_ref[pl.ds(row, BLOCK), col : col + HEAD_WIDTH] for col in columns], axis=0)
            heads.append(jnp.concatenate([own if other == head else blank for other in range(kv_heads)], axis=1))
        return jnp.concatenate(heads, axis=0)

    def several(turn, carry):
        @pl.when(turn < groups)
        def _():
            mine = cache_ref.at[pl.ds(turn * TOGETHER, TOGETHER)]
            pltpu.make_async_copy(mine, mine, group_sems.at[turn]).wait()

        places = []
        for lane in range(TOGETHER):
            index = turn * TOGETHER + lane
            row = pl.multiple_of(steps_ref[1, index] * BLOCK, BLOCK)
            places.append((steps_ref[0, index], row, steps_ref[2, index], steps_ref[3, index]))
        scores = []
        for request, row, start, _ in places:
            score = lax.dot_general(queries(row), side_by_side(request, 0), dims, preferred_element_type=jnp.float32)
            scores.append((score[:, :held], jnp.where(ahead <= row - start, score[:, held:], NEGATIVE)))
        weights = []
        for old_s, new_s in scores:
            top = jnp.maximum(
                jnp.max(old_s, axis=1, keepdims=True), jnp.max(new_s, axis=1, keepdims=True)
            )
            old_e = jnp.exp2((old_s - top) * sharp)
            new_e = jnp.exp2((new_s - top) * sharp)
            total = jnp.sum(old_e, axis=1, keepdims=True) + jnp.sum(new_e, axis=1, keepdims=True)
            weights.append((jnp.concatenate([old_e, new_e], axis=1).astype(jnp.bfloat16), total))
        results = []
        for (request, _, _, _), (weight, total) in zip(places, weights):
            summed = jnp.dot(weight, side_by_side(request, 1), preferred_element_type=jnp.float32)
            results.append((summed, total))
        for (_, row, start, end), (summed, total) in zip(places, results):
            own = (own_at >= start - row) & (own_at < end - row)
            for head in range(kv_heads):
                rows = slice(head * tall, (head + 1) * tall)
                result = summed[rows, head * HEAD_WIDTH : (head + 1) * HEAD_WIDTH] / total[rows]
                result = result.astype(jnp.bfloat16)
                for g in range(group):
                    col = (head * group + g) * HEAD_WIDTH
                    cols = slice(col, col + HEAD_WIDTH)
                    before = out_ref[pl.ds(row, BLOCK), cols]
                    out_ref[pl.ds(row, BLOCK), cols] = jnp.where(own, result[g * BLOCK : (g + 1) * BLOCK], before)
        return carry

    lax.fori_loop(0, steps_ref.shape[1] // TOGETHER, several, 0)


def attend(query_base, spread, up, fresh, pages, last_pages, source, place, last, starts, ends):
    rows, q_cols = query_base.shape
    requests = fresh.shape[0]
    keys = HITS * pages.shape[1] + MOST
    steps_total = -(-(rows // BLOCK + requests - 1) // TOGETHER) * TOGETHER
    steps = attention_steps(starts, ends, steps_total)
    hbm = pl.BlockSpec(memory_space=pltpu.HBM)
    scalars = pl.BlockSpec(memory_space=pltpu.SMEM)
    return pl.pallas_call(
        functools.partial(attention_kernel, last),
        out_shape=jax.ShapeDtypeStruct((rows, q_cols), jnp.bfloat16),
        in_specs=[scalars] * 3 + [hbm, pl.BlockSpec(memory_space=pl.ANY)] + [hbm] * 4,
        out_specs=pl.BlockSpec(memory_space=pltpu.VMEM),
        scratch_shapes=[
            pltpu.VMEM((rows, q_cols), jnp.bfloat16),
            *[pltpu.VMEM(each.shape, each.dtype) for each in (spread, up, query_base)],
            pltpu.VMEM((requests, keys, pages.shape[2]), pages.dtype),
            pltpu.SemaphoreType.DMA,
            pltpu.SemaphoreType.DMA((requests // TOGETHER,)),
            pltpu.SemaphoreType.DMA((2, q_cols // TILE)),
        ],
        compiler_params=pltpu.CompilerParams(vmem_limit_bytes=VMEM_GRANT - 2 * up.size),
        cost_estimate=pl.CostEstimate(
            flops=4 * steps_total * BLOCK * q_cols * keys + 2 * spread.size * q_cols,
            bytes_accessed=4 * query_base.size + 2 * (2 * spread.size + up.size + fresh.size + pages.size),
            transcendentals=0,
        ),
        name="attend",
    )(steps, source, place, spread, up, query_base, fresh, pages, last_pages)


def serve_kernel(asked_ref, store_ref, *refs):
    outs, sems = refs[:-1], refs[-1]
    for index, out in enumerate(outs):
        for place in range(out.shape[0]):
            page = asked_ref[index * out.shape[0] + place]
            pltpu.make_async_copy(store_ref.at[page], out.at[place], sems.at[index]).start()
    for index, out in enumerate(outs):
        pltpu.make_async_copy(out, out, sems.at[index]).wait()


def serve(asked, store, grant):
    blocks, capacity = asked.shape
    shape = (capacity,) + store.shape[1:]
    return pl.pallas_call(
        serve_kernel,
        out_shape=[jax.ShapeDtypeStruct(shape, store.dtype)] * blocks,
        in_specs=[pl.BlockSpec(memory_space=pltpu.SMEM), pl.BlockSpec(memory_space=pl.ANY)],
        out_specs=[pl.BlockSpec(memory_space=pltpu.VMEM)] * blocks,
        scratch_shapes=[pltpu.SemaphoreType.DMA((blocks,))],
        compiler_params=pltpu.CompilerParams(vmem_limit_bytes=grant),
        cost_estimate=pl.CostEstimate(
            flops=0, bytes_accessed=4 * blocks * math.prod(shape), transcendentals=0
        ),
        name="serve",
    )(asked.reshape(-1), store)


def assemble_kernel(source_ref, place_ref, *refs):
    sources, out, sem = refs[:-2], refs[-2], refs[-1]

    def one(index, carry):
        source = source_ref[index]
        place = place_ref[index]
        for number, ref in enumerate(sources):

            @pl.when(source == number)
            def _():
                pltpu.make_async_copy(ref.at[place], out.at[index], sem).start()

        @pl.when(source == len(sources))
        def _():
            pltpu.make_async_copy(sources[0].at[0], out.at[index], sem).start()

        return carry

    lax.fori_loop(0, out.shape[0], one, 0)
    pltpu.make_async_copy(out, out, sem).wait()


def assemble(source, place, sources):
    scalars = pl.BlockSpec(memory_space=pltpu.SMEM)
    shape = (source.shape[0],) + sources[0].shape[1:]
    return pl.pallas_call(
        assemble_kernel,
        out_shape=jax.ShapeDtypeStruct(shape, sources[0].dtype),
        in_specs=[scalars, scalars] + [pl.BlockSpec(memory_space=pltpu.HBM)] * len(sources),
        out_specs=pl.BlockSpec(memory_space=pltpu.VMEM),
        scratch_shapes=[pltpu.SemaphoreType.DMA],
        compiler_params=pltpu.CompilerParams(vmem_limit_bytes=VMEM_GRANT),
        cost_estimate=pl.CostEstimate(flops=0, bytes_accessed=4 * math.prod(shape), transcendentals=0),
        name="assemble",
    )(source, place, *sources)


def on_device(
    tokens,
    query_weight,
    keyvalue_weight,
    adapter_down_weight,
    adapter_up_weight,
    keyvalue_page_store,
    span_token_length,
    adapter_owner,
    adapter_local_index,
    page_owner,
    page_local_index,
):
    peers = lax.axis_size("dp")
    half = peers // 2
    me = lax.axis_index("dp")
    tok_rows = tokens.shape[0]
    q_cols = query_weight.shape[1]
    rank = adapter_down_weight.shape[2]
    adapter_slots = peers * ADP_CAP

    def swap(array, distance):
        return lax.ppermute(array, "dp", [(peer, peer ^ distance) for peer in range(peers)])

    page_count = page_local_index.shape[0]
    request_count = adapter_local_index.shape[0]
    raw = jnp.concatenate([page_owner[:, 0], page_local_index, adapter_owner[:, 0], adapter_local_index])
    everyone = lax.all_to_all(
        jnp.broadcast_to(raw[None], (peers, raw.shape[0])), "dp", split_axis=0, concat_axis=0, tiled=True
    )
    store, down_store, everyone = lax.optimization_barrier((keyvalue_page_store, adapter_down_weight, everyone))
    mirrored_store = swap(store, half)

    page_cap = max(2, 2 * page_count // peers)
    group = everyone[jnp.arange(half, dtype=jnp.int32) ^ me]
    group_owner = group[:, :page_count]
    group_local = group[:, page_count : 2 * page_count]
    group_order = earlier_alike(group_owner)
    near_asked = asked_of(me, group_owner, group_order, group_local, page_cap)
    far_asked = asked_of(me ^ half, group_owner, group_order, group_local, page_cap)
    all_owner = everyone[:, 2 * page_count : 2 * page_count + request_count]
    all_local = everyone[:, 2 * page_count + request_count :]
    adapter_asked = asked_of(me, all_owner, earlier_alike(all_owner), all_local, ADP_CAP).reshape(-1)
    adapter_pos = adapter_owner[:, 0] * ADP_CAP + earlier_alike(adapter_owner[:, 0])
    page_source = page_owner[:, 0] ^ me
    page_place = jnp.where(page_source % half == 0, page_local_index, earlier_alike(page_owner[:, 0]))

    near = [swap(pages, i + 1) for i, pages in enumerate(serve(near_asked[1:], store, VMEM_GRANT))]
    down_rows = down_store[adapter_asked]
    up_rows = adapter_up_weight[adapter_asked]

    piece = lax.all_gather(tokens, "tensor", axis=1, tiled=True)
    query_base = jnp.dot(piece, query_weight, preferred_element_type=jnp.float32)
    new_cache = jnp.dot(piece, keyvalue_weight, preferred_element_type=jnp.float32).astype(jnp.bfloat16)

    down_rows, mirrored_store, query_base, new_cache, near = lax.optimization_barrier(
        (down_rows, mirrored_store, query_base, new_cache, near)
    )
    down_sent = lax.all_to_all(down_rows, "dp", split_axis=0, concat_axis=0, tiled=True)
    far = list(serve(far_asked[1:], mirrored_store, SMALL_GRANT))
    far = [swap(pages, i + 1) for i, pages in enumerate(far[:-1])] + far[-1:]
    up_rows, down_sent, far = lax.optimization_barrier((up_rows, down_sent, far))
    up_sent = lax.all_to_all(up_rows, "dp", split_axis=0, concat_axis=0, tiled=True)
    far[-1] = swap(far[-1], half - 1)

    lengths = span_token_length[0]
    ends = jnp.cumsum(lengths)
    starts = ends - lengths
    steps = jnp.arange(tok_rows, dtype=jnp.int32)[:, None]
    member = (steps >= starts[None, :]) & (steps < ends[None, :])
    slot = jnp.sum(jnp.where(member, adapter_pos[None, :], 0), axis=1)
    in_slot = slot[:, None] == jnp.arange(adapter_slots, dtype=jnp.int32)[None, :]

    down_part = jnp.einsum("tn,snk->tsk", tokens, down_sent, preferred_element_type=jnp.float32)
    shrink_part = jnp.sum(jnp.where(in_slot[:, :, None], down_part, 0.0), axis=1)
    shrink = lax.psum(shrink_part, "tensor").astype(jnp.bfloat16)
    spread = jnp.where(in_slot[:, :, None], shrink[:, None, :], 0).reshape(tok_rows, adapter_slots * rank)
    prefix_pages = assemble(page_source, page_place, [store, *near, mirrored_store, *far[:-1]])

    taken = starts[:, None] + jnp.arange(MOST, dtype=jnp.int32)[None, :]
    pick = (taken.reshape(-1, 1) == jnp.arange(tok_rows, dtype=jnp.int32)[None, :]).astype(jnp.bfloat16)
    fresh = jnp.dot(pick, new_cache, preferred_element_type=jnp.float32).astype(jnp.bfloat16)
    fresh = fresh.reshape(request_count, MOST, -1)
    up = up_sent.reshape(adapter_slots * rank, q_cols)
    out = attend(
        query_base, spread, up, fresh, prefix_pages, far[-1], page_source, page_place, peers - 1, starts, ends
    )
    return (out, new_cache)


def solution(mesh):
    return jax.shard_map(
        on_device,
        mesh=mesh,
        in_specs=(
            P("dp", "tensor"),
            P(None, "tensor"),
            P(None, "tensor"),
            P("dp", "tensor", None),
            P("dp", None, "tensor"),
            P("dp", None, "tensor"),
            P("dp", None),
            P("dp", None),
            P("dp"),
            P("dp", None),
            P("dp"),
        ),
        out_specs=(P("dp", "tensor"), P("dp", "tensor")),
        check_vma=False,
    )
```

```python
import functools
import math

import jax
import jax.numpy as jnp
from jax import lax
from jax.experimental import pallas as pl
from jax.experimental.pallas import tpu as pltpu
from jax.sharding import PartitionSpec as P

HEAD_WIDTH = 128
ADP_CAP = 2
HITS = 4
MOST = 128
BLOCK = 16
TOGETHER = 8
TILE = 256
VMEM_GRANT = 60 * 1024 * 1024
SMALL_GRANT = 16 * 1024 * 1024

ADAPTER_SCALE = 0.5
NEGATIVE = -1e30


def earlier_alike(owner):
    count = owner.shape[-1]
    ahead = jnp.arange(count, dtype=jnp.int32)[None, :] < jnp.arange(count, dtype=jnp.int32)[:, None]
    alike = owner[..., None, :] == owner[..., :, None]
    return jnp.sum((alike & ahead).astype(jnp.int32), axis=-1)


def asked_of(holder, owner, order, local, capacity):
    place = jnp.arange(capacity, dtype=jnp.int32)[None, :, None]
    match = (owner[:, None, :] == holder) & (order[:, None, :] == place)
    return jnp.sum(jnp.where(match, local[:, None, :], 0), axis=2)


def attention_steps(starts, ends, total):
    first = starts // BLOCK
    count = (ends - 1) // BLOCK - first + 1
    upto = jnp.cumsum(count)
    step = jnp.minimum(jnp.arange(total, dtype=jnp.int32), upto[-1] - 1)
    request = jnp.sum((upto[None, :] <= step[:, None]).astype(jnp.int32), axis=1)
    pick = request[:, None] == jnp.arange(starts.shape[0], dtype=jnp.int32)[None, :]

    def at(values):
        return jnp.sum(jnp.where(pick, values[None, :], 0), axis=1)

    block = at(first) + step - at(upto - count)
    return jnp.stack([request, block, at(starts), at(ends)])


def attention_kernel(
    last, steps_ref, source_ref, place_ref, spread_hbm, up_any, base_hbm, fresh_hbm, pages_hbm, last_hbm, *rest
):
    out_ref, query_ref, spread_ref, up_ref, base_ref, cache_ref, sems, tile_sems = rest
    q_cols = base_ref.shape[1]
    kv_heads = cache_ref.shape[2] // (2 * HEAD_WIDTH)
    group = q_cols // HEAD_WIDTH // kv_heads
    page = pages_hbm.shape[1]
    held = HITS * page
    sharp = HEAD_WIDTH ** -0.5 * math.log2(math.e)

    def tile_copies(index):
        cols = pl.ds(pl.multiple_of(index * TILE, TILE), TILE)
        return (
            pltpu.make_async_copy(up_any.at[:, cols], up_ref.at[:, cols], tile_sems.at[0, index]),
            pltpu.make_async_copy(base_hbm.at[:, cols], base_ref.at[:, cols], tile_sems.at[1, index]),
        )

    def fetch(index, carry):
        rows = pl.ds(pl.multiple_of(index % HITS * page, page), page)
        to = cache_ref.at[index // HITS, rows]
        late = source_ref[index] == last

        @pl.when(late)
        def _():
            pltpu.make_async_copy(last_hbm.at[place_ref[index]], to, sems.at[1]).start()

        @pl.when(jnp.logical_not(late))
        def _():
            pltpu.make_async_copy(pages_hbm.at[index], to, sems.at[1]).start()

        return carry

    spread_copy = pltpu.make_async_copy(spread_hbm, spread_ref, sems.at[0])
    fresh_copy = pltpu.make_async_copy(fresh_hbm, cache_ref.at[:, held:], sems.at[2])
    spread_copy.start()
    for index in range(q_cols // TILE):
        for copy in tile_copies(index):
            copy.start()
    fresh_copy.start()
    lax.fori_loop(0, pages_hbm.shape[0], fetch, 0)
    spread_copy.wait()

    def project(index, carry):
        for copy in tile_copies(index):
            copy.wait()
        cols = pl.ds(pl.multiple_of(index * TILE, TILE), TILE)
        correction = jnp.dot(spread_ref[...], up_ref[:, cols], preferred_element_type=jnp.float32)
        query_ref[:, cols] = (base_ref[:, cols] + ADAPTER_SCALE * correction).astype(jnp.bfloat16)
        return carry

    lax.fori_loop(0, q_cols // TILE, project, 0)
    fresh_copy.wait()
    prefix = cache_ref.at[:, :held]
    pltpu.make_async_copy(prefix, prefix, sems.at[1]).wait()
    dims = (((1,), (1,)), ((), ()))
    tall = group * BLOCK
    q_at = lax.broadcasted_iota(jnp.int32, (kv_heads * tall, MOST), 0) % BLOCK
    ahead = lax.broadcasted_iota(jnp.int32, (kv_heads * tall, MOST), 1) - q_at
    own_at = lax.broadcasted_iota(jnp.int32, (BLOCK, HEAD_WIDTH), 0)
    blank = jnp.zeros((tall, HEAD_WIDTH), jnp.bfloat16)

    def side_by_side(request, offset):
        columns = [(2 * head + offset) * HEAD_WIDTH for head in range(kv_heads)]
        return jnp.concatenate([cache_ref[request, :, col : col + HEAD_WIDTH] for col in columns], axis=1)

    def queries(row):
        heads = []
        for head in range(kv_heads):
            columns = [(head * group + g) * HEAD_WIDTH for g in range(group)]
            own = jnp.concatenate([query_ref[pl.ds(row, BLOCK), col : col + HEAD_WIDTH] for col in columns], axis=0)
            heads.append(jnp.concatenate([own if other == head else blank for other in range(kv_heads)], axis=1))
        return jnp.concatenate(heads, axis=0)

    def several(turn, carry):
        places = []
        for lane in range(TOGETHER):
            index = turn * TOGETHER + lane
            row = pl.multiple_of(steps_ref[1, index] * BLOCK, BLOCK)
            places.append((steps_ref[0, index], row, steps_ref[2, index], steps_ref[3, index]))
        scores = []
        for request, row, start, _ in places:
            score = lax.dot_general(queries(row), side_by_side(request, 0), dims, preferred_element_type=jnp.float32)
            scores.append((score[:, :held], jnp.where(ahead <= row - start, score[:, held:], NEGATIVE)))
        weights = []
        for old_s, new_s in scores:
            top = jnp.maximum(
                jnp.max(old_s, axis=1, keepdims=True), jnp.max(new_s, axis=1, keepdims=True)
            )
            old_e = jnp.exp2((old_s - top) * sharp)
            new_e = jnp.exp2((new_s - top) * sharp)
            total = jnp.sum(old_e, axis=1, keepdims=True) + jnp.sum(new_e, axis=1, keepdims=True)
            weights.append((jnp.concatenate([old_e, new_e], axis=1).astype(jnp.bfloat16), total))
        results = []
        for (request, _, _, _), (weight, total) in zip(places, weights):
            summed = jnp.dot(weight, side_by_side(request, 1), preferred_element_type=jnp.float32)
            results.append((summed, total))
        for (_, row, start, end), (summed, total) in zip(places, results):
            own = (own_at >= start - row) & (own_at < end - row)
            for head in range(kv_heads):
                rows = slice(head * tall, (head + 1) * tall)
                result = summed[rows, head * HEAD_WIDTH : (head + 1) * HEAD_WIDTH] / total[rows]
                result = result.astype(jnp.bfloat16)
                for g in range(group):
                    col = (head * group + g) * HEAD_WIDTH
                    cols = slice(col, col + HEAD_WIDTH)
                    before = out_ref[pl.ds(row, BLOCK), cols]
                    out_ref[pl.ds(row, BLOCK), cols] = jnp.where(own, result[g * BLOCK : (g + 1) * BLOCK], before)
        return carry

    lax.fori_loop(0, steps_ref.shape[1] // TOGETHER, several, 0)


def attend(query_base, spread, up, fresh, pages, last_pages, source, place, last, steps):
    rows, q_cols = query_base.shape
    requests = fresh.shape[0]
    keys = HITS * pages.shape[1] + MOST
    hbm = pl.BlockSpec(memory_space=pltpu.HBM)
    scalars = pl.BlockSpec(memory_space=pltpu.SMEM)
    return pl.pallas_call(
        functools.partial(attention_kernel, last),
        out_shape=jax.ShapeDtypeStruct((rows, q_cols), jnp.bfloat16),
        in_specs=[scalars] * 3 + [hbm] * 6,
        out_specs=pl.BlockSpec(memory_space=pltpu.VMEM),
        scratch_shapes=[
            pltpu.VMEM((rows, q_cols), jnp.bfloat16),
            *[pltpu.VMEM(each.shape, each.dtype) for each in (spread, up, query_base)],
            pltpu.VMEM((requests, keys, pages.shape[2]), pages.dtype),
            pltpu.SemaphoreType.DMA((3,)),
            pltpu.SemaphoreType.DMA((2, q_cols // TILE)),
        ],
        compiler_params=pltpu.CompilerParams(vmem_limit_bytes=VMEM_GRANT),
        cost_estimate=pl.CostEstimate(
            flops=4 * steps.shape[1] * BLOCK * q_cols * keys + 2 * spread.size * q_cols,
            bytes_accessed=4 * query_base.size + 2 * (2 * spread.size + up.size + fresh.size + pages.size),
            transcendentals=0,
        ),
        name="attend",
    )(steps, source, place, spread, up, query_base, fresh, pages, last_pages)


def serve_kernel(asked_ref, store_ref, *refs):
    outs, sems = refs[:-1], refs[-1]
    for index, out in enumerate(outs):
        for place in range(out.shape[0]):
            page = asked_ref[index * out.shape[0] + place]
            pltpu.make_async_copy(store_ref.at[page], out.at[place], sems.at[index]).start()
    for index, out in enumerate(outs):
        pltpu.make_async_copy(out, out, sems.at[index]).wait()


def serve(asked, store, grant):
    blocks, capacity = asked.shape
    shape = (capacity,) + store.shape[1:]
    return pl.pallas_call(
        serve_kernel,
        out_shape=[jax.ShapeDtypeStruct(shape, store.dtype)] * blocks,
        in_specs=[pl.BlockSpec(memory_space=pltpu.SMEM), pl.BlockSpec(memory_space=pl.ANY)],
        out_specs=[pl.BlockSpec(memory_space=pltpu.VMEM)] * blocks,
        scratch_shapes=[pltpu.SemaphoreType.DMA((blocks,))],
        compiler_params=pltpu.CompilerParams(vmem_limit_bytes=grant),
        cost_estimate=pl.CostEstimate(
            flops=0, bytes_accessed=4 * blocks * math.prod(shape), transcendentals=0
        ),
        name="serve",
    )(asked.reshape(-1), store)


def assemble_kernel(source_ref, place_ref, *refs):
    sources, out, sem = refs[:-2], refs[-2], refs[-1]

    def one(index, carry):
        source = source_ref[index]
        place = place_ref[index]
        for number, ref in enumerate(sources):

            @pl.when(source == number)
            def _():
                pltpu.make_async_copy(ref.at[place], out.at[index], sem).start()

        @pl.when(source == len(sources))
        def _():
            pltpu.make_async_copy(sources[0].at[0], out.at[index], sem).start()

        return carry

    lax.fori_loop(0, out.shape[0], one, 0)
    pltpu.make_async_copy(out, out, sem).wait()


def assemble(source, place, sources):
    scalars = pl.BlockSpec(memory_space=pltpu.SMEM)
    shape = (source.shape[0],) + sources[0].shape[1:]
    return pl.pallas_call(
        assemble_kernel,
        out_shape=jax.ShapeDtypeStruct(shape, sources[0].dtype),
        in_specs=[scalars, scalars] + [pl.BlockSpec(memory_space=pltpu.HBM)] * len(sources),
        out_specs=pl.BlockSpec(memory_space=pltpu.VMEM),
        scratch_shapes=[pltpu.SemaphoreType.DMA],
        compiler_params=pltpu.CompilerParams(vmem_limit_bytes=VMEM_GRANT),
        cost_estimate=pl.CostEstimate(flops=0, bytes_accessed=4 * math.prod(shape), transcendentals=0),
        name="assemble",
    )(source, place, *sources)


def on_device(
    tokens,
    query_weight,
    keyvalue_weight,
    adapter_down_weight,
    adapter_up_weight,
    keyvalue_page_store,
    span_token_length,
    adapter_owner,
    adapter_local_index,
    page_owner,
    page_local_index,
):
    peers = lax.axis_size("dp")
    half = peers // 2
    me = lax.axis_index("dp")
    tok_rows = tokens.shape[0]
    q_cols = query_weight.shape[1]
    rank = adapter_down_weight.shape[2]
    adapter_slots = peers * ADP_CAP

    def swap(array, distance):
        return lax.ppermute(array, "dp", [(peer, peer ^ distance) for peer in range(peers)])

    page_count = page_local_index.shape[0]
    request_count = adapter_local_index.shape[0]
    raw = jnp.concatenate([page_owner[:, 0], page_local_index, adapter_owner[:, 0], adapter_local_index])
    everyone = lax.all_to_all(
        jnp.broadcast_to(raw[None], (peers, raw.shape[0])), "dp", split_axis=0, concat_axis=0, tiled=True
    )
    store, down_store, everyone = lax.optimization_barrier((keyvalue_page_store, adapter_down_weight, everyone))
    mirrored_store = swap(store, half)

    page_cap = max(2, 2 * page_count // peers)
    group = everyone[jnp.arange(half, dtype=jnp.int32) ^ me]
    group_owner = group[:, :page_count]
    group_local = group[:, page_count : 2 * page_count]
    group_order = earlier_alike(group_owner)
    near_asked = asked_of(me, group_owner, group_order, group_local, page_cap)
    far_asked = asked_of(me ^ half, group_owner, group_order, group_local, page_cap)
    all_owner = everyone[:, 2 * page_count : 2 * page_count + request_count]
    all_local = everyone[:, 2 * page_count + request_count :]
    adapter_asked = asked_of(me, all_owner, earlier_alike(all_owner), all_local, ADP_CAP).reshape(-1)
    adapter_pos = adapter_owner[:, 0] * ADP_CAP + earlier_alike(adapter_owner[:, 0])
    page_source = page_owner[:, 0] ^ me
    page_place = jnp.where(page_source % half == 0, page_local_index, earlier_alike(page_owner[:, 0]))

    near = [swap(pages, i + 1) for i, pages in enumerate(serve(near_asked[1:], store, VMEM_GRANT))]
    down_rows = down_store[adapter_asked]
    up_rows = adapter_up_weight[adapter_asked]

    piece = lax.all_gather(tokens, "tensor", axis=1, tiled=True)
    query_base = jnp.dot(piece, query_weight, preferred_element_type=jnp.float32)
    new_cache = jnp.dot(piece, keyvalue_weight, preferred_element_type=jnp.float32).astype(jnp.bfloat16)

    down_rows, mirrored_store, query_base, new_cache, near = lax.optimization_barrier(
        (down_rows, mirrored_store, query_base, new_cache, near)
    )
    lengths = span_token_length[0]
    ends = jnp.cumsum(lengths)
    starts = ends - lengths
    row = jnp.arange(tok_rows, dtype=jnp.int32)[:, None]
    member = (row >= starts[None, :]) & (row < ends[None, :])
    slot = jnp.sum(jnp.where(member, adapter_pos[None, :], 0), axis=1)
    in_slot = slot[:, None] == jnp.arange(adapter_slots, dtype=jnp.int32)[None, :]
    steps_total = -(-(tok_rows // BLOCK + request_count - 1) // TOGETHER) * TOGETHER
    steps = attention_steps(starts, ends, steps_total)

    down_sent = lax.all_to_all(down_rows, "dp", split_axis=0, concat_axis=0, tiled=True)
    far = list(serve(far_asked[1:], mirrored_store, SMALL_GRANT))
    far = [swap(pages, i + 1) for i, pages in enumerate(far[:-1])] + far[-1:]
    up_rows, down_sent, far, in_slot, steps, page_source, page_place = lax.optimization_barrier(
        (up_rows, down_sent, far, in_slot, steps, page_source, page_place)
    )
    up_sent = lax.all_to_all(up_rows, "dp", split_axis=0, concat_axis=0, tiled=True)
    far[-1] = swap(far[-1], half - 1)

    down_part = jnp.einsum("tn,snk->tsk", tokens, down_sent, preferred_element_type=jnp.float32)
    shrink_part = jnp.sum(jnp.where(in_slot[:, :, None], down_part, 0.0), axis=1)
    shrink = lax.psum(shrink_part, "tensor").astype(jnp.bfloat16)
    spread = jnp.where(in_slot[:, :, None], shrink[:, None, :], 0).reshape(tok_rows, adapter_slots * rank)
    prefix_pages = assemble(page_source, page_place, [store, *near, mirrored_store, *far[:-1]])

    taken = starts[:, None] + jnp.arange(MOST, dtype=jnp.int32)[None, :]
    pick = (taken.reshape(-1, 1) == jnp.arange(tok_rows, dtype=jnp.int32)[None, :]).astype(jnp.bfloat16)
    fresh = jnp.dot(pick, new_cache, preferred_element_type=jnp.float32).astype(jnp.bfloat16)
    fresh = fresh.reshape(request_count, MOST, -1)
    up = up_sent.reshape(adapter_slots * rank, q_cols)
    out = attend(
        query_base, spread, up, fresh, prefix_pages, far[-1], page_source, page_place, peers - 1, steps
    )
    return (out, new_cache)


def solution(mesh):
    return jax.shard_map(
        on_device,
        mesh=mesh,
        in_specs=(
            P("dp", "tensor"),
            P(None, "tensor"),
            P(None, "tensor"),
            P("dp", "tensor", None),
            P("dp", None, "tensor"),
            P("dp", None, "tensor"),
            P("dp", None),
            P("dp", None),
            P("dp"),
            P("dp", None),
            P("dp"),
        ),
        out_specs=(P("dp", "tensor"), P("dp", "tensor")),
        check_vma=False,
    )
```

```python
import functools
import math

import jax
import jax.numpy as jnp
from jax import lax
from jax.experimental import pallas as pl
from jax.experimental.pallas import tpu as pltpu
from jax.sharding import PartitionSpec as P

HEAD_WIDTH = 128
ADP_CAP = 2
HITS = 4
MOST = 128
BLOCK = 16
TOGETHER = 16
TILE = 256
VMEM_GRANT = 60 * 1024 * 1024
SMALL_GRANT = 16 * 1024 * 1024

ADAPTER_SCALE = 0.5
NEGATIVE = -1e30


def earlier_alike(owner):
    count = owner.shape[-1]
    ahead = jnp.arange(count, dtype=jnp.int32)[None, :] < jnp.arange(count, dtype=jnp.int32)[:, None]
    alike = owner[..., None, :] == owner[..., :, None]
    return jnp.sum((alike & ahead).astype(jnp.int32), axis=-1)


def asked_of(holder, owner, order, local, capacity):
    place = jnp.arange(capacity, dtype=jnp.int32)[None, :, None]
    match = (owner[:, None, :] == holder) & (order[:, None, :] == place)
    return jnp.sum(jnp.where(match, local[:, None, :], 0), axis=2)


def attention_steps(starts, ends, total):
    first = starts // BLOCK
    count = (ends - 1) // BLOCK - first + 1
    upto = jnp.cumsum(count)
    step = jnp.minimum(jnp.arange(total, dtype=jnp.int32), upto[-1] - 1)
    request = jnp.sum((upto[None, :] <= step[:, None]).astype(jnp.int32), axis=1)
    pick = request[:, None] == jnp.arange(starts.shape[0], dtype=jnp.int32)[None, :]

    def at(values):
        return jnp.sum(jnp.where(pick, values[None, :], 0), axis=1)

    block = at(first) + step - at(upto - count)
    return jnp.stack([request, block, at(starts), at(ends)])


def attention_kernel(
    last, steps_ref, source_ref, place_ref, spread_hbm, up_any, base_hbm, fresh_hbm, pages_hbm, last_hbm, *rest
):
    out_ref, query_ref, spread_ref, up_ref, base_ref, cache_ref, sems, tile_sems = rest
    q_cols = base_ref.shape[1]
    kv_heads = cache_ref.shape[2] // (2 * HEAD_WIDTH)
    group = q_cols // HEAD_WIDTH // kv_heads
    page = pages_hbm.shape[1]
    held = HITS * page
    sharp = HEAD_WIDTH ** -0.5 * math.log2(math.e)

    def tile_copies(index):
        cols = pl.ds(pl.multiple_of(index * TILE, TILE), TILE)
        return (
            pltpu.make_async_copy(up_any.at[:, cols], up_ref.at[:, cols], tile_sems.at[0, index]),
            pltpu.make_async_copy(base_hbm.at[:, cols], base_ref.at[:, cols], tile_sems.at[1, index]),
        )

    def fetch(index, carry):
        rows = pl.ds(pl.multiple_of(index % HITS * page, page), page)
        to = cache_ref.at[index // HITS, rows]
        late = source_ref[index] == last

        @pl.when(late)
        def _():
            pltpu.make_async_copy(last_hbm.at[place_ref[index]], to, sems.at[1]).start()

        @pl.when(jnp.logical_not(late))
        def _():
            pltpu.make_async_copy(pages_hbm.at[index], to, sems.at[1]).start()

        return carry

    spread_copy = pltpu.make_async_copy(spread_hbm, spread_ref, sems.at[0])
    fresh_copy = pltpu.make_async_copy(fresh_hbm, cache_ref.at[:, held:], sems.at[2])
    spread_copy.start()
    for index in range(q_cols // TILE):
        for copy in tile_copies(index):
            copy.start()
    fresh_copy.start()
    lax.fori_loop(0, pages_hbm.shape[0], fetch, 0)
    spread_copy.wait()

    def project(index, carry):
        for copy in tile_copies(index):
            copy.wait()
        cols = pl.ds(pl.multiple_of(index * TILE, TILE), TILE)
        correction = jnp.dot(spread_ref[...], up_ref[:, cols], preferred_element_type=jnp.float32)
        query_ref[:, cols] = (base_ref[:, cols] + ADAPTER_SCALE * correction).astype(jnp.bfloat16)
        return carry

    lax.fori_loop(0, q_cols // TILE, project, 0)
    fresh_copy.wait()
    prefix = cache_ref.at[:, :held]
    pltpu.make_async_copy(prefix, prefix, sems.at[1]).wait()
    dims = (((1,), (1,)), ((), ()))
    tall = group * BLOCK
    q_at = lax.broadcasted_iota(jnp.int32, (kv_heads * tall, MOST), 0) % BLOCK
    ahead = lax.broadcasted_iota(jnp.int32, (kv_heads * tall, MOST), 1) - q_at
    own_at = lax.broadcasted_iota(jnp.int32, (BLOCK, HEAD_WIDTH), 0)
    blank = jnp.zeros((tall, HEAD_WIDTH), jnp.bfloat16)

    def side_by_side(request, offset):
        columns = [(2 * head + offset) * HEAD_WIDTH for head in range(kv_heads)]
        return jnp.concatenate([cache_ref[request, :, col : col + HEAD_WIDTH] for col in columns], axis=1)

    def queries(row):
        heads = []
        for head in range(kv_heads):
            columns = [(head * group + g) * HEAD_WIDTH for g in range(group)]
            own = jnp.concatenate([query_ref[pl.ds(row, BLOCK), col : col + HEAD_WIDTH] for col in columns], axis=0)
            heads.append(jnp.concatenate([own if other == head else blank for other in range(kv_heads)], axis=1))
        return jnp.concatenate(heads, axis=0)

    def several(turn, carry):
        places = []
        for lane in range(TOGETHER):
            index = turn * TOGETHER + lane
            row = pl.multiple_of(steps_ref[1, index] * BLOCK, BLOCK)
            places.append((steps_ref[0, index], row, steps_ref[2, index], steps_ref[3, index]))
        scores = []
        for request, row, start, _ in places:
            score = lax.dot_general(queries(row), side_by_side(request, 0), dims, preferred_element_type=jnp.float32)
            scores.append((score[:, :held], jnp.where(ahead <= row - start, score[:, held:], NEGATIVE)))
        weights = []
        for old_s, new_s in scores:
            top = jnp.maximum(
                jnp.max(old_s, axis=1, keepdims=True), jnp.max(new_s, axis=1, keepdims=True)
            )
            old_e = jnp.exp2((old_s - top) * sharp)
            new_e = jnp.exp2((new_s - top) * sharp)
            total = jnp.sum(old_e, axis=1, keepdims=True) + jnp.sum(new_e, axis=1, keepdims=True)
            weights.append((jnp.concatenate([old_e, new_e], axis=1).astype(jnp.bfloat16), total))
        results = []
        for (request, _, _, _), (weight, total) in zip(places, weights):
            summed = jnp.dot(weight, side_by_side(request, 1), preferred_element_type=jnp.float32)
            results.append((summed, total))
        for (_, row, start, end), (summed, total) in zip(places, results):
            own = (own_at >= start - row) & (own_at < end - row)
            for head in range(kv_heads):
                rows = slice(head * tall, (head + 1) * tall)
                result = summed[rows, head * HEAD_WIDTH : (head + 1) * HEAD_WIDTH] / total[rows]
                result = result.astype(jnp.bfloat16)
                for g in range(group):
                    col = (head * group + g) * HEAD_WIDTH
                    cols = slice(col, col + HEAD_WIDTH)
                    before = out_ref[pl.ds(row, BLOCK), cols]
                    out_ref[pl.ds(row, BLOCK), cols] = jnp.where(own, result[g * BLOCK : (g + 1) * BLOCK], before)
        return carry

    lax.fori_loop(0, steps_ref.shape[1] // TOGETHER, several, 0)


def attend(query_base, spread, up, fresh, pages, last_pages, source, place, last, steps):
    rows, q_cols = query_base.shape
    requests = fresh.shape[0]
    keys = HITS * pages.shape[1] + MOST
    hbm = pl.BlockSpec(memory_space=pltpu.HBM)
    scalars = pl.BlockSpec(memory_space=pltpu.SMEM)
    return pl.pallas_call(
        functools.partial(attention_kernel, last),
        out_shape=jax.ShapeDtypeStruct((rows, q_cols), jnp.bfloat16),
        in_specs=[scalars] * 3 + [hbm] * 6,
        out_specs=pl.BlockSpec(memory_space=pltpu.VMEM),
        scratch_shapes=[
            pltpu.VMEM((rows, q_cols), jnp.bfloat16),
            *[pltpu.VMEM(each.shape, each.dtype) for each in (spread, up, query_base)],
            pltpu.VMEM((requests, keys, pages.shape[2]), pages.dtype),
            pltpu.SemaphoreType.DMA((3,)),
            pltpu.SemaphoreType.DMA((2, q_cols // TILE)),
        ],
        compiler_params=pltpu.CompilerParams(vmem_limit_bytes=VMEM_GRANT),
        cost_estimate=pl.CostEstimate(
            flops=4 * steps.shape[1] * BLOCK * q_cols * keys + 2 * spread.size * q_cols,
            bytes_accessed=4 * query_base.size + 2 * (2 * spread.size + up.size + fresh.size + pages.size),
            transcendentals=0,
        ),
        name="attend",
    )(steps, source, place, spread, up, query_base, fresh, pages, last_pages)


def serve_kernel(asked_ref, store_ref, *refs):
    outs, sems = refs[:-1], refs[-1]
    for index, out in enumerate(outs):
        for place in range(out.shape[0]):
            page = asked_ref[index * out.shape[0] + place]
            pltpu.make_async_copy(store_ref.at[page], out.at[place], sems.at[index]).start()
    for index, out in enumerate(outs):
        pltpu.make_async_copy(out, out, sems.at[index]).wait()


def serve(asked, store, grant):
    blocks, capacity = asked.shape
    shape = (capacity,) + store.shape[1:]
    return pl.pallas_call(
        serve_kernel,
        out_shape=[jax.ShapeDtypeStruct(shape, store.dtype)] * blocks,
        in_specs=[pl.BlockSpec(memory_space=pltpu.SMEM), pl.BlockSpec(memory_space=pl.ANY)],
        out_specs=[pl.BlockSpec(memory_space=pltpu.VMEM)] * blocks,
        scratch_shapes=[pltpu.SemaphoreType.DMA((blocks,))],
        compiler_params=pltpu.CompilerParams(vmem_limit_bytes=grant),
        cost_estimate=pl.CostEstimate(
            flops=0, bytes_accessed=4 * blocks * math.prod(shape), transcendentals=0
        ),
        name="serve",
    )(asked.reshape(-1), store)


def assemble_kernel(source_ref, place_ref, *refs):
    sources, out, sem = refs[:-2], refs[-2], refs[-1]

    def one(index, carry):
        source = source_ref[index]
        place = place_ref[index]
        for number, ref in enumerate(sources):

            @pl.when(source == number)
            def _():
                pltpu.make_async_copy(ref.at[place], out.at[index], sem).start()

        @pl.when(source == len(sources))
        def _():
            pltpu.make_async_copy(sources[0].at[0], out.at[index], sem).start()

        return carry

    lax.fori_loop(0, out.shape[0], one, 0)
    pltpu.make_async_copy(out, out, sem).wait()


def assemble(source, place, sources):
    scalars = pl.BlockSpec(memory_space=pltpu.SMEM)
    shape = (source.shape[0],) + sources[0].shape[1:]
    return pl.pallas_call(
        assemble_kernel,
        out_shape=jax.ShapeDtypeStruct(shape, sources[0].dtype),
        in_specs=[scalars, scalars] + [pl.BlockSpec(memory_space=pltpu.HBM)] * len(sources),
        out_specs=pl.BlockSpec(memory_space=pltpu.VMEM),
        scratch_shapes=[pltpu.SemaphoreType.DMA],
        compiler_params=pltpu.CompilerParams(vmem_limit_bytes=VMEM_GRANT),
        cost_estimate=pl.CostEstimate(flops=0, bytes_accessed=4 * math.prod(shape), transcendentals=0),
        name="assemble",
    )(source, place, *sources)


def on_device(
    tokens,
    query_weight,
    keyvalue_weight,
    adapter_down_weight,
    adapter_up_weight,
    keyvalue_page_store,
    span_token_length,
    adapter_owner,
    adapter_local_index,
    page_owner,
    page_local_index,
):
    peers = lax.axis_size("dp")
    half = peers // 2
    me = lax.axis_index("dp")
    tok_rows = tokens.shape[0]
    q_cols = query_weight.shape[1]
    rank = adapter_down_weight.shape[2]
    adapter_slots = peers * ADP_CAP

    def swap(array, distance):
        return lax.ppermute(array, "dp", [(peer, peer ^ distance) for peer in range(peers)])

    page_count = page_local_index.shape[0]
    request_count = adapter_local_index.shape[0]
    raw = jnp.concatenate([page_owner[:, 0], page_local_index, adapter_owner[:, 0], adapter_local_index])
    everyone = lax.all_to_all(
        jnp.broadcast_to(raw[None], (peers, raw.shape[0])), "dp", split_axis=0, concat_axis=0, tiled=True
    )
    store, down_store, everyone = lax.optimization_barrier((keyvalue_page_store, adapter_down_weight, everyone))
    mirrored_store = swap(store, half)

    page_cap = max(2, 2 * page_count // peers)
    group = everyone[jnp.arange(half, dtype=jnp.int32) ^ me]
    group_owner = group[:, :page_count]
    group_local = group[:, page_count : 2 * page_count]
    group_order = earlier_alike(group_owner)
    near_asked = asked_of(me, group_owner, group_order, group_local, page_cap)
    far_asked = asked_of(me ^ half, group_owner, group_order, group_local, page_cap)
    all_owner = everyone[:, 2 * page_count : 2 * page_count + request_count]
    all_local = everyone[:, 2 * page_count + request_count :]
    adapter_asked = asked_of(me, all_owner, earlier_alike(all_owner), all_local, ADP_CAP).reshape(-1)
    adapter_pos = adapter_owner[:, 0] * ADP_CAP + earlier_alike(adapter_owner[:, 0])
    page_source = page_owner[:, 0] ^ me
    page_place = jnp.where(page_source % half == 0, page_local_index, earlier_alike(page_owner[:, 0]))

    near = [swap(pages, i + 1) for i, pages in enumerate(serve(near_asked[1:], store, VMEM_GRANT))]
    down_rows = down_store[adapter_asked]
    up_rows = adapter_up_weight[adapter_asked]

    piece = lax.all_gather(tokens, "tensor", axis=1, tiled=True)
    query_base = jnp.dot(piece, query_weight, preferred_element_type=jnp.float32)
    new_cache = jnp.dot(piece, keyvalue_weight, preferred_element_type=jnp.float32).astype(jnp.bfloat16)

    down_rows, mirrored_store, query_base, new_cache, near = lax.optimization_barrier(
        (down_rows, mirrored_store, query_base, new_cache, near)
    )
    lengths = span_token_length[0]
    ends = jnp.cumsum(lengths)
    starts = ends - lengths
    row = jnp.arange(tok_rows, dtype=jnp.int32)[:, None]
    member = (row >= starts[None, :]) & (row < ends[None, :])
    slot = jnp.sum(jnp.where(member, adapter_pos[None, :], 0), axis=1)
    in_slot = slot[:, None] == jnp.arange(adapter_slots, dtype=jnp.int32)[None, :]
    steps_total = -(-(tok_rows // BLOCK + request_count - 1) // TOGETHER) * TOGETHER
    steps = attention_steps(starts, ends, steps_total)

    down_sent = lax.all_to_all(down_rows, "dp", split_axis=0, concat_axis=0, tiled=True)
    far = list(serve(far_asked[1:], mirrored_store, SMALL_GRANT))
    far = [swap(pages, i + 1) for i, pages in enumerate(far[:-1])] + far[-1:]
    up_rows, down_sent, far, in_slot, steps, page_source, page_place = lax.optimization_barrier(
        (up_rows, down_sent, far, in_slot, steps, page_source, page_place)
    )
    up_sent = lax.all_to_all(up_rows, "dp", split_axis=0, concat_axis=0, tiled=True)
    far[-1] = swap(far[-1], half - 1)

    down_part = jnp.einsum("tn,snk->tsk", tokens, down_sent, preferred_element_type=jnp.float32)
    shrink_part = jnp.sum(jnp.where(in_slot[:, :, None], down_part, 0.0), axis=1)
    shrink = lax.psum(shrink_part, "tensor").astype(jnp.bfloat16)
    spread = jnp.where(in_slot[:, :, None], shrink[:, None, :], 0).reshape(tok_rows, adapter_slots * rank)
    prefix_pages = assemble(page_source, page_place, [store, *near, mirrored_store, *far[:-1]])

    taken = starts[:, None] + jnp.arange(MOST, dtype=jnp.int32)[None, :]
    pick = (taken.reshape(-1, 1) == jnp.arange(tok_rows, dtype=jnp.int32)[None, :]).astype(jnp.bfloat16)
    fresh = jnp.dot(pick, new_cache, preferred_element_type=jnp.float32).astype(jnp.bfloat16)
    fresh = fresh.reshape(request_count, MOST, -1)
    up = up_sent.reshape(adapter_slots * rank, q_cols)
    out = attend(
        query_base, spread, up, fresh, prefix_pages, far[-1], page_source, page_place, peers - 1, steps
    )
    return (out, new_cache)


def solution(mesh):
    return jax.shard_map(
        on_device,
        mesh=mesh,
        in_specs=(
            P("dp", "tensor"),
            P(None, "tensor"),
            P(None, "tensor"),
            P("dp", "tensor", None),
            P("dp", None, "tensor"),
            P("dp", None, "tensor"),
            P("dp", None),
            P("dp", None),
            P("dp"),
            P("dp", None),
            P("dp"),
        ),
        out_specs=(P("dp", "tensor"), P("dp", "tensor")),
        check_vma=False,
    )
```

```python
import functools
import math

import jax
import jax.numpy as jnp
from jax import lax
from jax.experimental import pallas as pl
from jax.experimental.pallas import tpu as pltpu
from jax.sharding import PartitionSpec as P

HEAD_WIDTH = 128
ADP_CAP = 2
HITS = 4
MOST = 128
BLOCK = 16
TOGETHER = 8
TILE = 256
VMEM_GRANT = 60 * 1024 * 1024
SMALL_GRANT = 16 * 1024 * 1024

ADAPTER_SCALE = 0.5
NEGATIVE = -1e30


def earlier_alike(owner):
    count = owner.shape[-1]
    ahead = jnp.arange(count, dtype=jnp.int32)[None, :] < jnp.arange(count, dtype=jnp.int32)[:, None]
    alike = owner[..., None, :] == owner[..., :, None]
    return jnp.sum((alike & ahead).astype(jnp.int32), axis=-1)


def asked_of(holder, owner, order, local, capacity):
    place = jnp.arange(capacity, dtype=jnp.int32)[None, :, None]
    match = (owner[:, None, :] == holder) & (order[:, None, :] == place)
    return jnp.sum(jnp.where(match, local[:, None, :], 0), axis=2)


def attention_steps(starts, ends, total):
    first = starts // BLOCK
    count = (ends - 1) // BLOCK - first + 1
    upto = jnp.cumsum(count)
    step = jnp.minimum(jnp.arange(total, dtype=jnp.int32), upto[-1] - 1)
    request = jnp.sum((upto[None, :] <= step[:, None]).astype(jnp.int32), axis=1)
    pick = request[:, None] == jnp.arange(starts.shape[0], dtype=jnp.int32)[None, :]

    def at(values):
        return jnp.sum(jnp.where(pick, values[None, :], 0), axis=1)

    block = at(first) + step - at(upto - count)
    return jnp.stack([request, block, at(starts), at(ends)])


def attention_kernel(
    last, steps_ref, source_ref, place_ref, spread_hbm, up_any, base_hbm, fresh_hbm, pages_hbm, last_hbm, lower_hbm, *rest
):
    out_ref, query_ref, spread_ref, up_ref, base_ref, cache_ref, sems, tile_sems = rest
    q_cols = base_ref.shape[1]
    kv_heads = cache_ref.shape[2] // (2 * HEAD_WIDTH)
    group = q_cols // HEAD_WIDTH // kv_heads
    page = pages_hbm.shape[1]
    cut = last_hbm.shape[1]
    held = HITS * page
    sharp = HEAD_WIDTH ** -0.5 * math.log2(math.e)

    def tile_copies(index):
        cols = pl.ds(pl.multiple_of(index * TILE, TILE), TILE)
        return (
            pltpu.make_async_copy(up_any.at[:, cols], up_ref.at[:, cols], tile_sems.at[0, index]),
            pltpu.make_async_copy(base_hbm.at[:, cols], base_ref.at[:, cols], tile_sems.at[1, index]),
        )

    def fetch(index, carry):
        rows = pl.ds(pl.multiple_of(index % HITS * page, page), page)
        to = cache_ref.at[index // HITS, rows]
        late = source_ref[index] == last

        @pl.when(late)
        def _():
            upper = cache_ref.at[index // HITS, pl.ds(pl.multiple_of(index % HITS * page, page), cut)]
            lower = cache_ref.at[index // HITS, pl.ds(pl.multiple_of(index % HITS * page + cut, cut), page - cut)]
            pltpu.make_async_copy(last_hbm.at[place_ref[index]], upper, sems.at[1]).start()
            pltpu.make_async_copy(lower_hbm.at[place_ref[index]], lower, sems.at[1]).start()

        @pl.when(jnp.logical_not(late))
        def _():
            pltpu.make_async_copy(pages_hbm.at[index], to, sems.at[1]).start()

        return carry

    spread_copy = pltpu.make_async_copy(spread_hbm, spread_ref, sems.at[0])
    fresh_copy = pltpu.make_async_copy(fresh_hbm, cache_ref.at[:, held:], sems.at[2])
    spread_copy.start()
    for index in range(q_cols // TILE):
        for copy in tile_copies(index):
            copy.start()
    fresh_copy.start()
    lax.fori_loop(0, pages_hbm.shape[0], fetch, 0)
    spread_copy.wait()

    def project(index, carry):
        for copy in tile_copies(index):
            copy.wait()
        cols = pl.ds(pl.multiple_of(index * TILE, TILE), TILE)
        correction = jnp.dot(spread_ref[...], up_ref[:, cols], preferred_element_type=jnp.float32)
        query_ref[:, cols] = (base_ref[:, cols] + ADAPTER_SCALE * correction).astype(jnp.bfloat16)
        return carry

    lax.fori_loop(0, q_cols // TILE, project, 0)
    fresh_copy.wait()
    prefix = cache_ref.at[:, :held]
    pltpu.make_async_copy(prefix, prefix, sems.at[1]).wait()
    dims = (((1,), (1,)), ((), ()))
    tall = group * BLOCK
    q_at = lax.broadcasted_iota(jnp.int32, (kv_heads * tall, MOST), 0) % BLOCK
    ahead = lax.broadcasted_iota(jnp.int32, (kv_heads * tall, MOST), 1) - q_at
    own_at = lax.broadcasted_iota(jnp.int32, (BLOCK, HEAD_WIDTH), 0)
    blank = jnp.zeros((tall, HEAD_WIDTH), jnp.bfloat16)

    def side_by_side(request, offset):
        columns = [(2 * head + offset) * HEAD_WIDTH for head in range(kv_heads)]
        return jnp.concatenate([cache_ref[request, :, col : col + HEAD_WIDTH] for col in columns], axis=1)

    def queries(row):
        heads = []
        for head in range(kv_heads):
            columns = [(head * group + g) * HEAD_WIDTH for g in range(group)]
            own = jnp.concatenate([query_ref[pl.ds(row, BLOCK), col : col + HEAD_WIDTH] for col in columns], axis=0)
            heads.append(jnp.concatenate([own if other == head else blank for other in range(kv_heads)], axis=1))
        return jnp.concatenate(heads, axis=0)

    def several(turn, carry):
        places = []
        for lane in range(TOGETHER):
            index = turn * TOGETHER + lane
            row = pl.multiple_of(steps_ref[1, index] * BLOCK, BLOCK)
            places.append((steps_ref[0, index], row, steps_ref[2, index], steps_ref[3, index]))
        scores = []
        for request, row, start, _ in places:
            score = lax.dot_general(queries(row), side_by_side(request, 0), dims, preferred_element_type=jnp.float32)
            scores.append((score[:, :held], jnp.where(ahead <= row - start, score[:, held:], NEGATIVE)))
        weights = []
        for old_s, new_s in scores:
            top = jnp.maximum(
                jnp.max(old_s, axis=1, keepdims=True), jnp.max(new_s, axis=1, keepdims=True)
            )
            old_e = jnp.exp2((old_s - top) * sharp)
            new_e = jnp.exp2((new_s - top) * sharp)
            total = jnp.sum(old_e, axis=1, keepdims=True) + jnp.sum(new_e, axis=1, keepdims=True)
            weights.append((jnp.concatenate([old_e, new_e], axis=1).astype(jnp.bfloat16), total))
        results = []
        for (request, _, _, _), (weight, total) in zip(places, weights):
            summed = jnp.dot(weight, side_by_side(request, 1), preferred_element_type=jnp.float32)
            results.append((summed, total))
        for (_, row, start, end), (summed, total) in zip(places, results):
            own = (own_at >= start - row) & (own_at < end - row)
            for head in range(kv_heads):
                rows = slice(head * tall, (head + 1) * tall)
                result = summed[rows, head * HEAD_WIDTH : (head + 1) * HEAD_WIDTH] / total[rows]
                result = result.astype(jnp.bfloat16)
                for g in range(group):
                    col = (head * group + g) * HEAD_WIDTH
                    cols = slice(col, col + HEAD_WIDTH)
                    before = out_ref[pl.ds(row, BLOCK), cols]
                    out_ref[pl.ds(row, BLOCK), cols] = jnp.where(own, result[g * BLOCK : (g + 1) * BLOCK], before)
        return carry

    lax.fori_loop(0, steps_ref.shape[1] // TOGETHER, several, 0)


def attend(query_base, spread, up, fresh, pages, last_pages, lower_pages, source, place, last, steps):
    rows, q_cols = query_base.shape
    requests = fresh.shape[0]
    keys = HITS * pages.shape[1] + MOST
    hbm = pl.BlockSpec(memory_space=pltpu.HBM)
    scalars = pl.BlockSpec(memory_space=pltpu.SMEM)
    return pl.pallas_call(
        functools.partial(attention_kernel, last),
        out_shape=jax.ShapeDtypeStruct((rows, q_cols), jnp.bfloat16),
        in_specs=[scalars] * 3 + [hbm] * 7,
        out_specs=pl.BlockSpec(memory_space=pltpu.VMEM),
        scratch_shapes=[
            pltpu.VMEM((rows, q_cols), jnp.bfloat16),
            *[pltpu.VMEM(each.shape, each.dtype) for each in (spread, up, query_base)],
            pltpu.VMEM((requests, keys, pages.shape[2]), pages.dtype),
            pltpu.SemaphoreType.DMA((3,)),
            pltpu.SemaphoreType.DMA((2, q_cols // TILE)),
        ],
        compiler_params=pltpu.CompilerParams(vmem_limit_bytes=VMEM_GRANT),
        cost_estimate=pl.CostEstimate(
            flops=4 * steps.shape[1] * BLOCK * q_cols * keys + 2 * spread.size * q_cols,
            bytes_accessed=4 * query_base.size + 2 * (2 * spread.size + up.size + fresh.size + pages.size),
            transcendentals=0,
        ),
        name="attend",
    )(steps, source, place, spread, up, query_base, fresh, pages, last_pages, lower_pages)


def serve_kernel(parts, asked_ref, *refs):
    stores, outs, sems = refs[:parts], refs[parts:-1], refs[-1]
    for index, out in enumerate(outs):
        for place in range(out.shape[0]):
            page = asked_ref[index * out.shape[0] + place]
            first = 0
            for store_ref in stores:
                rows = out.at[place, first : first + store_ref.shape[1]]
                pltpu.make_async_copy(store_ref.at[page], rows, sems.at[index]).start()
                first += store_ref.shape[1]
    for index, out in enumerate(outs):
        pltpu.make_async_copy(out, out, sems.at[index]).wait()


def serve(asked, stores, grant):
    blocks, capacity = asked.shape
    shape = (capacity, sum(store.shape[1] for store in stores), stores[0].shape[2])
    return pl.pallas_call(
        functools.partial(serve_kernel, len(stores)),
        out_shape=[jax.ShapeDtypeStruct(shape, stores[0].dtype)] * blocks,
        in_specs=[pl.BlockSpec(memory_space=pltpu.SMEM)] + [pl.BlockSpec(memory_space=pl.ANY)] * len(stores),
        out_specs=[pl.BlockSpec(memory_space=pltpu.VMEM)] * blocks,
        scratch_shapes=[pltpu.SemaphoreType.DMA((blocks,))],
        compiler_params=pltpu.CompilerParams(vmem_limit_bytes=grant),
        cost_estimate=pl.CostEstimate(
            flops=0, bytes_accessed=4 * blocks * math.prod(shape), transcendentals=0
        ),
        name="serve",
    )(asked.reshape(-1), *stores)


def assemble_kernel(mirror, source_ref, place_ref, *refs):
    sources, lower, out, sem = refs[:-3], refs[-3], refs[-2], refs[-1]
    cut = sources[mirror].shape[1]

    def one(index, carry):
        source = source_ref[index]
        place = place_ref[index]
        for number, ref in enumerate(sources):

            @pl.when(source == number)
            def _():
                if number == mirror:
                    pltpu.make_async_copy(ref.at[place], out.at[index, :cut], sem).start()
                    pltpu.make_async_copy(lower.at[place], out.at[index, cut:], sem).start()
                else:
                    pltpu.make_async_copy(ref.at[place], out.at[index], sem).start()

        @pl.when(source == len(sources))
        def _():
            pltpu.make_async_copy(sources[0].at[0], out.at[index], sem).start()

        return carry

    lax.fori_loop(0, out.shape[0], one, 0)
    pltpu.make_async_copy(out, out, sem).wait()


def assemble(source, place, sources, mirror, lower):
    scalars = pl.BlockSpec(memory_space=pltpu.SMEM)
    shape = (source.shape[0],) + sources[0].shape[1:]
    return pl.pallas_call(
        functools.partial(assemble_kernel, mirror),
        out_shape=jax.ShapeDtypeStruct(shape, sources[0].dtype),
        in_specs=[scalars, scalars] + [pl.BlockSpec(memory_space=pltpu.HBM)] * (len(sources) + 1),
        out_specs=pl.BlockSpec(memory_space=pltpu.VMEM),
        scratch_shapes=[pltpu.SemaphoreType.DMA],
        compiler_params=pltpu.CompilerParams(vmem_limit_bytes=VMEM_GRANT),
        cost_estimate=pl.CostEstimate(flops=0, bytes_accessed=4 * math.prod(shape), transcendentals=0),
        name="assemble",
    )(source, place, *sources, lower)


def on_device(
    tokens,
    query_weight,
    keyvalue_weight,
    adapter_down_weight,
    adapter_up_weight,
    keyvalue_page_store,
    span_token_length,
    adapter_owner,
    adapter_local_index,
    page_owner,
    page_local_index,
):
    peers = lax.axis_size("dp")
    half = peers // 2
    me = lax.axis_index("dp")
    tok_rows = tokens.shape[0]
    q_cols = query_weight.shape[1]
    rank = adapter_down_weight.shape[2]
    adapter_slots = peers * ADP_CAP

    def swap(array, distance):
        return lax.ppermute(array, "dp", [(peer, peer ^ distance) for peer in range(peers)])

    page_count = page_local_index.shape[0]
    request_count = adapter_local_index.shape[0]
    raw = jnp.concatenate([page_owner[:, 0], page_local_index, adapter_owner[:, 0], adapter_local_index])
    everyone = lax.all_to_all(
        jnp.broadcast_to(raw[None], (peers, raw.shape[0])), "dp", split_axis=0, concat_axis=0, tiled=True
    )
    cut = keyvalue_page_store.shape[1] // 2
    pools = [keyvalue_page_store[:, :cut], keyvalue_page_store[:, cut:]]
    store, down_store, everyone, pools = lax.optimization_barrier(
        (keyvalue_page_store, adapter_down_weight, everyone, pools)
    )
    upper = swap(pools[0], half)
    upper, pools[1] = lax.optimization_barrier((upper, pools[1]))
    lower = swap(pools[1], half)

    page_cap = max(2, 2 * page_count // peers)
    group = everyone[jnp.arange(half, dtype=jnp.int32) ^ me]
    group_owner = group[:, :page_count]
    group_local = group[:, page_count : 2 * page_count]
    group_order = earlier_alike(group_owner)
    near_asked = asked_of(me, group_owner, group_order, group_local, page_cap)
    far_asked = asked_of(me ^ half, group_owner, group_order, group_local, page_cap)
    all_owner = everyone[:, 2 * page_count : 2 * page_count + request_count]
    all_local = everyone[:, 2 * page_count + request_count :]
    adapter_asked = asked_of(me, all_owner, earlier_alike(all_owner), all_local, ADP_CAP).reshape(-1)
    adapter_pos = adapter_owner[:, 0] * ADP_CAP + earlier_alike(adapter_owner[:, 0])
    page_source = page_owner[:, 0] ^ me
    page_place = jnp.where(page_source % half == 0, page_local_index, earlier_alike(page_owner[:, 0]))

    near = [swap(pages, i + 1) for i, pages in enumerate(serve(near_asked[1:], [store], VMEM_GRANT))]
    down_rows = down_store[adapter_asked]
    up_rows = adapter_up_weight[adapter_asked]

    piece = lax.all_gather(tokens, "tensor", axis=1, tiled=True)
    query_base = jnp.dot(piece, query_weight, preferred_element_type=jnp.float32)
    new_cache = jnp.dot(piece, keyvalue_weight, preferred_element_type=jnp.float32).astype(jnp.bfloat16)

    (last_upper,) = serve(far_asked[half - 1 :], [upper], SMALL_GRANT)
    last_upper = swap(last_upper, half - 1)
    down_rows, upper, lower, query_base, new_cache, near, last_upper = lax.optimization_barrier(
        (down_rows, upper, lower, query_base, new_cache, near, last_upper)
    )
    lengths = span_token_length[0]
    ends = jnp.cumsum(lengths)
    starts = ends - lengths
    row = jnp.arange(tok_rows, dtype=jnp.int32)[:, None]
    member = (row >= starts[None, :]) & (row < ends[None, :])
    slot = jnp.sum(jnp.where(member, adapter_pos[None, :], 0), axis=1)
    in_slot = slot[:, None] == jnp.arange(adapter_slots, dtype=jnp.int32)[None, :]
    steps_total = -(-(tok_rows // BLOCK + request_count - 1) // TOGETHER) * TOGETHER
    steps = attention_steps(starts, ends, steps_total)

    down_sent = lax.all_to_all(down_rows, "dp", split_axis=0, concat_axis=0, tiled=True)
    far = serve(far_asked[1 : half - 1], [upper, lower], SMALL_GRANT)
    far = [swap(pages, i + 1) for i, pages in enumerate(far)]
    (last_lower,) = serve(far_asked[half - 1 :], [lower], SMALL_GRANT)
    up_rows, down_sent, far, last_lower, in_slot, steps, page_source, page_place = lax.optimization_barrier(
        (up_rows, down_sent, far, last_lower, in_slot, steps, page_source, page_place)
    )
    up_sent = lax.all_to_all(up_rows, "dp", split_axis=0, concat_axis=0, tiled=True)
    last_lower = swap(last_lower, half - 1)

    down_part = jnp.einsum("tn,snk->tsk", tokens, down_sent, preferred_element_type=jnp.float32)
    shrink_part = jnp.sum(jnp.where(in_slot[:, :, None], down_part, 0.0), axis=1)
    shrink = lax.psum(shrink_part, "tensor").astype(jnp.bfloat16)
    spread = jnp.where(in_slot[:, :, None], shrink[:, None, :], 0).reshape(tok_rows, adapter_slots * rank)
    prefix_pages = assemble(page_source, page_place, [store, *near, upper, *far], half, lower)

    taken = starts[:, None] + jnp.arange(MOST, dtype=jnp.int32)[None, :]
    pick = (taken.reshape(-1, 1) == jnp.arange(tok_rows, dtype=jnp.int32)[None, :]).astype(jnp.bfloat16)
    fresh = jnp.dot(pick, new_cache, preferred_element_type=jnp.float32).astype(jnp.bfloat16)
    fresh = fresh.reshape(request_count, MOST, -1)
    up = up_sent.reshape(adapter_slots * rank, q_cols)
    out = attend(
        query_base, spread, up, fresh, prefix_pages, last_upper, last_lower, page_source, page_place, peers - 1, steps
    )
    return (out, new_cache)


def solution(mesh):
    return jax.shard_map(
        on_device,
        mesh=mesh,
        in_specs=(
            P("dp", "tensor"),
            P(None, "tensor"),
            P(None, "tensor"),
            P("dp", "tensor", None),
            P("dp", None, "tensor"),
            P("dp", None, "tensor"),
            P("dp", None),
            P("dp", None),
            P("dp"),
            P("dp", None),
            P("dp"),
        ),
        out_specs=(P("dp", "tensor"), P("dp", "tensor")),
        check_vma=False,
    )
```

```python
import functools
import math

import jax
import jax.numpy as jnp
from jax import lax
from jax.experimental import pallas as pl
from jax.experimental.pallas import tpu as pltpu
from jax.sharding import PartitionSpec as P

HEAD_WIDTH = 128
ADP_CAP = 2
HITS = 4
MOST = 128
BLOCK = 16
TOGETHER = 16
TILE = 512
VMEM_GRANT = 60 * 1024 * 1024
SMALL_GRANT = 16 * 1024 * 1024

ADAPTER_SCALE = 0.5
NEGATIVE = -1e30


def earlier_alike(owner):
    count = owner.shape[-1]
    ahead = jnp.arange(count, dtype=jnp.int32)[None, :] < jnp.arange(count, dtype=jnp.int32)[:, None]
    alike = owner[..., None, :] == owner[..., :, None]
    return jnp.sum((alike & ahead).astype(jnp.int32), axis=-1)


def asked_of(holder, owner, order, local, capacity):
    place = jnp.arange(capacity, dtype=jnp.int32)[None, :, None]
    match = (owner[:, None, :] == holder) & (order[:, None, :] == place)
    return jnp.sum(jnp.where(match, local[:, None, :], 0), axis=2)


def attention_steps(starts, ends, total):
    first = starts // BLOCK
    count = (ends - 1) // BLOCK - first + 1
    upto = jnp.cumsum(count)
    step = jnp.minimum(jnp.arange(total, dtype=jnp.int32), upto[-1] - 1)
    request = jnp.sum((upto[None, :] <= step[:, None]).astype(jnp.int32), axis=1)
    pick = request[:, None] == jnp.arange(starts.shape[0], dtype=jnp.int32)[None, :]

    def at(values):
        return jnp.sum(jnp.where(pick, values[None, :], 0), axis=1)

    block = at(first) + step - at(upto - count)
    return jnp.stack([request, block, at(starts), at(ends)])


def attention_kernel(
    last, steps_ref, source_ref, place_ref, spread_hbm, up_any, base_hbm, fresh_hbm, pages_hbm, last_hbm, lower_hbm, *rest
):
    out_ref, query_ref, spread_ref, up_ref, base_ref, cache_ref, sems, tile_sems = rest
    q_cols = base_ref.shape[1]
    kv_heads = cache_ref.shape[2] // (2 * HEAD_WIDTH)
    group = q_cols // HEAD_WIDTH // kv_heads
    page = pages_hbm.shape[1]
    cut = last_hbm.shape[1]
    held = HITS * page
    sharp = HEAD_WIDTH ** -0.5 * math.log2(math.e)

    def tile_copies(index):
        cols = pl.ds(pl.multiple_of(index * TILE, TILE), TILE)
        return (
            pltpu.make_async_copy(up_any.at[:, cols], up_ref.at[:, cols], tile_sems.at[0, index]),
            pltpu.make_async_copy(base_hbm.at[:, cols], base_ref.at[:, cols], tile_sems.at[1, index]),
        )

    def fetch(index, carry):
        rows = pl.ds(pl.multiple_of(index % HITS * page, page), page)
        to = cache_ref.at[index // HITS, rows]
        late = source_ref[index] == last

        @pl.when(late)
        def _():
            upper = cache_ref.at[index // HITS, pl.ds(pl.multiple_of(index % HITS * page, page), cut)]
            lower = cache_ref.at[index // HITS, pl.ds(pl.multiple_of(index % HITS * page + cut, cut), page - cut)]
            pltpu.make_async_copy(last_hbm.at[place_ref[index]], upper, sems.at[1]).start()
            pltpu.make_async_copy(lower_hbm.at[place_ref[index]], lower, sems.at[1]).start()

        @pl.when(jnp.logical_not(late))
        def _():
            pltpu.make_async_copy(pages_hbm.at[index], to, sems.at[1]).start()

        return carry

    spread_copy = pltpu.make_async_copy(spread_hbm, spread_ref, sems.at[0])
    fresh_copy = pltpu.make_async_copy(fresh_hbm, cache_ref.at[:, held:], sems.at[2])
    spread_copy.start()
    for index in range(q_cols // TILE):
        for copy in tile_copies(index):
            copy.start()
    fresh_copy.start()
    lax.fori_loop(0, pages_hbm.shape[0], fetch, 0)
    spread_copy.wait()

    def project(index, carry):
        for copy in tile_copies(index):
            copy.wait()
        cols = pl.ds(pl.multiple_of(index * TILE, TILE), TILE)
        correction = jnp.dot(spread_ref[...], up_ref[:, cols], preferred_element_type=jnp.float32)
        query_ref[:, cols] = (base_ref[:, cols] + ADAPTER_SCALE * correction).astype(jnp.bfloat16)
        return carry

    lax.fori_loop(0, q_cols // TILE, project, 0)
    fresh_copy.wait()
    prefix = cache_ref.at[:, :held]
    pltpu.make_async_copy(prefix, prefix, sems.at[1]).wait()
    dims = (((1,), (1,)), ((), ()))
    tall = group * BLOCK
    q_at = lax.broadcasted_iota(jnp.int32, (kv_heads * tall, MOST), 0) % BLOCK
    ahead = lax.broadcasted_iota(jnp.int32, (kv_heads * tall, MOST), 1) - q_at
    own_at = lax.broadcasted_iota(jnp.int32, (BLOCK, HEAD_WIDTH), 0)
    blank = jnp.zeros((tall, HEAD_WIDTH), jnp.bfloat16)

    def side_by_side(request, offset):
        columns = [(2 * head + offset) * HEAD_WIDTH for head in range(kv_heads)]
        return jnp.concatenate([cache_ref[request, :, col : col + HEAD_WIDTH] for col in columns], axis=1)

    def queries(row):
        heads = []
        for head in range(kv_heads):
            columns = [(head * group + g) * HEAD_WIDTH for g in range(group)]
            own = jnp.concatenate([query_ref[pl.ds(row, BLOCK), col : col + HEAD_WIDTH] for col in columns], axis=0)
            heads.append(jnp.concatenate([own if other == head else blank for other in range(kv_heads)], axis=1))
        return jnp.concatenate(heads, axis=0)

    def several(turn, carry):
        places = []
        for lane in range(TOGETHER):
            index = turn * TOGETHER + lane
            row = pl.multiple_of(steps_ref[1, index] * BLOCK, BLOCK)
            places.append((steps_ref[0, index], row, steps_ref[2, index], steps_ref[3, index]))
        scores = []
        for request, row, start, _ in places:
            score = lax.dot_general(queries(row), side_by_side(request, 0), dims, preferred_element_type=jnp.float32)
            scores.append((score[:, :held], jnp.where(ahead <= row - start, score[:, held:], NEGATIVE)))
        weights = []
        for old_s, new_s in scores:
            top = jnp.maximum(
                jnp.max(old_s, axis=1, keepdims=True), jnp.max(new_s, axis=1, keepdims=True)
            )
            old_e = jnp.exp2((old_s - top) * sharp)
            new_e = jnp.exp2((new_s - top) * sharp)
            total = jnp.sum(old_e, axis=1, keepdims=True) + jnp.sum(new_e, axis=1, keepdims=True)
            weights.append((jnp.concatenate([old_e, new_e], axis=1).astype(jnp.bfloat16), total))
        results = []
        for (request, _, _, _), (weight, total) in zip(places, weights):
            summed = jnp.dot(weight, side_by_side(request, 1), preferred_element_type=jnp.float32)
            results.append((summed, total))
        for (_, row, start, end), (summed, total) in zip(places, results):
            own = (own_at >= start - row) & (own_at < end - row)
            for head in range(kv_heads):
                rows = slice(head * tall, (head + 1) * tall)
                result = summed[rows, head * HEAD_WIDTH : (head + 1) * HEAD_WIDTH] / total[rows]
                result = result.astype(jnp.bfloat16)
                for g in range(group):
                    col = (head * group + g) * HEAD_WIDTH
                    cols = slice(col, col + HEAD_WIDTH)
                    before = out_ref[pl.ds(row, BLOCK), cols]
                    out_ref[pl.ds(row, BLOCK), cols] = jnp.where(own, result[g * BLOCK : (g + 1) * BLOCK], before)
        return carry

    lax.fori_loop(0, steps_ref.shape[1] // TOGETHER, several, 0)


def attend(query_base, spread, up, fresh, pages, last_pages, lower_pages, source, place, last, steps):
    rows, q_cols = query_base.shape
    requests = fresh.shape[0]
    keys = HITS * pages.shape[1] + MOST
    hbm = pl.BlockSpec(memory_space=pltpu.HBM)
    scalars = pl.BlockSpec(memory_space=pltpu.SMEM)
    return pl.pallas_call(
        functools.partial(attention_kernel, last),
        out_shape=jax.ShapeDtypeStruct((rows, q_cols), jnp.bfloat16),
        in_specs=[scalars] * 3 + [hbm] * 7,
        out_specs=pl.BlockSpec(memory_space=pltpu.VMEM),
        scratch_shapes=[
            pltpu.VMEM((rows, q_cols), jnp.bfloat16),
            *[pltpu.VMEM(each.shape, each.dtype) for each in (spread, up, query_base)],
            pltpu.VMEM((requests, keys, pages.shape[2]), pages.dtype),
            pltpu.SemaphoreType.DMA((3,)),
            pltpu.SemaphoreType.DMA((2, q_cols // TILE)),
        ],
        compiler_params=pltpu.CompilerParams(vmem_limit_bytes=VMEM_GRANT),
        cost_estimate=pl.CostEstimate(
            flops=4 * steps.shape[1] * BLOCK * q_cols * keys + 2 * spread.size * q_cols,
            bytes_accessed=4 * query_base.size + 2 * (2 * spread.size + up.size + fresh.size + pages.size),
            transcendentals=0,
        ),
        name="attend",
    )(steps, source, place, spread, up, query_base, fresh, pages, last_pages, lower_pages)


def serve_kernel(parts, asked_ref, *refs):
    stores, outs, sems = refs[:parts], refs[parts:-1], refs[-1]
    for index, out in enumerate(outs):
        for place in range(out.shape[0]):
            page = asked_ref[index * out.shape[0] + place]
            first = 0
            for store_ref in stores:
                rows = out.at[place, first : first + store_ref.shape[1]]
                pltpu.make_async_copy(store_ref.at[page], rows, sems.at[index]).start()
                first += store_ref.shape[1]
    for index, out in enumerate(outs):
        pltpu.make_async_copy(out, out, sems.at[index]).wait()


def serve(asked, stores, grant):
    blocks, capacity = asked.shape
    shape = (capacity, sum(store.shape[1] for store in stores), stores[0].shape[2])
    return pl.pallas_call(
        functools.partial(serve_kernel, len(stores)),
        out_shape=[jax.ShapeDtypeStruct(shape, stores[0].dtype)] * blocks,
        in_specs=[pl.BlockSpec(memory_space=pltpu.SMEM)] + [pl.BlockSpec(memory_space=pl.ANY)] * len(stores),
        out_specs=[pl.BlockSpec(memory_space=pltpu.VMEM)] * blocks,
        scratch_shapes=[pltpu.SemaphoreType.DMA((blocks,))],
        compiler_params=pltpu.CompilerParams(vmem_limit_bytes=grant),
        cost_estimate=pl.CostEstimate(
            flops=0, bytes_accessed=4 * blocks * math.prod(shape), transcendentals=0
        ),
        name="serve",
    )(asked.reshape(-1), *stores)


def assemble_kernel(mirror, source_ref, place_ref, *refs):
    sources, lower, out, sem = refs[:-3], refs[-3], refs[-2], refs[-1]
    cut = sources[mirror].shape[1]

    def one(index, carry):
        source = source_ref[index]
        place = place_ref[index]
        for number, ref in enumerate(sources):

            @pl.when(source == number)
            def _():
                if number == mirror:
                    pltpu.make_async_copy(ref.at[place], out.at[index, :cut], sem).start()
                    pltpu.make_async_copy(lower.at[place], out.at[index, cut:], sem).start()
                else:
                    pltpu.make_async_copy(ref.at[place], out.at[index], sem).start()

        @pl.when(source == len(sources))
        def _():
            pltpu.make_async_copy(sources[0].at[0], out.at[index], sem).start()

        return carry

    lax.fori_loop(0, out.shape[0], one, 0)
    pltpu.make_async_copy(out, out, sem).wait()


def assemble(source, place, sources, mirror, lower):
    scalars = pl.BlockSpec(memory_space=pltpu.SMEM)
    shape = (source.shape[0],) + sources[0].shape[1:]
    return pl.pallas_call(
        functools.partial(assemble_kernel, mirror),
        out_shape=jax.ShapeDtypeStruct(shape, sources[0].dtype),
        in_specs=[scalars, scalars] + [pl.BlockSpec(memory_space=pltpu.HBM)] * (len(sources) + 1),
        out_specs=pl.BlockSpec(memory_space=pltpu.VMEM),
        scratch_shapes=[pltpu.SemaphoreType.DMA],
        compiler_params=pltpu.CompilerParams(vmem_limit_bytes=VMEM_GRANT),
        cost_estimate=pl.CostEstimate(flops=0, bytes_accessed=4 * math.prod(shape), transcendentals=0),
        name="assemble",
    )(source, place, *sources, lower)


def on_device(
    tokens,
    query_weight,
    keyvalue_weight,
    adapter_down_weight,
    adapter_up_weight,
    keyvalue_page_store,
    span_token_length,
    adapter_owner,
    adapter_local_index,
    page_owner,
    page_local_index,
):
    peers = lax.axis_size("dp")
    half = peers // 2
    me = lax.axis_index("dp")
    tok_rows = tokens.shape[0]
    q_cols = query_weight.shape[1]
    rank = adapter_down_weight.shape[2]
    adapter_slots = peers * ADP_CAP

    def swap(array, distance):
        return lax.ppermute(array, "dp", [(peer, peer ^ distance) for peer in range(peers)])

    page_count = page_local_index.shape[0]
    request_count = adapter_local_index.shape[0]
    raw = jnp.concatenate([page_owner[:, 0], page_local_index, adapter_owner[:, 0], adapter_local_index])
    everyone = lax.all_to_all(
        jnp.broadcast_to(raw[None], (peers, raw.shape[0])), "dp", split_axis=0, concat_axis=0, tiled=True
    )
    cut = keyvalue_page_store.shape[1] // 2
    pools = [keyvalue_page_store[:, :cut], keyvalue_page_store[:, cut:]]
    store, down_store, everyone, pools = lax.optimization_barrier(
        (keyvalue_page_store, adapter_down_weight, everyone, pools)
    )
    upper = swap(pools[0], half)
    upper, pools[1] = lax.optimization_barrier((upper, pools[1]))
    lower = swap(pools[1], half)

    page_cap = max(2, 2 * page_count // peers)
    group = everyone[jnp.arange(half, dtype=jnp.int32) ^ me]
    group_owner = group[:, :page_count]
    group_local = group[:, page_count : 2 * page_count]
    group_order = earlier_alike(group_owner)
    near_asked = asked_of(me, group_owner, group_order, group_local, page_cap)
    far_asked = asked_of(me ^ half, group_owner, group_order, group_local, page_cap)
    all_owner = everyone[:, 2 * page_count : 2 * page_count + request_count]
    all_local = everyone[:, 2 * page_count + request_count :]
    adapter_asked = asked_of(me, all_owner, earlier_alike(all_owner), all_local, ADP_CAP).reshape(-1)
    adapter_pos = adapter_owner[:, 0] * ADP_CAP + earlier_alike(adapter_owner[:, 0])
    page_source = page_owner[:, 0] ^ me
    page_place = jnp.where(page_source % half == 0, page_local_index, earlier_alike(page_owner[:, 0]))

    near = [swap(pages, i + 1) for i, pages in enumerate(serve(near_asked[1:], [store], VMEM_GRANT))]
    down_rows = down_store[adapter_asked]
    up_rows = adapter_up_weight[adapter_asked]

    piece = lax.all_gather(tokens, "tensor", axis=1, tiled=True)
    query_base = jnp.dot(piece, query_weight, preferred_element_type=jnp.float32)
    new_cache = jnp.dot(piece, keyvalue_weight, preferred_element_type=jnp.float32).astype(jnp.bfloat16)

    (last_upper,) = serve(far_asked[half - 1 :], [upper], SMALL_GRANT)
    last_upper = swap(last_upper, half - 1)
    down_rows, upper, lower, query_base, new_cache, near, last_upper = lax.optimization_barrier(
        (down_rows, upper, lower, query_base, new_cache, near, last_upper)
    )
    lengths = span_token_length[0]
    ends = jnp.cumsum(lengths)
    starts = ends - lengths
    row = jnp.arange(tok_rows, dtype=jnp.int32)[:, None]
    member = (row >= starts[None, :]) & (row < ends[None, :])
    slot = jnp.sum(jnp.where(member, adapter_pos[None, :], 0), axis=1)
    in_slot = slot[:, None] == jnp.arange(adapter_slots, dtype=jnp.int32)[None, :]
    steps_total = -(-(tok_rows // BLOCK + request_count - 1) // TOGETHER) * TOGETHER
    steps = attention_steps(starts, ends, steps_total)

    down_sent = lax.all_to_all(down_rows, "dp", split_axis=0, concat_axis=0, tiled=True)
    far = serve(far_asked[1 : half - 1], [upper, lower], SMALL_GRANT)
    far = [swap(pages, i + 1) for i, pages in enumerate(far)]
    (last_lower,) = serve(far_asked[half - 1 :], [lower], SMALL_GRANT)
    up_rows, down_sent, far, last_lower, in_slot, steps, page_source, page_place = lax.optimization_barrier(
        (up_rows, down_sent, far, last_lower, in_slot, steps, page_source, page_place)
    )
    up_sent = lax.all_to_all(up_rows, "dp", split_axis=0, concat_axis=0, tiled=True)
    last_lower = swap(last_lower, half - 1)

    down_part = jnp.einsum("tn,snk->tsk", tokens, down_sent, preferred_element_type=jnp.float32)
    shrink_part = jnp.sum(jnp.where(in_slot[:, :, None], down_part, 0.0), axis=1)
    shrink = lax.psum(shrink_part, "tensor").astype(jnp.bfloat16)
    spread = jnp.where(in_slot[:, :, None], shrink[:, None, :], 0).reshape(tok_rows, adapter_slots * rank)
    prefix_pages = assemble(page_source, page_place, [store, *near, upper, *far], half, lower)

    taken = starts[:, None] + jnp.arange(MOST, dtype=jnp.int32)[None, :]
    pick = (taken.reshape(-1, 1) == jnp.arange(tok_rows, dtype=jnp.int32)[None, :]).astype(jnp.bfloat16)
    fresh = jnp.dot(pick, new_cache, preferred_element_type=jnp.float32).astype(jnp.bfloat16)
    fresh = fresh.reshape(request_count, MOST, -1)
    up = up_sent.reshape(adapter_slots * rank, q_cols)
    out = attend(
        query_base, spread, up, fresh, prefix_pages, last_upper, last_lower, page_source, page_place, peers - 1, steps
    )
    return (out, new_cache)


def solution(mesh):
    return jax.shard_map(
        on_device,
        mesh=mesh,
        in_specs=(
            P("dp", "tensor"),
            P(None, "tensor"),
            P(None, "tensor"),
            P("dp", "tensor", None),
            P("dp", None, "tensor"),
            P("dp", None, "tensor"),
            P("dp", None),
            P("dp", None),
            P("dp"),
            P("dp", None),
            P("dp"),
        ),
        out_specs=(P("dp", "tensor"), P("dp", "tensor")),
        check_vma=False,
    )
```
